256 devices in a mesh: space: 32 (over z_hi, x, core), chan: 8 (over y, z_lo).
Axes of the slice: x: 4, y: 4, z: 8 (z_hi: 4, z_lo: 2; z = z_hi * 2 + z_lo), core: 2. Of those that a mesh axis runs over, the one named last changes fastest.
Arguments:
- field: bfloat16 [256, 8, 4096], P('chan', None, 'space'), may hold values from -6 to 6
- first_weight: bfloat16 [256, 9, 256], P('chan'), may hold values from -0.125 to 0.125
- second_weight: bfloat16 [256, 9, 256], P('chan'), may hold values from -0.125 to 0.125
- cotangent: bfloat16 [256, 8, 4096], P('chan', None, 'space'), may hold values from -6 to 6
Outputs:
- field_grad: bfloat16 [256, 8, 4096], P('chan', None, 'space')
- first_grad: float32 [256, 9, 256], P('chan')
- second_grad: float32 [256, 9, 256], P('chan')
The draws below stay inside these ranges and needn't reach their ends.
All inputs are finite; a program needn't handle non-finite values.
Results may differ from the reference program's by a relative error of at most 0.0053.
Values may be sent and summed in bfloat16 or wider, within the bound.
A program may use at most 64 MiB of HBM per device.

```python
import math
import jax
import jax.numpy as jnp

C = 256
ROWS = 8
COLS = 4096


def block_scale(key, dims, cuts, low, high):
    level = 1.0
    for position, parts in cuts:
        draws = jax.random.uniform(jax.random.fold_in(jax.random.fold_in(key, 6), position), (parts,), jnp.float32, low / len(cuts), high / len(cuts))
        level = level * jnp.repeat(jnp.exp(draws), dims[position] // parts).reshape((-1,) + (1,) * (len(dims) - 1 - position))
    return level


def bell_draw(stream_key, shape, scale, most, cuts=(), held_as=jnp.bfloat16):
    array = jax.random.normal(stream_key, shape, jnp.float32) * scale
    if len(cuts) > 0:
        array = block_scale(stream_key, shape, cuts, -0.22, 0.18) * array
    return jnp.clip(array, min=-most, max=most).astype(held_as)


def setup_inputs(seed: int = 0) -> dict:
    arg_keys = jax.random.split(jax.random.key(seed), 5)
    field = bell_draw(arg_keys[0], (C, ROWS, COLS), 1.0, 6.0, ((0, 8), (2, 32)))
    first_weight = bell_draw(arg_keys[1], (C, 9, C), (9 * C) ** -0.5, 0.125, ((0, 8),))
    second_weight = bell_draw(arg_keys[2], (C, 9, C), (9 * C) ** -0.5, 0.125, ((0, 8),))
    cotangent = bell_draw(arg_keys[3], (C, ROWS, COLS), 1.0, 6.0, ((0, 8), (2, 32)))
    return {"field": field, "first_weight": first_weight, "second_weight": second_weight, "cotangent": cotangent}


def wrap_cols(values, width):
    return jnp.concatenate([values[:, :, -width:], values, values[:, :, :width]], axis=2)

def pad_rows(values):
    return jnp.pad(values, ((0, 0), (1, 1), (0, 0)))

def conv_forward(padded, weight):
    height = padded.shape[1] - 2
    length = padded.shape[2] - 2
    total = jnp.zeros((weight.shape[0], height, length), jnp.float32)
    for tap_row in range(3):
        for tap_col in range(3):
            window = padded[:, tap_row:tap_row + height, tap_col:tap_col + length].astype(jnp.float32)
            total = total + jnp.einsum('oi,irc->orc', weight[:, 3 * tap_row + tap_col, :].astype(jnp.float32), window)
    return total

def conv_back(padded, weight):
    height = padded.shape[1] - 2
    length = padded.shape[2] - 2
    total = jnp.zeros((weight.shape[2], height, length), jnp.float32)
    for tap_row in range(3):
        for tap_col in range(3):
            window = padded[:, 2 - tap_row:2 - tap_row + height, 2 - tap_col:2 - tap_col + length].astype(jnp.float32)
            total = total + jnp.einsum('oi,orc->irc', weight[:, 3 * tap_row + tap_col, :].astype(jnp.float32), window)
    return total

def weight_grad(upstream, padded):
    height = upstream.shape[1]
    length = upstream.shape[2]
    pieces = []
    for tap_row in range(3):
        for tap_col in range(3):
            window = padded[:, tap_row:tap_row + height, tap_col:tap_col + length].astype(jnp.float32)
            pieces.append(jnp.einsum('orc,irc->oi', upstream.astype(jnp.float32), window))
    return jnp.stack(pieces, axis=1)

def smooth_gelu(values):
    return jax.nn.gelu(values, approximate=True)

def resample(extended):
    lower = jnp.pad(extended, ((0, 0), (0, 1), (0, 0)))
    top_left = lower[:, :-1, :-1]
    top_right = lower[:, :-1, 1:]
    low_left = lower[:, 1:, :-1]
    low_right = lower[:, 1:, 1:]
    even_even = smooth_gelu(top_left)
    even_odd = smooth_gelu((top_left + top_right) * 0.5)
    odd_even = smooth_gelu((top_left + low_left) * 0.5)
    odd_odd = smooth_gelu((top_left + top_right + low_left + low_right) * 0.25)
    row_even = (even_odd[:, :, :-1] + 2.0 * even_even[:, :, 1:] + even_odd[:, :, 1:]) * 0.25
    row_odd = (odd_odd[:, :, :-1] + 2.0 * odd_even[:, :, 1:] + odd_odd[:, :, 1:]) * 0.25
    shifted = jnp.pad(row_odd, ((0, 0), (1, 0), (0, 0)))[:, :-1]
    return (shifted + 2.0 * row_even + row_odd) * 0.25

def periodic_resample(hidden_values):
    return resample(wrap_cols(hidden_values, 1))

def reference(field, first_weight, second_weight, cotangent):
    grad_scale = 1.0 / math.sqrt(ROWS * COLS)
    field_pad = pad_rows(wrap_cols(field, 1))
    hidden = conv_forward(field_pad, first_weight).astype(jnp.bfloat16)
    smooth_values, pullback = jax.vjp(periodic_resample, hidden.astype(jnp.float32))
    smooth = smooth_values.astype(jnp.bfloat16)
    cot_pad = pad_rows(wrap_cols(cotangent, 1))
    smooth_grad = conv_back(cot_pad, second_weight).astype(jnp.bfloat16)
    hidden_grad = pullback(smooth_grad.astype(jnp.float32))[0].astype(jnp.bfloat16)
    smooth_pad = pad_rows(wrap_cols(smooth, 1))
    second_grad = weight_grad(cotangent, smooth_pad) * grad_scale
    first_grad = weight_grad(hidden_grad, field_pad) * grad_scale
    hidden_pad = pad_rows(wrap_cols(hidden_grad, 1))
    field_grad = (cotangent.astype(jnp.float32) + conv_back(hidden_pad, first_weight)).astype(jnp.bfloat16)
    return (field_grad, first_grad, second_grad)
```

```python
import math

import jax
import jax.numpy as jnp
from jax import lax
from jax.experimental import pallas as pl
from jax.experimental.pallas import tpu as pltpu
from jax.sharding import PartitionSpec as P

MESH = pl.DeviceIdType.MESH
F32 = jnp.float32
BF16 = jnp.bfloat16
CH = 8
SP = 32
NB = 32
ROWS = 8
LANES = 128
PEERS = SP // 2
TILES = 3
TAPS = [(p, q) for p in (-1, 0, 1) for q in (-1, 0, 1)]


def tap(p, q):
    return 3 * (p + 1) + q + 1


def lane_ids(shape):
    return lax.broadcasted_iota(jnp.int32, shape, len(shape) - 1)


def roll(values, amount):
    amount = amount % LANES
    if amount == 0:
        return values
    return pltpu.roll(values, amount, 1)


def shift(main, ext, step):
    rolled, rolled_ext = roll(main, -step), roll(ext, -step)
    edge = lane_ids(main.shape) == (LANES - 1 if step == 1 else 0)
    return jnp.where(edge, rolled_ext, rolled), jnp.where(edge, rolled, rolled_ext)


def row_up(values, size):
    return jnp.concatenate([values[size:], jnp.zeros((size, LANES), F32)], axis=0)


def row_down(values, size):
    return jnp.concatenate([jnp.zeros((size, LANES), F32), values[:-size]], axis=0)


def row_of_lane(shape):
    return ((lane_ids(shape) + 8) // 16) % 8


def pack(tiles):
    total = jnp.zeros(tiles[0].shape, F32)
    owner = row_of_lane(tiles[0].shape)
    for r in range(ROWS):
        total = jnp.where(owner == r, roll(tiles[r], 16 * r), total)
    return total


def load_tap(prod, t, group, size):
    rows = pl.ds(pl.multiple_of(t * NB + group * size, 8), size)
    main = prod[0:ROWS, rows, :].reshape(ROWS * size, LANES)
    return main, prod[ROWS, rows, :]


def combine(prod, group, size):
    mains, packs = [], []
    owner = row_of_lane((size, LANES))
    for q in (-1, 0, 1):
        up_main, up_pack = load_tap(prod, tap(1, q), group, size)
        mid_main, mid_pack = load_tap(prod, tap(0, q), group, size)
        down_main, down_pack = load_tap(prod, tap(-1, q), group, size)
        mains.append(mid_main + row_up(up_main, size) + row_down(down_main, size))
        packs.append(
            mid_pack
            + jnp.where(owner == ROWS - 1, 0.0, roll(up_pack, -16))
            + jnp.where(owner == 0, 0.0, roll(down_pack, 16))
        )
    lane = lane_ids(mains[1].shape)
    left_edge, right_edge = lane == 0, lane == LANES - 1

    def expand(values, q):
        return jnp.concatenate([roll(values, -16 * r - q) for r in range(ROWS)], axis=0)

    before, before_ext = roll(mains[0], 1), expand(packs[0], -1)
    after, after_ext = roll(mains[2], -1), expand(packs[2], 1)
    main = mains[1] + jnp.where(left_edge, before_ext, before) + jnp.where(right_edge, after_ext, after)
    ext = (
        expand(packs[1], 0)
        + jnp.where(left_edge, before, before_ext)
        + jnp.where(right_edge, after, after_ext)
    )
    return main, ext


def gelu_both(v):
    scale = math.sqrt(2.0 / math.pi)
    square = v * v
    t = jnp.tanh(scale * v * (1.0 + 0.044715 * square))
    half = 0.5 * (1.0 + t)
    slope = half + 0.5 * v * (1.0 - t * t) * (scale * (1.0 + 3.0 * 0.044715 * square))
    return v * half, slope


def rounded(values):
    return values.astype(BF16).astype(F32)


def resample_forward(prod, group, size, slopes, smooth):
    h, h_ext = combine(prod, group, size)
    h, h_ext = rounded(h), rounded(h_ext)
    hc, hc_ext = shift(h, h_ext, 1)
    acts = []
    for part, (x, y) in enumerate(((h, hc), (h_ext, hc_ext))):
        x_low, y_low = row_up(x, size), row_up(y, size)
        points = (x, (x + y) * 0.5, (x + x_low) * 0.5, (x + y + x_low + y_low) * 0.25)
        values = []
        for kind, point in enumerate(points):
            value, slope = gelu_both(point)
            values.append(value)
            slopes[part, kind, :, group_rows(group, size), :] = slope.reshape(ROWS, size, LANES)
        acts.append(values)
    left_even = shift(acts[0][1], acts[1][1], -1)
    left_odd = shift(acts[0][3], acts[1][3], -1)
    out = []
    for part in range(2):
        even = (left_even[part] + 2.0 * acts[part][0] + acts[part][1]) * 0.25
        odd = (left_odd[part] + 2.0 * acts[part][2] + acts[part][3]) * 0.25
        out.append(rounded((row_down(odd, size) + 2.0 * even + odd) * 0.25))
    main, ext = out
    store_shifted(smooth, shift(main, ext, -1)[0], main, shift(main, ext, 1)[0], group, size)


def group_rows(group, size):
    return pl.ds(pl.multiple_of(group * size, 8), size)


def store_shifted(ref, *args):
    before, here, after, group, size = args
    for q, values in enumerate((before, here, after)):
        ref[q, 1 : ROWS + 1, group_rows(group, size), :] = values.reshape(ROWS, size, LANES)


def resample_backward(prod, group, size, slopes, grads, packed):
    g, g_ext = combine(prod, group, size)
    g, g_ext = rounded(g), rounded(g_ext)
    gc, gc_ext = shift(g, g_ext, 1)
    base, moved = [], []
    for part, (x, y) in enumerate(((g, gc), (g_ext, gc_ext))):
        odd = (x + row_up(x, size)) * 0.25
        odd_next = (y + row_up(y, size)) * 0.25
        ups = (x * 0.25, (x + y) * 0.125, odd * 0.5, (odd + odd_next) * 0.25)
        b = [
            up * slopes[part, kind, :, group_rows(group, size), :].reshape(ROWS * size, LANES)
            for kind, up in enumerate(ups)
        ]
        half = b[1] * 0.5 + (b[3] + row_down(b[3], size)) * 0.25
        base.append(b[0] + (b[2] + row_down(b[2], size)) * 0.5 + half)
        moved.append(half)
    left, left_ext = shift(moved[0], moved[1], -1)
    main, ext = rounded(base[0] + left), rounded(base[1] + left_ext)
    store_shifted(grads, shift(main, ext, 1)[0], main, shift(main, ext, -1)[0], group, size)
    packed[group_rows(group, size), :] = pack([ext[r * size : (r + 1) * size] for r in range(ROWS)])


def products(weights, block, halo, prod):
    for r in range(0, ROWS, 2):
        pair = jnp.concatenate(
            [block[:, r].reshape(CH * NB, LANES), block[:, r + 1].reshape(CH * NB, LANES)], axis=1
        )
        out = jnp.dot(weights[...], pair, preferred_element_type=F32)
        prod[r] = out[:, :LANES]
        prod[r + 1] = out[:, LANES:]
    prod[ROWS] = jnp.dot(weights[...], halo.reshape(CH * NB, LANES), preferred_element_type=F32)


def row_pair(block, r):
    return jnp.concatenate(
        [block[:, r].reshape(CH * NB, LANES), block[:, r + 1].reshape(CH * NB, LANES)], axis=1
    )


def tap_rows(ref, r, sign):
    return jnp.concatenate(
        [ref[:, r + sign * p + 1].reshape(3 * NB, LANES) for p in (-1, 0, 1)], axis=0
    )


def tap_row_pair(ref, r, sign):
    return jnp.concatenate([tap_rows(ref, r, sign), tap_rows(ref, r + 1, sign)], axis=1)


def contract_last(a, b):
    return lax.dot_general(a, b, (((1,), (1,)), ((), ())), preferred_element_type=F32)


def kernel(
    field_ref, w1_ref, w2_ref, cot_ref, out_ref, grads_ref,
    rows32, w32, gath, gath_halo, edge, edge_in, cot32, lhs1, lhs2, wsend, wrecv,
    prod, slopes, shifted32, shifted, packed32, hgath,
    g2send, g2recv, part, part_in, rs_send, rs_recv, piece, sib_in,
    edge_sems, main_sems, halo_sems, w_sems, hg_sems, g2_sems, part_sems, rs_sems, ag_sems, sib_sems,
):
    chan = lax.axis_index("chan")
    space = lax.axis_index("space")
    core = lax.rem(space, 2)
    chip = lax.div(space, 2)
    left = lax.rem(space + SP - 1, SP)
    right = lax.rem(space + 1, SP)
    sibling = space + 1 - 2 * core
    scale = 1.0 / math.sqrt(ROWS * LANES * SP)

    def chan_at(k):
        return lax.rem(chan + k, CH)

    def peer_at(k):
        return lax.rem(chip + k, PEERS)

    def peer_space(k):
        return peer_at(k) * 2 + core

    barrier = pltpu.get_barrier_semaphore()

    def greet(axis, target):
        pl.semaphore_signal(barrier, inc=1, device_id={axis: target}, device_id_type=MESH)

    greet("space", left)
    greet("space", right)

    @pl.loop(1, CH)
    def _(k):
        greet("chan", chan_at(k))

    @pl.loop(1, PEERS)
    def _(k):
        greet("space", peer_space(k))

    def remote(src, dst, sems, k, axis, target):
        return pltpu.make_async_remote_copy(
            src_ref=src, dst_ref=dst, send_sem=sems.at[0, k], recv_sem=sems.at[1, k],
            device_id={axis: target}, device_id_type=MESH,
        )

    for which, ref in enumerate((field_ref, cot_ref)):
        rows32[...] = ref[...].astype(F32).reshape(NB * ROWS, LANES)
        tiles = [rows32[pl.ds(r, NB, stride=ROWS), :] for r in range(ROWS)]
        for r in range(ROWS):
            gath[which, chan, r] = tiles[r].astype(BF16)
            if which == 1:
                cot32[r] = tiles[r]
        edge[which] = pack(tiles).astype(BF16)

    pl.semaphore_wait(barrier, CH - 1 + PEERS - 1 + 2)

    to_left = remote(edge, edge_in.at[0], edge_sems, 0, "space", left)
    to_right = remote(edge, edge_in.at[1], edge_sems, 1, "space", right)
    to_left.start()
    to_right.start()

    def main_copy(which, k, slot):
        return remote(
            gath.at[which, slot], gath.at[which, slot], main_sems.at[which], k, "chan", chan_at(k)
        )

    def halo_copy(k, slot):
        return remote(gath_halo.at[slot], gath_halo.at[slot], halo_sems, k, "chan", chan_at(k))

    for which in range(2):
        @pl.loop(1, CH)
        def _(k):
            main_copy(which, k, chan).start()

    for which, ref in enumerate((w1_ref, w2_ref)):
        w32[:, 0:9, :] = ref[...].astype(F32)
        if which == 0:
            for t in range(9):
                lhs1[t * NB : (t + 1) * NB, :] = w32[:, t, :].astype(BF16)
        lane = lane_ids((NB, LANES))
        for k in range(3):
            taps = range(4 * k, min(4 * k + 4, 9))
            loaded = [w32[:, 8 - t, :] for t in taps]
            for dest in range(CH):
                half, place = dest // 4, dest % 4
                total = jnp.zeros((NB, LANES), F32)
                for t, values in zip(taps, loaded):
                    source = values[:, half * LANES : (half + 1) * LANES]
                    total = jnp.where(
                        lane // NB == t % 4, roll(source, (t % 4 - place) * NB), total
                    )
                wsend[dest, which, k] = total.astype(BF16)

    def w_copy(k, dest, slot):
        return remote(wsend.at[dest], wrecv.at[slot], w_sems, k, "chan", chan_at(k))

    @pl.loop(1, CH)
    def _(k):
        w_copy(k, chan_at(k), chan).start()

    wrecv[chan] = wsend[chan]

    to_left.wait_recv()
    to_right.wait_recv()
    for which in range(2):
        from_right = edge_in[0, which].astype(F32)
        from_left = edge_in[1, which].astype(F32)
        merged = jnp.where(lane_ids((NB, LANES)) % 16 < 8, from_right, from_left)
        gath_halo[chan, which] = merged.astype(BF16)

    @pl.loop(1, CH)
    def _(k):
        halo_copy(k, chan).start()

    @pl.loop(1, CH)
    def _(k):
        main_copy(0, k, chan_at(CH - k)).wait_recv()
        halo_copy(k, chan_at(CH - k)).wait_recv()

    group_size = 8
    shifted32[:, 0] = jnp.zeros((3, NB, LANES), F32)
    shifted32[:, ROWS + 1] = jnp.zeros((3, NB, LANES), F32)
    products(lhs1, gath.at[0], gath_halo[:, 0], prod)

    @pl.loop(0, NB // group_size)
    def _(group):
        resample_forward(prod, group, group_size, slopes, shifted32)

    shifted[0] = shifted32[...].astype(BF16)

    @pl.loop(1, CH)
    def _(k):
        main_copy(1, k, chan_at(CH - k)).wait_recv()
        w_copy(k, chan_at(k), chan_at(CH - k)).wait_recv()

    for which in range(2):
        for k in range(3):
            turned = wrecv[:, which, k].reshape(CH * NB, LANES).T
            if k < 2:
                lhs2[which, k * LANES : (k + 1) * LANES, :] = turned
            else:
                lhs2[which, 2 * LANES :, :] = turned[:NB]
    products(lhs2.at[1], gath.at[1], gath_halo[:, 1], prod)

    @pl.loop(0, NB // group_size)
    def _(group):
        resample_backward(prod, group, group_size, slopes, shifted32, packed32)

    shifted[1] = shifted32[...].astype(BF16)
    hgath[chan, 0:ROWS] = shifted[1, 1, 1 : ROWS + 1]
    hgath[chan, ROWS] = packed32[...].astype(BF16)

    def hg_copy(k, slot):
        return remote(hgath.at[slot], hgath.at[slot], hg_sems, k, "chan", chan_at(k))

    @pl.loop(1, CH)
    def _(k):
        hg_copy(k, chan).start()

    total = jnp.zeros((CH * NB, 3 * LANES), F32)
    for r in range(0, ROWS, 2):
        rhs = tap_row_pair(shifted.at[0], r, 1)
        rhs = jnp.concatenate([rhs, jnp.zeros((3 * NB, 2 * LANES), BF16)], axis=0)
        total = total + contract_last(row_pair(gath.at[1], r), rhs)
    total = (total * scale).astype(BF16)
    for k in range(3):
        g2send[:, k] = total[:, k * LANES : (k + 1) * LANES].reshape(CH, NB, LANES)

    def g2_copy(k, dest, slot):
        return remote(g2send.at[dest], g2recv.at[slot], g2_sems, k, "chan", chan_at(k))

    @pl.loop(1, CH)
    def _(k):
        g2_copy(k, chan_at(k), chan).start()

    g2recv[chan] = g2send[chan]

    total = jnp.zeros((9 * NB, CH * NB), F32)
    for r in range(0, ROWS, 2):
        total = total + contract_last(
            tap_row_pair(shifted.at[1], r, -1), row_pair(gath.at[0], r)
        )
    part[0] = total * scale

    @pl.loop(1, CH)
    def _(k):
        g2_copy(k, chan_at(k), chan_at(CH - k)).wait_recv()

    lane = lane_ids((NB, LANES))
    for k in range(3):
        loaded = [g2recv[s, k].astype(F32) for s in range(CH)]
        for t in range(4 * k, min(4 * k + 4, 9)):
            for half in range(2):
                total = jnp.zeros((NB, LANES), F32)
                for place in range(4):
                    moved = roll(loaded[4 * half + place], (place - t % 4) * NB)
                    total = jnp.where(lane // NB == place, moved, total)
                part[1, t * NB : (t + 1) * NB, half * LANES : (half + 1) * LANES] = total

    swap = remote(part.at[1 - core], part_in, part_sems, 0, "space", sibling)
    swap.start()
    swap.wait_recv()
    for tile in range(0, 36, 2):
        rows = tile // 2 * 16
        both = part[core, rows : rows + 16, :] + part_in[rows : rows + 16, :]
        for half in range(2):
            rs_send[(tile + half) // TILES, (tile + half) % TILES] = both[
                :, half * LANES : (half + 1) * LANES
            ].astype(BF16)
    rs_send[12:] = jnp.zeros((4, TILES, 16, LANES), BF16)

    def rs_copy(k, dest, slot):
        return remote(rs_send.at[dest], rs_recv.at[slot], rs_sems, k, "space", peer_space(k))

    @pl.loop(1, PEERS)
    def _(k):
        rs_copy(k, peer_at(k), chip).start()

    rs_recv[chip] = rs_send[chip]

    @pl.loop(1, CH)
    def _(k):
        hg_copy(k, chan_at(CH - k)).wait_recv()

    products(lhs2.at[0], hgath, hgath[:, ROWS], prod)

    @pl.loop(0, NB // group_size)
    def _(group):
        main, _ = combine(prod, group, group_size)
        rows = group_rows(group, group_size)
        cot32[:, rows, :] = cot32[:, rows, :] + main.reshape(ROWS, group_size, LANES)

    out_ref[...] = cot32[...].astype(BF16)

    @pl.loop(1, PEERS)
    def _(k):
        rs_copy(k, peer_at(k), peer_at(PEERS - k)).wait_recv()

    total = rs_recv[0].astype(F32)
    for s in range(1, PEERS):
        total = total + rs_recv[s].astype(F32)
    piece[chip] = total.astype(BF16)

    def ag_copy(k, slot):
        return remote(piece.at[slot], piece.at[slot], ag_sems, k, "space", peer_space(k))

    def sib_copy(k, slot):
        return remote(piece.at[slot], sib_in.at[slot], sib_sems, k, "space", sibling)

    @pl.loop(1, PEERS)
    def _(k):
        ag_copy(k, chip).start()

    sib_copy(0, chip).start()

    @pl.loop(1, PEERS)
    def _(k):
        ag_copy(k, peer_at(PEERS - k)).wait_recv()
        sib_copy(k, peer_at(PEERS - k)).start()

    @pl.loop(0, PEERS)
    def _(k):
        sib_copy(k, peer_at(PEERS - k)).wait_recv()

    for tile in range(36):
        rows = slice(tile // 2 * 16, tile // 2 * 16 + 16)
        lanes = slice(tile % 2 * LANES, (tile % 2 + 1) * LANES)
        grads_ref[core, rows, lanes] = piece[tile // TILES, tile % TILES]
        grads_ref[1 - core, rows, lanes] = sib_in[tile // TILES, tile % TILES]

    to_left.wait_send()
    to_right.wait_send()
    swap.wait_send()
    sib_copy(0, chip).wait_send()

    @pl.loop(1, CH)
    def _(k):
        main_copy(0, k, chan).wait_send()
        main_copy(1, k, chan).wait_send()
        halo_copy(k, chan).wait_send()
        w_copy(k, chan_at(k), chan).wait_send()
        hg_copy(k, chan).wait_send()
        g2_copy(k, chan_at(k), chan).wait_send()

    @pl.loop(1, PEERS)
    def _(k):
        rs_copy(k, peer_at(k), chip).wait_send()
        ag_copy(k, chip).wait_send()
        sib_copy(k, peer_at(PEERS - k)).wait_send()


def on_device(field, first_weight, second_weight, cotangent):
    vmem = pl.BlockSpec(memory_space=pltpu.VMEM)
    dma = pltpu.SemaphoreType.DMA
    out, grads = pl.pallas_call(
        kernel,
        out_shape=(
            jax.ShapeDtypeStruct((ROWS, NB, LANES), BF16),
            jax.ShapeDtypeStruct((2, 9 * NB, CH * NB), BF16),
        ),
        in_specs=[vmem] * 4,
        out_specs=(vmem, vmem),
        scratch_shapes=[
            pltpu.VMEM((NB * ROWS, LANES), F32),
            pltpu.VMEM((NB, 16, CH * NB), F32),
            pltpu.VMEM((2, CH, ROWS, NB, LANES), BF16),
            pltpu.VMEM((CH, 2, NB, LANES), BF16),
            pltpu.VMEM((2, NB, LANES), BF16),
            pltpu.VMEM((2, 2, NB, LANES), BF16),
            pltpu.VMEM((ROWS, NB, LANES), F32),
            pltpu.VMEM((9 * NB, CH * NB), BF16),
            pltpu.VMEM((2, 9 * NB, CH * NB), BF16),
            pltpu.VMEM((CH, 2, 3, NB, LANES), BF16),
            pltpu.VMEM((CH, 2, 3, NB, LANES), BF16),
            pltpu.VMEM((ROWS + 1, 9 * NB, LANES), F32),
            pltpu.VMEM((2, 4, ROWS, NB, LANES), F32),
            pltpu.VMEM((3, ROWS + 2, NB, LANES), F32),
            pltpu.VMEM((2, 3, ROWS + 2, NB, LANES), BF16),
            pltpu.VMEM((NB, LANES), F32),
            pltpu.VMEM((CH, ROWS + 1, NB, LANES), BF16),
            pltpu.VMEM((CH, 3, NB, LANES), BF16),
            pltpu.VMEM((CH, 3, NB, LANES), BF16),
            pltpu.VMEM((2, 9 * NB, CH * NB), F32),
            pltpu.VMEM((9 * NB, CH * NB), F32),
            pltpu.VMEM((PEERS, TILES, 16, LANES), BF16),
            pltpu.VMEM((PEERS, TILES, 16, LANES), BF16),
            pltpu.VMEM((PEERS, TILES, 16, LANES), BF16),
            pltpu.VMEM((PEERS, TILES, 16, LANES), BF16),
            dma((2, 2)),
            dma((2, 2, CH)),
            dma((2, CH)),
            dma((2, CH)),
            dma((2, CH)),
            dma((2, CH)),
            dma((2, 1)),
            dma((2, PEERS)),
            dma((2, PEERS)),
            dma((2, PEERS)),
        ],
        compiler_params=pltpu.CompilerParams(
            collective_id=0, has_side_effects=True, vmem_limit_bytes=40 * 1024 * 1024
        ),
    )(field, first_weight, second_weight, cotangent)
    field_grad = out.transpose(1, 0, 2)
    grads = grads.astype(F32).reshape(2, 9, NB, CH * NB).transpose(0, 2, 1, 3)
    return (field_grad, grads[0], grads[1])


def solution(mesh):
    in_specs = (
        P("chan", None, "space"),
        P("chan", None, None),
        P("chan", None, None),
        P("chan", None, "space"),
    )
    out_specs = (P("chan", None, "space"), P("chan", None, None), P("chan", None, None))
    return jax.shard_map(
        on_device, mesh=mesh, in_specs=in_specs, out_specs=out_specs, check_vma=False
    )
```

```python
import math

import jax
import jax.numpy as jnp
from jax import lax
from jax.experimental import pallas as pl
from jax.experimental.pallas import tpu as pltpu
from jax.sharding import PartitionSpec as P

MESH = pl.DeviceIdType.MESH
F32 = jnp.float32
BF16 = jnp.bfloat16
CH = 8
SP = 32
NB = 32
ROWS = 8
LANES = 128
PEERS = SP // 2
OWNERS = 12
TILES = 3
TAPS = [(p, q) for p in (-1, 0, 1) for q in (-1, 0, 1)]


def tap(p, q):
    return 3 * (p + 1) + q + 1


def lane_ids(shape):
    return lax.broadcasted_iota(jnp.int32, shape, len(shape) - 1)


def roll(values, amount):
    amount = amount % LANES
    if amount == 0:
        return values
    return pltpu.roll(values, amount, 1)


def shift(main, ext, step):
    rolled, rolled_ext = roll(main, -step), roll(ext, -step)
    edge = lane_ids(main.shape) == (LANES - 1 if step == 1 else 0)
    return jnp.where(edge, rolled_ext, rolled), jnp.where(edge, rolled, rolled_ext)


def row_up(values, size):
    return jnp.concatenate([values[size:], jnp.zeros((size, LANES), F32)], axis=0)


def row_down(values, size):
    return jnp.concatenate([jnp.zeros((size, LANES), F32), values[:-size]], axis=0)


def row_of_lane(shape, offset=0):
    return ((lane_ids(shape) + 8 - offset) // 16) % 8


def pack(tiles):
    total = jnp.zeros(tiles[0].shape, F32)
    owner = row_of_lane(tiles[0].shape)
    for r in range(ROWS):
        total = jnp.where(owner == r, roll(tiles[r], 16 * r), total)
    return total


def load_tap(prod, t, group, size):
    rows = pl.ds(pl.multiple_of(t * NB + group * size, 8), size)
    main = prod[0:ROWS, rows, :].reshape(ROWS * size, LANES)
    return main, prod[ROWS, rows, :]


def combine(prod, group, size, offset=0):
    mains, packs = [], []
    owner = row_of_lane((size, LANES), offset)
    for q in (-1, 0, 1):
        up_main, up_pack = load_tap(prod, tap(1, q), group, size)
        mid_main, mid_pack = load_tap(prod, tap(0, q), group, size)
        down_main, down_pack = load_tap(prod, tap(-1, q), group, size)
        mains.append(mid_main + row_up(up_main, size) + row_down(down_main, size))
        packs.append(
            mid_pack
            + jnp.where(owner == ROWS - 1, 0.0, roll(up_pack, -16))
            + jnp.where(owner == 0, 0.0, roll(down_pack, 16))
        )
    lane = lane_ids(mains[1].shape)
    left_edge, right_edge = lane == 0, lane == LANES - 1

    def expand(values, q):
        return jnp.concatenate([roll(values, -16 * r - q - offset) for r in range(ROWS)], axis=0)

    before, before_ext = roll(mains[0], 1), expand(packs[0], -1)
    after, after_ext = roll(mains[2], -1), expand(packs[2], 1)
    main = mains[1] + jnp.where(left_edge, before_ext, before) + jnp.where(right_edge, after_ext, after)
    ext = (
        expand(packs[1], 0)
        + jnp.where(left_edge, before, before_ext)
        + jnp.where(right_edge, after, after_ext)
    )
    return main, ext


def gelu_both(v):
    scale = math.sqrt(2.0 / math.pi)
    square = v * v
    t = jnp.tanh(scale * v * (1.0 + 0.044715 * square))
    half = 0.5 * (1.0 + t)
    slope = half + 0.5 * v * (1.0 - t * t) * (scale * (1.0 + 3.0 * 0.044715 * square))
    return v * half, slope


def rounded(values):
    return values.astype(BF16).astype(F32)


def resample_forward(prod, group, size, slopes, smooth):
    h, h_ext = combine(prod, group, size)
    h, h_ext = rounded(h), rounded(h_ext)
    hc, hc_ext = shift(h, h_ext, 1)
    acts = []
    for part, (x, y) in enumerate(((h, hc), (h_ext, hc_ext))):
        x_low, y_low = row_up(x, size), row_up(y, size)
        points = (x, (x + y) * 0.5, (x + x_low) * 0.5, (x + y + x_low + y_low) * 0.25)
        values = []
        for kind, point in enumerate(points):
            value, slope = gelu_both(point)
            values.append(value)
            slopes[part, kind, :, group_rows(group, size), :] = slope.reshape(ROWS, size, LANES)
        acts.append(values)
    left_even = shift(acts[0][1], acts[1][1], -1)
    left_odd = shift(acts[0][3], acts[1][3], -1)
    out = []
    for part in range(2):
        even = (left_even[part] + 2.0 * acts[part][0] + acts[part][1]) * 0.25
        odd = (left_odd[part] + 2.0 * acts[part][2] + acts[part][3]) * 0.25
        out.append(rounded((row_down(odd, size) + 2.0 * even + odd) * 0.25))
    main, ext = out
    store_shifted(smooth, shift(main, ext, -1)[0], main, shift(main, ext, 1)[0], group, size)


def group_rows(group, size):
    return pl.ds(pl.multiple_of(group * size, 8), size)


def store_shifted(ref, *args):
    before, here, after, group, size = args
    for q, values in enumerate((before, here, after)):
        ref[q, 1 : ROWS + 1, group_rows(group, size), :] = values.reshape(ROWS, size, LANES)


def resample_backward(prod, group, size, slopes, grads, packed):
    g, g_ext = combine(prod, group, size, 8)
    g, g_ext = rounded(g), rounded(g_ext)
    gc, gc_ext = shift(g, g_ext, 1)
    base, moved = [], []
    for part, (x, y) in enumerate(((g, gc), (g_ext, gc_ext))):
        odd = (x + row_up(x, size)) * 0.25
        odd_next = (y + row_up(y, size)) * 0.25
        ups = (x * 0.25, (x + y) * 0.125, odd * 0.5, (odd + odd_next) * 0.25)
        b = [
            up * slopes[part, kind, :, group_rows(group, size), :].reshape(ROWS * size, LANES)
            for kind, up in enumerate(ups)
        ]
        half = b[1] * 0.5 + (b[3] + row_down(b[3], size)) * 0.25
        base.append(b[0] + (b[2] + row_down(b[2], size)) * 0.5 + half)
        moved.append(half)
    left, left_ext = shift(moved[0], moved[1], -1)
    main, ext = rounded(base[0] + left), rounded(base[1] + left_ext)
    store_shifted(grads, shift(main, ext, 1)[0], main, shift(main, ext, -1)[0], group, size)
    packed[group_rows(group, size), :] = pack([ext[r * size : (r + 1) * size] for r in range(ROWS)])


def products(weights, block, halo, prod):
    for r in range(0, ROWS, 2):
        pair = jnp.concatenate(
            [block[:, r].reshape(CH * NB, LANES), block[:, r + 1].reshape(CH * NB, LANES)], axis=1
        )
        out = jnp.dot(weights, pair, preferred_element_type=F32)
        prod[r] = out[:, :LANES]
        prod[r + 1] = out[:, LANES:]
    prod[ROWS] = jnp.dot(weights, halo.reshape(CH * NB, LANES), preferred_element_type=F32)


def row_pair(block, r):
    return jnp.concatenate(
        [block[:, r].reshape(CH * NB, LANES), block[:, r + 1].reshape(CH * NB, LANES)], axis=1
    )


def tap_rows(ref, r, sign):
    return jnp.concatenate(
        [ref[:, r + sign * p + 1].reshape(3 * NB, LANES) for p in (-1, 0, 1)], axis=0
    )


def tap_row_pair(ref, r, sign):
    return jnp.concatenate([tap_rows(ref, r, sign), tap_rows(ref, r + 1, sign)], axis=1)


def contract_last(a, b):
    return lax.dot_general(a, b, (((1,), (1,)), ((), ())), preferred_element_type=F32)


HOPS = (
    ((0, 0), (1, 0), (-1, 0)),
    ((0, 0), (-1, 0), (1, 0)),
    ((0, 0), (0, 1), (0, 1)),
    ((0, 0), (2, 0), (2, 0)),
    ((0, 1), (1, 0), (-1, 1)),
    ((0, 1), (-1, 0), (1, 1)),
    ((2, 0), (0, 1), (2, 1)),
)


def kernel(
    field_hbm, w1_hbm, w2_hbm, cot_hbm, out_ref, grads_ref,
    field_in, cot_in, w1_in, w_in,
    rows32, gath, halo, edge, edge_in, cot32, lhs2, wsend, wrecv,
    prod, slopes, shifted32, shifted, packed32, hgath,
    g2part, g2swap, g2send, g2recv, g1part, g1swap, rs_send, rs_recv, piece, sib_in,
    in_sems, edge_sems, main_sems, halo_sems, w_sems, wsib_sems, hg_sems, g2swap_sems, g2_sems,
    g1_sems, rs_sems, ag_sems, sib_sems,
):
    chan = lax.axis_index("chan")
    space = lax.axis_index("space")
    core = lax.rem(space, 2)
    chip = lax.div(space, 2)
    line, level = lax.div(chan, 2), lax.rem(chan, 2)
    left = lax.rem(space + SP - 1, SP)
    right = lax.rem(space + 1, SP)
    sibling = space + 1 - 2 * core
    scale = 1.0 / math.sqrt(ROWS * LANES * SP)

    def chan_at(k):
        return lax.rem(chan + k, CH)

    def block_at(place):
        step, other = place
        at = 1 - level if other else level
        return lax.rem(line + step + 4, 4) * 2 + at

    barrier = pltpu.get_barrier_semaphore()

    def greet(**target):
        pl.semaphore_signal(barrier, inc=1, device_id=target, device_id_type=MESH)

    greet(space=left)
    greet(space=right)

    @pl.loop(1, CH)
    def _(k):
        greet(chan=chan_at(k))
        greet(chan=chan_at(k), space=sibling)

    @pl.loop(1, PEERS)
    def _(k):
        greet(space=lax.rem(chip + k, PEERS) * 2 + core)

    def fetch(src, dst, k):
        return pltpu.make_async_copy(src, dst, in_sems.at[k])

    fetch(field_hbm, field_in, 0).start()
    fetch(cot_hbm, cot_in, 1).start()
    fetch(w1_hbm, w1_in, 2).start()

    @pl.when(core == 0)
    def _():
        fetch(w1_hbm, w_in, 3).start()

    @pl.when(core == 1)
    def _():
        fetch(w2_hbm, w_in, 3).start()

    def remote(src, dst, sems, k, **target):
        return pltpu.make_async_remote_copy(
            src_ref=src, dst_ref=dst, send_sem=sems.at[0, k], recv_sem=sems.at[1, k],
            device_id=target, device_id_type=MESH,
        )

    def hop(buf, sems, j):
        sent = block_at(HOPS[j][0])
        return remote(buf.at[sent], buf.at[sent], sems, j, chan=block_at(HOPS[j][1]))

    def hop_in(buf, sems, j):
        got = block_at(HOPS[j][2])
        return remote(buf.at[got], buf.at[got], sems, j, chan=block_at(HOPS[j][1]))

    def first_hops(buf, sems):
        for j in range(4):
            hop(buf, sems, j).start()

    def second_hops(buf, sems):
        hop_in(buf, sems, 2).wait_recv()
        hop(buf, sems, 4).start()
        hop(buf, sems, 5).start()
        hop_in(buf, sems, 3).wait_recv()
        hop(buf, sems, 6).start()

    def last_hops(buf, sems):
        for j in (0, 1, 4, 5, 6):
            hop_in(buf, sems, j).wait_recv()

    def split_rows(source):
        rows32[...] = source[...].astype(F32).reshape(NB * ROWS, LANES)
        return [rows32[pl.ds(r, NB, stride=ROWS), :] for r in range(ROWS)]

    fetch(field_hbm, field_in, 0).wait()
    field_rows = split_rows(field_in)
    for r in range(ROWS):
        gath[0, chan, r] = field_rows[r].astype(BF16)

    pl.semaphore_wait(barrier, 2 * (CH - 1) + PEERS - 1 + 2)
    first_hops(gath.at[0], main_sems.at[0])

    fetch(cot_hbm, cot_in, 1).wait()
    edge_field = pack(field_rows)
    cot_rows = split_rows(cot_in)
    for r in range(ROWS):
        gath[1, chan, r] = cot_rows[r].astype(BF16)
        cot32[r] = cot_rows[r]
    lane = lane_ids((NB, LANES))
    near = (lane % 16 < 4) | (lane % 16 >= 12)
    edge[...] = jnp.where(near, edge_field, roll(pack(cot_rows), 8)).astype(BF16)
    to_left = remote(edge, edge_in.at[0], edge_sems, 0, space=left)
    to_right = remote(edge, edge_in.at[1], edge_sems, 1, space=right)
    to_left.start()
    to_right.start()
    first_hops(gath.at[1], main_sems.at[1])

    fetch(w1_hbm, w1_in, 2).wait()
    fetch(w1_hbm, w_in, 3).wait()
    for k in range(3):
        taps = range(4 * k, min(4 * k + 4, 9))
        loaded = [w_in[8 - t].astype(F32) for t in taps]
        for dest in range(CH):
            half, place = dest // 4, dest % 4
            total = jnp.zeros((NB, LANES), F32)
            for t, values in zip(taps, loaded):
                source = values[:, half * LANES : (half + 1) * LANES]
                total = jnp.where(lane // NB == t % 4, roll(source, (t % 4 - place) * NB), total)
            wsend[dest, k] = total.astype(BF16)

    def w_copy(k, dest, slot):
        return remote(wsend.at[dest], wrecv.at[core, slot], w_sems, k, chan=chan_at(k))

    @pl.loop(1, CH)
    def _(k):
        w_copy(k, chan_at(k), chan).start()

    wrecv[core, chan] = wsend[chan]

    to_left.wait_recv()
    to_right.wait_recv()
    from_right = edge_in[0].astype(F32)
    from_left = edge_in[1].astype(F32)
    halo[chan] = jnp.where(lane % 8 < 4, from_right, from_left).astype(BF16)

    def halo_copy(k, slot):
        return remote(halo.at[slot], halo.at[slot], halo_sems, k, chan=chan_at(k))

    @pl.loop(1, CH)
    def _(k):
        halo_copy(k, chan).start()

    second_hops(gath.at[0], main_sems.at[0])
    second_hops(gath.at[1], main_sems.at[1])

    last_hops(gath.at[0], main_sems.at[0])

    @pl.loop(1, CH)
    def _(k):
        halo_copy(k, chan_at(CH - k)).wait_recv()

    group_size = 8
    shifted32[:, 0] = jnp.zeros((3, NB, LANES), F32)
    shifted32[:, ROWS + 1] = jnp.zeros((3, NB, LANES), F32)
    products(w1_in[...].reshape(9 * NB, CH * NB), gath.at[0], halo[...], prod)

    @pl.loop(0, NB // group_size)
    def _(group):
        resample_forward(prod, group, group_size, slopes, shifted32)

    shifted[0] = shifted32[...].astype(BF16)

    @pl.loop(1, CH)
    def _(k):
        w_copy(k, chan_at(k), chan_at(CH - k)).wait_recv()

    w_out = remote(wrecv.at[core], wrecv.at[core], wsib_sems, 0, space=sibling)
    w_out.start()

    last_hops(gath.at[1], main_sems.at[1])
    total = jnp.zeros((CH * NB, 3 * LANES), F32)
    for r in range(0, ROWS, 2):
        rhs = tap_row_pair(shifted.at[0], r, 1)
        rhs = jnp.concatenate([rhs, jnp.zeros((3 * NB, 2 * LANES), BF16)], axis=0)
        total = total + contract_last(row_pair(gath.at[1], r), rhs)
    total = total * scale
    for k in range(3):
        g2part[:, k] = total[:, k * LANES : (k + 1) * LANES].reshape(CH, NB, LANES)

    g2_swap = remote(g2part.at[pl.ds(4 - 4 * core, 4)], g2swap, g2swap_sems, 0, space=sibling)
    g2_swap.start()

    remote(wrecv.at[1 - core], wrecv.at[1 - core], wsib_sems, 0, space=sibling).wait_recv()

    def turn_weights(which):
        for k in range(3):
            turned = wrecv[which, :, k].reshape(CH * NB, LANES).T
            if k < 2:
                lhs2[which, k * LANES : (k + 1) * LANES, :] = turned
            else:
                lhs2[which, 2 * LANES :, :] = turned[:NB]

    turn_weights(1)
    products(lhs2[1], gath.at[1], halo[...], prod)

    def g2_copy(j, slot):
        return remote(
            g2send.at[j], g2recv.at[slot], g2_sems, slot, chan=core * 4 + j, space=2 * chip + 1
        )

    def g2_sent(j):
        return pltpu.make_async_remote_copy(
            src_ref=g2send.at[j], dst_ref=g2recv.at[chan], send_sem=g2_sems.at[0, j],
            recv_sem=g2_sems.at[1, chan],
            device_id={"chan": core * 4 + j, "space": 2 * chip + 1}, device_id_type=MESH,
        )

    g2_swap.wait_recv()
    for j in range(4):
        g2send[j] = (g2part[core * 4 + j] + g2swap[j]).astype(BF16)
        mine = (core == 1) & (core * 4 + j == chan)

        @pl.when(mine)
        def _():
            g2recv[chan] = g2send[j]

        @pl.when(jnp.logical_not(mine))
        def _():
            g2_sent(j).start()

    @pl.loop(0, NB // group_size)
    def _(group):
        resample_backward(prod, group, group_size, slopes, shifted32, packed32)

    shifted[1] = shifted32[...].astype(BF16)
    hgath[chan, 0:ROWS] = shifted[1, 1, 1 : ROWS + 1]
    hgath[chan, ROWS] = packed32[...].astype(BF16)
    first_hops(hgath, hg_sems)

    def g1_copy(p):
        return remote(g1part.at[p], g1swap.at[p], g1_sems, p, space=sibling)

    for p in range(3):
        total = jnp.zeros((3 * NB, CH * NB), F32)
        for r in range(0, ROWS, 2):
            lhs = jnp.concatenate(
                [shifted[1, :, r + i - p + 2].reshape(3 * NB, LANES) for i in range(2)], axis=1
            )
            total = total + contract_last(lhs, row_pair(gath.at[0], r))
        g1part[p] = total * scale

        @pl.when(core == 1)
        def _():
            g1_copy(p).start()

    def rs_copy(owner, slot):
        return pltpu.make_async_remote_copy(
            src_ref=rs_send.at[owner], dst_ref=rs_recv.at[slot], send_sem=rs_sems.at[0, owner],
            recv_sem=rs_sems.at[1, slot],
            device_id={"space": owner * 2 + core}, device_id_type=MESH,
        )

    def to_owners(low, high):
        @pl.loop(low, high)
        def _(owner):
            @pl.when(owner == chip)
            def _():
                rs_recv[chip] = rs_send[chip]

            @pl.when(owner != chip)
            def _():
                rs_copy(owner, chip).start()

    def put_tiles(first, values):
        for i in range(values.shape[0] // 16):
            for half in range(2):
                tile = first + 2 * i + half
                rs_send[tile // TILES, tile % TILES] = values[
                    16 * i : 16 * i + 16, half * LANES : (half + 1) * LANES
                ].astype(BF16)

    @pl.when(core == 1)
    def _():
        @pl.loop(0, CH)
        def _(s):
            @pl.when((s != chan) | (chan < 4))
            def _():
                g2_copy(0, s).wait_recv()

        for k in range(3):
            loaded = [g2recv[s, k].astype(F32) for s in range(CH)]
            for t in range(4 * k, min(4 * k + 4, 9)):
                halves = []
                for half in range(2):
                    total = jnp.zeros((NB, LANES), F32)
                    for place in range(4):
                        moved = roll(loaded[4 * half + place], (place - t % 4) * NB)
                        total = jnp.where(lane // NB == place, moved, total)
                    halves.append(total)
                put_tiles(4 * t, jnp.concatenate(halves, axis=1))
        to_owners(0, OWNERS)

    @pl.when(core == 0)
    def _():
        for p in range(3):
            g1_copy(p).wait_recv()
            put_tiles(12 * p, g1part[p] + g1swap[p])
            to_owners(4 * p, 4 * p + 4)

    second_hops(hgath, hg_sems)
    turn_weights(0)

    def ag_copy(k, slot):
        return pltpu.make_async_remote_copy(
            src_ref=piece.at[slot], dst_ref=piece.at[slot], send_sem=ag_sems.at[0, k],
            recv_sem=ag_sems.at[1, slot],
            device_id={"space": lax.rem(chip + k, PEERS) * 2 + core}, device_id_type=MESH,
        )

    def sib_copy(slot):
        return remote(piece.at[slot], sib_in.at[slot], sib_sems, slot, space=sibling)

    @pl.when(chip < OWNERS)
    def _():
        @pl.loop(1, PEERS)
        def _(k):
            rs_copy(0, lax.rem(chip + k, PEERS)).wait_recv()

        total = rs_recv[0].astype(F32)
        for s in range(1, PEERS):
            total = total + rs_recv[s].astype(F32)
        piece[chip] = total.astype(BF16)

        @pl.loop(1, PEERS)
        def _(k):
            ag_copy(k, chip).start()

        sib_copy(chip).start()

    last_hops(hgath, hg_sems)
    products(lhs2[0], hgath, hgath[:, ROWS], prod)

    @pl.loop(0, NB // group_size)
    def _(group):
        main, _ = combine(prod, group, group_size)
        rows = group_rows(group, group_size)
        cot32[:, rows, :] = cot32[:, rows, :] + main.reshape(ROWS, group_size, LANES)

    out_ref[...] = cot32[...].astype(BF16)

    @pl.loop(1, PEERS)
    def _(k):
        source = lax.rem(chip + k, PEERS)

        @pl.when(source < OWNERS)
        def _():
            ag_copy(k, source).wait_recv()
            sib_copy(source).start()

    @pl.loop(0, OWNERS)
    def _(source):
        sib_copy(source).wait_recv()

    for tile in range(4 * 9):
        rows = slice(tile // 2 * 16, tile // 2 * 16 + 16)
        lanes = slice(tile % 2 * LANES, (tile % 2 + 1) * LANES)
        grads_ref[core, rows, lanes] = piece[tile // TILES, tile % TILES]
        grads_ref[1 - core, rows, lanes] = sib_in[tile // TILES, tile % TILES]

    to_left.wait_send()
    to_right.wait_send()
    w_out.wait_send()
    g2_swap.wait_send()
    for buf, sems in ((gath.at[0], main_sems.at[0]), (gath.at[1], main_sems.at[1]), (hgath, hg_sems)):
        for j in range(len(HOPS)):
            hop(buf, sems, j).wait_send()

    @pl.loop(1, CH)
    def _(k):
        halo_copy(k, chan).wait_send()
        w_copy(k, chan_at(k), chan).wait_send()

    for j in range(4):
        @pl.when((core == 0) | (core * 4 + j != chan))
        def _():
            g2_sent(j).wait_send()

    @pl.when(core == 1)
    def _():
        for p in range(3):
            g1_copy(p).wait_send()

    @pl.loop(0, OWNERS)
    def _(owner):
        sib_copy(owner).wait_send()

        @pl.when(owner != chip)
        def _():
            rs_copy(owner, chip).wait_send()

    @pl.when(chip < OWNERS)
    def _():
        @pl.loop(1, PEERS)
        def _(k):
            ag_copy(k, chip).wait_send()


def on_device(field, first_weight, second_weight, cotangent):
    vmem = pl.BlockSpec(memory_space=pltpu.VMEM)
    hbm = pl.BlockSpec(memory_space=pl.ANY)
    dma = pltpu.SemaphoreType.DMA
    out, grads = pl.pallas_call(
        kernel,
        out_shape=(
            jax.ShapeDtypeStruct((ROWS, NB, LANES), BF16),
            jax.ShapeDtypeStruct((2, 9 * NB, CH * NB), BF16),
        ),
        in_specs=[hbm] * 4,
        out_specs=(vmem, vmem),
        scratch_shapes=[
            pltpu.VMEM((NB, ROWS, LANES), BF16),
            pltpu.VMEM((NB, ROWS, LANES), BF16),
            pltpu.VMEM((9, NB, CH * NB), BF16),
            pltpu.VMEM((9, NB, CH * NB), BF16),
            pltpu.VMEM((NB * ROWS, LANES), F32),
            pltpu.VMEM((2, CH, ROWS, NB, LANES), BF16),
            pltpu.VMEM((CH, NB, LANES), BF16),
            pltpu.VMEM((NB, LANES), BF16),
            pltpu.VMEM((2, NB, LANES), BF16),
            pltpu.VMEM((ROWS, NB, LANES), F32),
            pltpu.VMEM((2, 9 * NB, CH * NB), BF16),
            pltpu.VMEM((CH, 3, NB, LANES), BF16),
            pltpu.VMEM((2, CH, 3, NB, LANES), BF16),
            pltpu.VMEM((ROWS + 1, 9 * NB, LANES), F32),
            pltpu.VMEM((2, 4, ROWS, NB, LANES), F32),
            pltpu.VMEM((3, ROWS + 2, NB, LANES), F32),
            pltpu.VMEM((2, 3, ROWS + 2, NB, LANES), BF16),
            pltpu.VMEM((NB, LANES), F32),
            pltpu.VMEM((CH, ROWS + 1, NB, LANES), BF16),
            pltpu.VMEM((CH, 3, NB, LANES), F32),
            pltpu.VMEM((4, 3, NB, LANES), F32),
            pltpu.VMEM((4, 3, NB, LANES), BF16),
            pltpu.VMEM((CH, 3, NB, LANES), BF16),
            pltpu.VMEM((3, 3 * NB, CH * NB), F32),
            pltpu.VMEM((3, 3 * NB, CH * NB), F32),
            pltpu.VMEM((OWNERS, TILES, 16, LANES), BF16),
            pltpu.VMEM((PEERS, TILES, 16, LANES), BF16),
            pltpu.VMEM((OWNERS, TILES, 16, LANES), BF16),
            pltpu.VMEM((OWNERS, TILES, 16, LANES), BF16),
            dma((4,)),
            dma((2, 2)),
            dma((2, 2, len(HOPS))),
            dma((2, CH)),
            dma((2, CH)),
            dma((2, 1)),
            dma((2, len(HOPS))),
            dma((2, 1)),
            dma((2, CH)),
            dma((2, 3)),
            dma((2, PEERS)),
            dma((2, PEERS)),
            dma((2, OWNERS)),
        ],
        compiler_params=pltpu.CompilerParams(
            collective_id=0, has_side_effects=True, vmem_limit_bytes=40 * 1024 * 1024
        ),
    )(field, first_weight.transpose(1, 0, 2), second_weight.transpose(1, 0, 2), cotangent)
    field_grad = out.transpose(1, 0, 2)
    grads = grads.astype(F32).reshape(2, 9, NB, CH * NB).transpose(0, 2, 1, 3)
    return (field_grad, grads[0], grads[1])


def solution(mesh):
    in_specs = (
        P("chan", None, "space"),
        P("chan", None, None),
        P("chan", None, None),
        P("chan", None, "space"),
    )
    out_specs = (P("chan", None, "space"), P("chan", None, None), P("chan", None, None))
    return jax.shard_map(
        on_device, mesh=mesh, in_specs=in_specs, out_specs=out_specs, check_vma=False
    )
```

```python
import math

import jax
import jax.numpy as jnp
from jax import lax
from jax.experimental import pallas as pl
from jax.experimental.pallas import tpu as pltpu
from jax.sharding import PartitionSpec as P

MESH = pl.DeviceIdType.MESH
F32 = jnp.float32
BF16 = jnp.bfloat16
CH = 8
SP = 32
NB = 32
ROWS = 8
LANES = 128
PEERS = SP // 2
OWNERS = 12
PIECE = 48
TAPS = [(p, q) for p in (-1, 0, 1) for q in (-1, 0, 1)]


def tap(p, q):
    return 3 * (p + 1) + q + 1


def lane_ids(shape):
    return lax.broadcasted_iota(jnp.int32, shape, len(shape) - 1)


def roll(values, amount):
    amount = amount % LANES
    if amount == 0:
        return values
    return pltpu.roll(values, amount, 1)


def shift(main, ext, step):
    rolled, rolled_ext = roll(main, -step), roll(ext, -step)
    edge = lane_ids(main.shape) == (LANES - 1 if step == 1 else 0)
    return jnp.where(edge, rolled_ext, rolled), jnp.where(edge, rolled, rolled_ext)


def row_up(values, size):
    return jnp.concatenate([values[size:], jnp.zeros((size, LANES), F32)], axis=0)


def row_down(values, size):
    return jnp.concatenate([jnp.zeros((size, LANES), F32), values[:-size]], axis=0)


def row_of_lane(shape, offset=0):
    return ((lane_ids(shape) + 8 - offset) // 16) % 8


def pack(tiles):
    total = jnp.zeros(tiles[0].shape, F32)
    owner = row_of_lane(tiles[0].shape)
    for r in range(ROWS):
        total = jnp.where(owner == r, roll(tiles[r], 16 * r), total)
    return total


def load_tap(prod, t, group, size):
    rows = pl.ds(pl.multiple_of(t * NB + group * size, 8), size)
    main = prod[0:ROWS, rows, :].reshape(ROWS * size, LANES)
    return main, prod[ROWS, rows, :]


def combine(prod, group, size, offset=0):
    mains, packs = [], []
    owner = row_of_lane((size, LANES), offset)
    for q in (-1, 0, 1):
        up_main, up_pack = load_tap(prod, tap(1, q), group, size)
        mid_main, mid_pack = load_tap(prod, tap(0, q), group, size)
        down_main, down_pack = load_tap(prod, tap(-1, q), group, size)
        mains.append(mid_main + row_up(up_main, size) + row_down(down_main, size))
        packs.append(
            mid_pack
            + jnp.where(owner == ROWS - 1, 0.0, roll(up_pack, -16))
            + jnp.where(owner == 0, 0.0, roll(down_pack, 16))
        )
    lane = lane_ids(mains[1].shape)
    left_edge, right_edge = lane == 0, lane == LANES - 1

    def expand(values, q):
        return jnp.concatenate([roll(values, -16 * r - q - offset) for r in range(ROWS)], axis=0)

    before, before_ext = roll(mains[0], 1), expand(packs[0], -1)
    after, after_ext = roll(mains[2], -1), expand(packs[2], 1)
    main = mains[1] + jnp.where(left_edge, before_ext, before) + jnp.where(right_edge, after_ext, after)
    ext = (
        expand(packs[1], 0)
        + jnp.where(left_edge, before, before_ext)
        + jnp.where(right_edge, after, after_ext)
    )
    return main, ext


def gelu_both(v):
    scale = math.sqrt(2.0 / math.pi)
    square = v * v
    t = jnp.tanh(scale * v * (1.0 + 0.044715 * square))
    half = 0.5 * (1.0 + t)
    slope = half + 0.5 * v * (1.0 - t * t) * (scale * (1.0 + 3.0 * 0.044715 * square))
    return v * half, slope


def rounded(values):
    return values.astype(BF16).astype(F32)


def resample_forward(prod, group, size, slopes, smooth):
    h, h_ext = combine(prod, group, size)
    h, h_ext = rounded(h), rounded(h_ext)
    hc, hc_ext = shift(h, h_ext, 1)
    acts = []
    for part, (x, y) in enumerate(((h, hc), (h_ext, hc_ext))):
        x_low, y_low = row_up(x, size), row_up(y, size)
        points = (x, (x + y) * 0.5, (x + x_low) * 0.5, (x + y + x_low + y_low) * 0.25)
        values = []
        for kind, point in enumerate(points):
            value, slope = gelu_both(point)
            values.append(value)
            slopes[part, kind, :, group_rows(group, size), :] = slope.reshape(ROWS, size, LANES)
        acts.append(values)
    left_even = shift(acts[0][1], acts[1][1], -1)
    left_odd = shift(acts[0][3], acts[1][3], -1)
    out = []
    for part in range(2):
        even = (left_even[part] + 2.0 * acts[part][0] + acts[part][1]) * 0.25
        odd = (left_odd[part] + 2.0 * acts[part][2] + acts[part][3]) * 0.25
        out.append(rounded((row_down(odd, size) + 2.0 * even + odd) * 0.25))
    main, ext = out
    store_shifted(smooth, shift(main, ext, -1)[0], main, shift(main, ext, 1)[0], group, size)


def group_rows(group, size):
    return pl.ds(pl.multiple_of(group * size, 8), size)


def store_shifted(ref, *args):
    before, here, after, group, size = args
    for q, values in enumerate((before, here, after)):
        ref[q, 1 : ROWS + 1, group_rows(group, size), :] = values.reshape(ROWS, size, LANES)


def resample_backward(prod, group, size, slopes, grads, packed):
    g, g_ext = combine(prod, group, size, 8)
    g, g_ext = rounded(g), rounded(g_ext)
    gc, gc_ext = shift(g, g_ext, 1)
    base, moved = [], []
    for part, (x, y) in enumerate(((g, gc), (g_ext, gc_ext))):
        odd = (x + row_up(x, size)) * 0.25
        odd_next = (y + row_up(y, size)) * 0.25
        ups = (x * 0.25, (x + y) * 0.125, odd * 0.5, (odd + odd_next) * 0.25)
        b = [
            up * slopes[part, kind, :, group_rows(group, size), :].reshape(ROWS * size, LANES)
            for kind, up in enumerate(ups)
        ]
        half = b[1] * 0.5 + (b[3] + row_down(b[3], size)) * 0.25
        base.append(b[0] + (b[2] + row_down(b[2], size)) * 0.5 + half)
        moved.append(half)
    left, left_ext = shift(moved[0], moved[1], -1)
    main, ext = rounded(base[0] + left), rounded(base[1] + left_ext)
    store_shifted(grads, shift(main, ext, 1)[0], main, shift(main, ext, -1)[0], group, size)
    packed[group_rows(group, size), :] = pack([ext[r * size : (r + 1) * size] for r in range(ROWS)])


def products(weights, block, halo, prod):
    for r in range(0, ROWS, 2):
        pair = jnp.concatenate(
            [block[:, r].reshape(CH * NB, LANES), block[:, r + 1].reshape(CH * NB, LANES)], axis=1
        )
        out = jnp.dot(weights, pair, preferred_element_type=F32)
        prod[r] = out[:, :LANES]
        prod[r + 1] = out[:, LANES:]
    prod[ROWS] = jnp.dot(weights, halo.reshape(CH * NB, LANES), preferred_element_type=F32)


def row_pair(block, r):
    return jnp.concatenate(
        [block[:, r].reshape(CH * NB, LANES), block[:, r + 1].reshape(CH * NB, LANES)], axis=1
    )


def tap_rows(ref, r, sign):
    return jnp.concatenate(
        [ref[:, r + sign * p + 1].reshape(3 * NB, LANES) for p in (-1, 0, 1)], axis=0
    )


def tap_row_pair(ref, r, sign):
    return jnp.concatenate([tap_rows(ref, r, sign), tap_rows(ref, r + 1, sign)], axis=1)


def contract_last(a, b):
    return lax.dot_general(a, b, (((1,), (1,)), ((), ())), preferred_element_type=F32)


HOPS = (
    ((0, 0), (1, 0), (-1, 0)),
    ((0, 0), (-1, 0), (1, 0)),
    ((0, 0), (0, 1), (0, 1)),
    ((0, 0), (2, 0), (2, 0)),
    ((0, 1), (1, 0), (-1, 1)),
    ((0, 1), (-1, 0), (1, 1)),
    ((2, 0), (0, 1), (2, 1)),
)


def kernel(
    field_hbm, w1_hbm, w2_hbm, cot_hbm, out_ref, g1_ref, g2_ref,
    field_in, cot_in, w1_in, w_in,
    rows32, gath, halo, edge, edge_in, cot32, lhs2, wsend, wrecv,
    prod, slopes, shifted32, shifted, packed32, hgath,
    g2part, g2swap, g2send, g2recv, g1part, g1swap, rs_send, rs_recv, sums, sib_in,
    in_sems, edge_sems, main_sems, halo_sems, w_sems, tile_sems, wsib_sems, hg_sems, g2swap_sems, g2_sems,
    g1_sems, rs_sems, ag_sems, sib_sems,
):
    chan = lax.axis_index("chan")
    space = lax.axis_index("space")
    core = lax.rem(space, 2)
    chip = lax.div(space, 2)
    line, level = lax.div(chan, 2), lax.rem(chan, 2)
    column = lax.rem(chip, 4)
    left = lax.rem(space + SP - 1, SP)
    right = lax.rem(space + 1, SP)
    sibling = space + 1 - 2 * core
    scale = 1.0 / math.sqrt(ROWS * LANES * SP)

    def chan_at(k):
        return lax.rem(chan + k, CH)

    def block_at(place):
        step, other = place
        at = 1 - level if other else level
        return lax.rem(line + step + 4, 4) * 2 + at

    def fetch(src, dst, k):
        return pltpu.make_async_copy(src, dst, in_sems.at[k])

    fetch(field_hbm, field_in, 0).start()
    fetch(cot_hbm, cot_in, 1).start()

    barrier = pltpu.get_barrier_semaphore()

    def greet(**target):
        pl.semaphore_signal(barrier, inc=1, device_id=target, device_id_type=MESH)

    @pl.loop(1, CH)
    def _(k):
        greet(chan=chan_at(k))
        greet(chan=chan_at(k), space=sibling)

    greet(space=left)
    greet(space=right)

    @pl.loop(1, PEERS)
    def _(k):
        greet(space=lax.rem(chip + k, PEERS) * 2 + core)

    fetch(w1_hbm, w1_in, 2).start()

    @pl.when(core == 0)
    def _():
        fetch(w1_hbm, w_in, 3).start()

    @pl.when(core == 1)
    def _():
        fetch(w2_hbm, w_in, 3).start()

    def remote(src, dst, sems, k, **target):
        return pltpu.make_async_remote_copy(
            src_ref=src, dst_ref=dst, send_sem=sems.at[0, k], recv_sem=sems.at[1, k],
            device_id=target, device_id_type=MESH,
        )

    def hop(buf, sems, j):
        sent = block_at(HOPS[j][0])
        return remote(buf.at[sent], buf.at[sent], sems, j, chan=block_at(HOPS[j][1]))

    def hop_in(buf, sems, j):
        got = block_at(HOPS[j][2])
        return remote(buf.at[got], buf.at[got], sems, j, chan=block_at(HOPS[j][1]))

    def first_hops(buf, sems):
        for j in range(4):
            hop(buf, sems, j).start()

    def second_hops(buf, sems):
        hop_in(buf, sems, 2).wait_recv()
        hop(buf, sems, 4).start()
        hop(buf, sems, 5).start()
        hop_in(buf, sems, 3).wait_recv()
        hop(buf, sems, 6).start()

    def last_hops(buf, sems):
        for j in (0, 1, 4, 5, 6):
            hop_in(buf, sems, j).wait_recv()

    def split_rows(source):
        rows32[...] = source[...].astype(F32).reshape(NB * ROWS, LANES)
        return [rows32[pl.ds(r, NB, stride=ROWS), :] for r in range(ROWS)]

    lane = lane_ids((NB, LANES))
    fetch(field_hbm, field_in, 0).wait()
    field_rows = split_rows(field_in)
    for r in range(ROWS):
        gath[0, chan, r] = field_rows[r].astype(BF16)
    edge_field = pack(field_rows)
    fetch(cot_hbm, cot_in, 1).wait()
    cot_rows = split_rows(cot_in)
    for r in range(ROWS):
        gath[1, chan, r] = cot_rows[r].astype(BF16)
        cot32[r] = cot_rows[r]
    near = (lane % 16 < 4) | (lane % 16 >= 12)
    edge[...] = jnp.where(near, edge_field, roll(pack(cot_rows), 8)).astype(BF16)

    fetch(w1_hbm, w1_in, 2).wait()
    fetch(w1_hbm, w_in, 3).wait()

    def w_copy(k, dest, slot):
        return remote(wsend.at[dest], wrecv.at[core, column, slot], w_sems, k, chan=chan_at(k))

    @pl.when(column < 3)
    def _():
        loaded = [
            jnp.where(
                4 * column + u < 9, w_in[jnp.maximum(8 - 4 * column - u, 0)].astype(F32), 0.0
            )
            for u in range(4)
        ]
        for dest in range(CH):
            half, place = dest // 4, dest % 4
            total = jnp.zeros((NB, LANES), F32)
            for u, values in enumerate(loaded):
                source = values[:, half * LANES : (half + 1) * LANES]
                total = jnp.where(lane // NB == u, roll(source, (u - place) * NB), total)
            wsend[dest] = total.astype(BF16)
        wrecv[core, column, chan] = wsend[chan]

    pl.semaphore_wait(barrier, 2 * (CH - 1) + PEERS - 1 + 2)

    to_left = remote(edge, edge_in.at[0], edge_sems, 0, space=left)
    to_right = remote(edge, edge_in.at[1], edge_sems, 1, space=right)
    to_left.start()
    to_right.start()

    @pl.when(column < 3)
    def _():
        @pl.loop(1, CH)
        def _(k):
            w_copy(k, chan_at(k), chan).start()

    first_hops(gath.at[0], main_sems.at[0])

    to_left.wait_recv()
    to_right.wait_recv()
    from_right = edge_in[0].astype(F32)
    from_left = edge_in[1].astype(F32)
    halo[chan] = jnp.where(lane % 8 < 4, from_right, from_left).astype(BF16)

    def halo_copy(k, slot):
        return remote(halo.at[slot], halo.at[slot], halo_sems, k, chan=chan_at(k))

    @pl.loop(1, CH)
    def _(k):
        halo_copy(k, chan).start()

    first_hops(gath.at[1], main_sems.at[1])

    def tile_copy(k, tile):
        target = (chip - column + lax.rem(column + k, 4)) * 2 + core
        return pltpu.make_async_remote_copy(
            src_ref=wrecv.at[core, tile], dst_ref=wrecv.at[core, tile], send_sem=tile_sems.at[0, k],
            recv_sem=tile_sems.at[1, tile], device_id={"space": target}, device_id_type=MESH,
        )

    @pl.when(column < 3)
    def _():
        @pl.loop(1, CH)
        def _(k):
            w_copy(k, chan_at(k), chan_at(CH - k)).wait_recv()

        @pl.loop(1, 4)
        def _(k):
            tile_copy(k, column).start()

    second_hops(gath.at[0], main_sems.at[0])
    second_hops(gath.at[1], main_sems.at[1])

    @pl.loop(0, 3)
    def _(tile):
        @pl.when(tile != column)
        def _():
            tile_copy(1, tile).wait_recv()

    w_out = remote(wrecv.at[core], wrecv.at[core], wsib_sems, 0, space=sibling)
    w_out.start()

    last_hops(gath.at[0], main_sems.at[0])

    @pl.loop(1, CH)
    def _(k):
        halo_copy(k, chan_at(CH - k)).wait_recv()

    group_size = 8
    shifted32[:, 0] = jnp.zeros((3, NB, LANES), F32)
    shifted32[:, ROWS + 1] = jnp.zeros((3, NB, LANES), F32)
    products(w1_in[...].reshape(9 * NB, CH * NB), gath.at[0], halo[...], prod)

    @pl.loop(0, NB // group_size)
    def _(group):
        resample_forward(prod, group, group_size, slopes, shifted32)

    shifted[0] = shifted32[...].astype(BF16)

    last_hops(gath.at[1], main_sems.at[1])
    total = jnp.zeros((CH * NB, 3 * LANES), F32)
    for r in range(0, ROWS, 2):
        rhs = tap_row_pair(shifted.at[0], r, 1)
        rhs = jnp.concatenate([rhs, jnp.zeros((3 * NB, 2 * LANES), BF16)], axis=0)
        total = total + contract_last(row_pair(gath.at[1], r), rhs)
    total = total * scale
    for k in range(3):
        g2part[:, k] = total[:, k * LANES : (k + 1) * LANES].reshape(CH, NB, LANES)

    g2_swap = remote(g2part.at[pl.ds(4 - 4 * core, 4)], g2swap, g2swap_sems, 0, space=sibling)
    g2_swap.start()

    remote(wrecv.at[1 - core], wrecv.at[1 - core], wsib_sems, 0, space=sibling).wait_recv()

    def turn_weights(which):
        for k in range(3):
            turned = wrecv[which, k].reshape(CH * NB, LANES).T
            if k < 2:
                lhs2[which, k * LANES : (k + 1) * LANES, :] = turned
            else:
                lhs2[which, 2 * LANES :, :] = turned[:NB]

    turn_weights(1)
    products(lhs2[1], gath.at[1], halo[...], prod)

    def g2_copy(j, slot):
        return remote(
            g2send.at[j], g2recv.at[slot], g2_sems, slot, chan=core * 4 + j, space=2 * chip + 1
        )

    def g2_sent(j):
        return pltpu.make_async_remote_copy(
            src_ref=g2send.at[j], dst_ref=g2recv.at[chan], send_sem=g2_sems.at[0, j],
            recv_sem=g2_sems.at[1, chan],
            device_id={"chan": core * 4 + j, "space": 2 * chip + 1}, device_id_type=MESH,
        )

    g2_swap.wait_recv()
    for j in range(4):
        g2send[j] = (g2part[core * 4 + j] + g2swap[j]).astype(BF16)
        mine = (core == 1) & (core * 4 + j == chan)

        @pl.when(mine)
        def _():
            g2recv[chan] = g2send[j]

        @pl.when(jnp.logical_not(mine))
        def _():
            g2_sent(j).start()

    @pl.loop(0, NB // group_size)
    def _(group):
        resample_backward(prod, group, group_size, slopes, shifted32, packed32)

    shifted[1] = shifted32[...].astype(BF16)
    hgath[chan, 0:ROWS] = shifted[1, 1, 1 : ROWS + 1]
    hgath[chan, ROWS] = packed32[...].astype(BF16)
    first_hops(hgath, hg_sems)

    def g1_copy(p):
        return remote(g1part.at[p], g1swap.at[p], g1_sems, p, space=sibling)

    for p in range(3):
        total = jnp.zeros((3 * NB, CH * NB), F32)
        for r in range(0, ROWS, 2):
            lhs = jnp.concatenate(
                [shifted[1, :, r + i - p + 2].reshape(3 * NB, LANES) for i in range(2)], axis=1
            )
            total = total + contract_last(lhs, row_pair(gath.at[0], r))
        g1part[p] = total * scale

        @pl.when(core == 1)
        def _():
            g1_copy(p).start()

    def piece_of(ref, owner):
        rows = pl.ds(pl.multiple_of(lax.div(owner, 2) * PIECE, 16), PIECE)
        return ref.at[lax.rem(owner, 2), rows]

    def rs_copy(owner, slot):
        return pltpu.make_async_remote_copy(
            src_ref=piece_of(rs_send, owner), dst_ref=rs_recv.at[slot], send_sem=rs_sems.at[0, owner],
            recv_sem=rs_sems.at[1, slot],
            device_id={"space": owner * 2 + core}, device_id_type=MESH,
        )

    def to_owners(low, high):
        @pl.loop(low, high)
        def _(owner):
            @pl.when(owner == chip)
            def _():
                rs_recv[chip] = piece_of(rs_send, chip)[...]

            @pl.when(owner != chip)
            def _():
                rs_copy(owner, chip).start()

    def put_rows(first, values):
        for half in range(2):
            rs_send[half, first : first + values.shape[0]] = values[
                :, half * LANES : (half + 1) * LANES
            ].astype(BF16)

    @pl.when(core == 1)
    def _():
        @pl.loop(0, CH)
        def _(s):
            @pl.when((s != chan) | (chan < 4))
            def _():
                g2_copy(0, s).wait_recv()

        for k in range(3):
            loaded = [g2recv[s, k].astype(F32) for s in range(CH)]
            for t in range(4 * k, min(4 * k + 4, 9)):
                for half in range(2):
                    total = jnp.zeros((NB, LANES), F32)
                    for place in range(4):
                        moved = roll(loaded[4 * half + place], (place - t % 4) * NB)
                        total = jnp.where(lane // NB == place, moved, total)
                    rs_send[half, t * NB : (t + 1) * NB] = total.astype(BF16)
        to_owners(0, OWNERS)

    @pl.when(core == 0)
    def _():
        for p in range(3):
            g1_copy(p).wait_recv()
            put_rows(96 * p, g1part[p] + g1swap[p])
            to_owners(4 * p, 4 * p + 4)

    second_hops(hgath, hg_sems)
    turn_weights(0)

    def ag_copy(k, slot):
        return pltpu.make_async_remote_copy(
            src_ref=piece_of(sums, slot), dst_ref=piece_of(sums, slot), send_sem=ag_sems.at[0, k],
            recv_sem=ag_sems.at[1, slot],
            device_id={"space": lax.rem(chip + k, PEERS) * 2 + core}, device_id_type=MESH,
        )

    def sib_copy(slot):
        return remote(piece_of(sums, slot), piece_of(sib_in, slot), sib_sems, slot, space=sibling)

    @pl.when(chip < OWNERS)
    def _():
        @pl.loop(1, PEERS)
        def _(k):
            rs_copy(0, lax.rem(chip + k, PEERS)).wait_recv()

        total = rs_recv[0].astype(F32)
        for s in range(1, PEERS):
            total = total + rs_recv[s].astype(F32)
        piece_of(sums, chip)[...] = total.astype(BF16)

        @pl.loop(1, PEERS)
        def _(k):
            ag_copy(k, chip).start()

        sib_copy(chip).start()

    last_hops(hgath, hg_sems)
    products(lhs2[0], hgath, hgath[:, ROWS], prod)

    @pl.loop(0, NB // group_size)
    def _(group):
        main, _ = combine(prod, group, group_size)
        rows = group_rows(group, group_size)
        cot32[:, rows, :] = cot32[:, rows, :] + main.reshape(ROWS, group_size, LANES)

    for r in range(ROWS):
        rows32[pl.ds(r, NB, stride=ROWS), :] = cot32[r]
    out_ref[...] = rows32[...].reshape(NB, ROWS, LANES).astype(BF16)

    @pl.loop(1, PEERS)
    def _(k):
        source = lax.rem(chip + k, PEERS)

        @pl.when(source < OWNERS)
        def _():
            ag_copy(k, source).wait_recv()
            sib_copy(source).start()

    def store(source, which):
        for grad, ref in enumerate((g1_ref, g2_ref)):
            @pl.when(which == grad)
            def _():
                for half in range(2):
                    ref[:, half * LANES : (half + 1) * LANES] = source[half]

    store(sums, core)

    @pl.loop(0, OWNERS)
    def _(source):
        sib_copy(source).wait_recv()

    store(sib_in, 1 - core)

    to_left.wait_send()
    to_right.wait_send()
    w_out.wait_send()
    g2_swap.wait_send()
    for buf, sems in ((gath.at[0], main_sems.at[0]), (gath.at[1], main_sems.at[1]), (hgath, hg_sems)):
        for j in range(len(HOPS)):
            hop(buf, sems, j).wait_send()

    @pl.loop(1, CH)
    def _(k):
        halo_copy(k, chan).wait_send()

    @pl.when(column < 3)
    def _():
        @pl.loop(1, CH)
        def _(k):
            w_copy(k, chan_at(k), chan).wait_send()

        @pl.loop(1, 4)
        def _(k):
            tile_copy(k, column).wait_send()

    for j in range(4):
        @pl.when((core == 0) | (core * 4 + j != chan))
        def _():
            g2_sent(j).wait_send()

    @pl.when(core == 1)
    def _():
        for p in range(3):
            g1_copy(p).wait_send()

    @pl.loop(0, OWNERS)
    def _(owner):
        sib_copy(owner).wait_send()

        @pl.when(owner != chip)
        def _():
            rs_copy(owner, chip).wait_send()

    @pl.when(chip < OWNERS)
    def _():
        @pl.loop(1, PEERS)
        def _(k):
            ag_copy(k, chip).wait_send()


def on_device(field, first_weight, second_weight, cotangent):
    vmem = pl.BlockSpec(memory_space=pltpu.VMEM)
    hbm = pl.BlockSpec(memory_space=pltpu.HBM)
    dma = pltpu.SemaphoreType.DMA
    out, first_grad, second_grad = pl.pallas_call(
        kernel,
        out_shape=(
            jax.ShapeDtypeStruct((NB, ROWS, LANES), BF16),
            jax.ShapeDtypeStruct((9 * NB, CH * NB), BF16),
            jax.ShapeDtypeStruct((9 * NB, CH * NB), BF16),
        ),
        in_specs=[hbm] * 4,
        out_specs=(vmem, vmem, vmem),
        scratch_shapes=[
            pltpu.VMEM((NB, ROWS, LANES), BF16),
            pltpu.VMEM((NB, ROWS, LANES), BF16),
            pltpu.VMEM((9, NB, CH * NB), BF16),
            pltpu.VMEM((9, NB, CH * NB), BF16),
            pltpu.VMEM((NB * ROWS, LANES), F32),
            pltpu.VMEM((2, CH, ROWS, NB, LANES), BF16),
            pltpu.VMEM((CH, NB, LANES), BF16),
            pltpu.VMEM((NB, LANES), BF16),
            pltpu.VMEM((2, NB, LANES), BF16),
            pltpu.VMEM((ROWS, NB, LANES), F32),
            pltpu.VMEM((2, 9 * NB, CH * NB), BF16),
            pltpu.VMEM((CH, NB, LANES), BF16),
            pltpu.VMEM((2, 3, CH, NB, LANES), BF16),
            pltpu.VMEM((ROWS + 1, 9 * NB, LANES), F32),
            pltpu.VMEM((2, 4, ROWS, NB, LANES), F32),
            pltpu.VMEM((3, ROWS + 2, NB, LANES), F32),
            pltpu.VMEM((2, 3, ROWS + 2, NB, LANES), BF16),
            pltpu.VMEM((NB, LANES), F32),
            pltpu.VMEM((CH, ROWS + 1, NB, LANES), BF16),
            pltpu.VMEM((CH, 3, NB, LANES), F32),
            pltpu.VMEM((4, 3, NB, LANES), F32),
            pltpu.VMEM((4, 3, NB, LANES), BF16),
            pltpu.VMEM((CH, 3, NB, LANES), BF16),
            pltpu.VMEM((3, 3 * NB, CH * NB), F32),
            pltpu.VMEM((3, 3 * NB, CH * NB), F32),
            pltpu.VMEM((2, 9 * NB, LANES), BF16),
            pltpu.VMEM((PEERS, PIECE, LANES), BF16),
            pltpu.VMEM((2, 9 * NB, LANES), BF16),
            pltpu.VMEM((2, 9 * NB, LANES), BF16),
            dma((4,)),
            dma((2, 2)),
            dma((2, 2, len(HOPS))),
            dma((2, CH)),
            dma((2, CH)),
            dma((2, 4)),
            dma((2, 1)),
            dma((2, len(HOPS))),
            dma((2, 1)),
            dma((2, CH)),
            dma((2, 3)),
            dma((2, PEERS)),
            dma((2, PEERS)),
            dma((2, OWNERS)),
        ],
        compiler_params=pltpu.CompilerParams(
            collective_id=0, has_side_effects=True, vmem_limit_bytes=40 * 1024 * 1024
        ),
    )(
        *(
            pltpu.with_memory_space_constraint(x, pltpu.HBM)
            for x in (
                field, first_weight.transpose(1, 0, 2), second_weight.transpose(1, 0, 2), cotangent
            )
        )
    )

    def taps_inside(grad):
        return grad.astype(F32).reshape(9, NB, CH * NB).transpose(1, 0, 2)

    return (out, taps_inside(first_grad), taps_inside(second_grad))


def solution(mesh):
    in_specs = (
        P("chan", None, "space"),
        P("chan", None, None),
        P("chan", None, None),
        P("chan", None, "space"),
    )
    out_specs = (P("chan", None, "space"), P("chan", None, None), P("chan", None, None))
    return jax.shard_map(
        on_device, mesh=mesh, in_specs=in_specs, out_specs=out_specs, check_vma=False
    )
```

```python
import math

import jax
import jax.numpy as jnp
from jax import lax
from jax.experimental import pallas as pl
from jax.experimental.pallas import tpu as pltpu
from jax.sharding import PartitionSpec as P

MESH = pl.DeviceIdType.MESH
F32 = jnp.float32
BF16 = jnp.bfloat16
CH = 8
SP = 32
NB = 32
ROWS = 8
LANES = 128
PEERS = SP // 2
OWNERS = 12
PIECE = 48
TAPS = [(p, q) for p in (-1, 0, 1) for q in (-1, 0, 1)]


def tap(p, q):
    return 3 * (p + 1) + q + 1


def lane_ids(shape):
    return lax.broadcasted_iota(jnp.int32, shape, len(shape) - 1)


def roll(values, amount):
    amount = amount % LANES
    if amount == 0:
        return values
    return pltpu.roll(values, amount, 1)


def shift(main, ext, step):
    rolled, rolled_ext = roll(main, -step), roll(ext, -step)
    edge = lane_ids(main.shape) == (LANES - 1 if step == 1 else 0)
    return jnp.where(edge, rolled_ext, rolled), jnp.where(edge, rolled, rolled_ext)


def row_up(values, size):
    return jnp.concatenate([values[size:], jnp.zeros((size, LANES), F32)], axis=0)


def row_down(values, size):
    return jnp.concatenate([jnp.zeros((size, LANES), F32), values[:-size]], axis=0)


def row_of_lane(shape, offset=0):
    return ((lane_ids(shape) + 8 - offset) // 16) % 8


def pack(tiles):
    total = jnp.zeros(tiles[0].shape, F32)
    owner = row_of_lane(tiles[0].shape)
    for r in range(ROWS):
        total = jnp.where(owner == r, roll(tiles[r], 16 * r), total)
    return total


def load_tap(prod, t, group, size):
    rows = pl.ds(pl.multiple_of(t * NB + group * size, 8), size)
    main = prod[0:ROWS, rows, :].reshape(ROWS * size, LANES)
    return main, prod[ROWS, rows, :]


def combine(prod, group, size, offset=0):
    mains, packs = [], []
    owner = row_of_lane((size, LANES), offset)
    for q in (-1, 0, 1):
        up_main, up_pack = load_tap(prod, tap(1, q), group, size)
        mid_main, mid_pack = load_tap(prod, tap(0, q), group, size)
        down_main, down_pack = load_tap(prod, tap(-1, q), group, size)
        mains.append(mid_main + row_up(up_main, size) + row_down(down_main, size))
        packs.append(
            mid_pack
            + jnp.where(owner == ROWS - 1, 0.0, roll(up_pack, -16))
            + jnp.where(owner == 0, 0.0, roll(down_pack, 16))
        )
    lane = lane_ids(mains[1].shape)
    left_edge, right_edge = lane == 0, lane == LANES - 1

    def expand(values, q):
        return jnp.concatenate([roll(values, -16 * r - q - offset) for r in range(ROWS)], axis=0)

    before, before_ext = roll(mains[0], 1), expand(packs[0], -1)
    after, after_ext = roll(mains[2], -1), expand(packs[2], 1)
    main = mains[1] + jnp.where(left_edge, before_ext, before) + jnp.where(right_edge, after_ext, after)
    ext = (
        expand(packs[1], 0)
        + jnp.where(left_edge, before, before_ext)
        + jnp.where(right_edge, after, after_ext)
    )
    return main, ext


def gelu_both(v):
    scale = math.sqrt(2.0 / math.pi)
    square = v * v
    t = jnp.tanh(scale * v * (1.0 + 0.044715 * square))
    half = 0.5 * (1.0 + t)
    slope = half + 0.5 * v * (1.0 - t * t) * (scale * (1.0 + 3.0 * 0.044715 * square))
    return v * half, slope


def rounded(values):
    return values.astype(BF16).astype(F32)


def resample_forward(prod, group, size, slopes, smooth):
    h, h_ext = combine(prod, group, size)
    h, h_ext = rounded(h), rounded(h_ext)
    hc, hc_ext = shift(h, h_ext, 1)
    acts = []
    for part, (x, y) in enumerate(((h, hc), (h_ext, hc_ext))):
        x_low, y_low = row_up(x, size), row_up(y, size)
        points = (x, (x + y) * 0.5, (x + x_low) * 0.5, (x + y + x_low + y_low) * 0.25)
        values = []
        for kind, point in enumerate(points):
            value, slope = gelu_both(point)
            values.append(value)
            slopes[part, kind, :, group_rows(group, size), :] = slope.reshape(ROWS, size, LANES)
        acts.append(values)
    left_even = shift(acts[0][1], acts[1][1], -1)
    left_odd = shift(acts[0][3], acts[1][3], -1)
    out = []
    for part in range(2):
        even = (left_even[part] + 2.0 * acts[part][0] + acts[part][1]) * 0.25
        odd = (left_odd[part] + 2.0 * acts[part][2] + acts[part][3]) * 0.25
        out.append(rounded((row_down(odd, size) + 2.0 * even + odd) * 0.25))
    main, ext = out
    store_shifted(smooth, shift(main, ext, -1)[0], main, shift(main, ext, 1)[0], group, size)


def group_rows(group, size):
    return pl.ds(pl.multiple_of(group * size, 8), size)


def store_shifted(ref, *args):
    before, here, after, group, size = args
    for q, values in enumerate((before, here, after)):
        ref[q, 1 : ROWS + 1, group_rows(group, size), :] = values.reshape(ROWS, size, LANES)


def resample_backward(prod, group, size, slopes, grads, packed):
    g, g_ext = combine(prod, group, size, 8)
    g, g_ext = rounded(g), rounded(g_ext)
    gc, gc_ext = shift(g, g_ext, 1)
    base, moved = [], []
    for part, (x, y) in enumerate(((g, gc), (g_ext, gc_ext))):
        odd = (x + row_up(x, size)) * 0.25
        odd_next = (y + row_up(y, size)) * 0.25
        ups = (x * 0.25, (x + y) * 0.125, odd * 0.5, (odd + odd_next) * 0.25)
        b = [
            up * slopes[part, kind, :, group_rows(group, size), :].reshape(ROWS * size, LANES)
            for kind, up in enumerate(ups)
        ]
        half = b[1] * 0.5 + (b[3] + row_down(b[3], size)) * 0.25
        base.append(b[0] + (b[2] + row_down(b[2], size)) * 0.5 + half)
        moved.append(half)
    left, left_ext = shift(moved[0], moved[1], -1)
    main, ext = rounded(base[0] + left), rounded(base[1] + left_ext)
    store_shifted(grads, shift(main, ext, 1)[0], main, shift(main, ext, -1)[0], group, size)
    packed[group_rows(group, size), :] = pack([ext[r * size : (r + 1) * size] for r in range(ROWS)])


def products(weights, block, halo, prod):
    for r in range(0, ROWS, 2):
        pair = jnp.concatenate(
            [block[:, r].reshape(CH * NB, LANES), block[:, r + 1].reshape(CH * NB, LANES)], axis=1
        )
        out = jnp.dot(weights, pair, preferred_element_type=F32)
        prod[r] = out[:, :LANES]
        prod[r + 1] = out[:, LANES:]
    prod[ROWS] = jnp.dot(weights, halo.reshape(CH * NB, LANES), preferred_element_type=F32)


def row_pair(block, r):
    return jnp.concatenate(
        [block[:, r].reshape(CH * NB, LANES), block[:, r + 1].reshape(CH * NB, LANES)], axis=1
    )


def tap_rows(ref, r, sign):
    return jnp.concatenate(
        [ref[:, r + sign * p + 1].reshape(3 * NB, LANES) for p in (-1, 0, 1)], axis=0
    )


def tap_row_pair(ref, r, sign):
    return jnp.concatenate([tap_rows(ref, r, sign), tap_rows(ref, r + 1, sign)], axis=1)


def contract_last(a, b):
    return lax.dot_general(a, b, (((1,), (1,)), ((), ())), preferred_element_type=F32)


NEAREST = sorted(
    ((dz, dx) for dz in range(4) for dx in range(4) if dz or dx),
    key=lambda d: (2 * min(d[0], 4 - d[0]) + min(d[1], 4 - d[1]), d),
)

HOPS = (
    ((0, 0), (1, 0), (-1, 0)),
    ((0, 0), (-1, 0), (1, 0)),
    ((0, 0), (0, 1), (0, 1)),
    ((0, 0), (2, 0), (2, 0)),
    ((0, 1), (1, 0), (-1, 1)),
    ((0, 1), (-1, 0), (1, 1)),
    ((2, 0), (0, 1), (2, 1)),
)


def kernel(
    field_hbm, w1_hbm, w2_hbm, cot_hbm, out_ref, g1_ref, g2_ref,
    field_in, cot_in, w1_in, w_in,
    rows32, gath, halo, edge, edge_in, cot32, lhs2, wsend, wrecv,
    prod, slopes, shifted32, shifted, packed32, hgath,
    g2part, g2swap, g2send, g2recv, g1part, g1swap, rs_send, rs_recv, sums, sib_in,
    in_sems, edge_sems, main_sems, halo_sems, w_sems, tile_sems, wsib_sems, hg_sems, g2swap_sems, g2_sems,
    g1_sems, rs_sems, ag_sems, sib_sems,
):
    chan = lax.axis_index("chan")
    space = lax.axis_index("space")
    core = lax.rem(space, 2)
    chip = lax.div(space, 2)
    line, level = lax.div(chan, 2), lax.rem(chan, 2)
    column = lax.rem(chip, 4)
    plane = lax.div(chip, 4)
    left = lax.rem(space + SP - 1, SP)
    right = lax.rem(space + 1, SP)
    sibling = space + 1 - 2 * core
    scale = 1.0 / math.sqrt(ROWS * LANES * SP)

    def chan_at(k):
        return lax.rem(chan + k, CH)

    def chip_at(k):
        dz, dx = NEAREST[k]
        return lax.rem(plane + dz, 4) * 4 + lax.rem(column + dx, 4)

    def block_at(place):
        step, other = place
        at = 1 - level if other else level
        return lax.rem(line + step + 4, 4) * 2 + at

    def fetch(src, dst, k):
        return pltpu.make_async_copy(src, dst, in_sems.at[k])

    fetch(field_hbm, field_in, 0).start()
    fetch(cot_hbm, cot_in, 1).start()

    barrier = pltpu.get_barrier_semaphore()

    def greet(**target):
        pl.semaphore_signal(barrier, inc=1, device_id=target, device_id_type=MESH)

    @pl.loop(1, CH)
    def _(k):
        greet(chan=chan_at(k))
        greet(chan=chan_at(k), space=sibling)

    greet(space=left)
    greet(space=right)

    @pl.loop(1, PEERS)
    def _(k):
        greet(space=lax.rem(chip + k, PEERS) * 2 + core)

    fetch(w1_hbm, w1_in, 2).start()

    @pl.when(core == 0)
    def _():
        fetch(w1_hbm, w_in, 3).start()

    @pl.when(core == 1)
    def _():
        fetch(w2_hbm, w_in, 3).start()

    def remote(src, dst, sems, k, **target):
        return pltpu.make_async_remote_copy(
            src_ref=src, dst_ref=dst, send_sem=sems.at[0, k], recv_sem=sems.at[1, k],
            device_id=target, device_id_type=MESH,
        )

    def hop(buf, sems, j):
        sent = block_at(HOPS[j][0])
        return remote(buf.at[sent], buf.at[sent], sems, j, chan=block_at(HOPS[j][1]))

    def hop_in(buf, sems, j):
        got = block_at(HOPS[j][2])
        return remote(buf.at[got], buf.at[got], sems, j, chan=block_at(HOPS[j][1]))

    def send(buf, sems, *hops):
        for j in hops:
            hop(buf, sems, j).start()

    def arrive(buf, sems, *hops):
        for j in hops:
            hop_in(buf, sems, j).wait_recv()

    def second_hops(buf, sems):
        arrive(buf, sems, 2)
        send(buf, sems, 4, 5)
        arrive(buf, sems, 3)
        send(buf, sems, 6)

    def last_hops(buf, sems):
        arrive(buf, sems, 0, 1, 4, 5, 6)

    def split_rows(source):
        rows32[...] = source[...].astype(F32).reshape(NB * ROWS, LANES)
        return [rows32[pl.ds(r, NB, stride=ROWS), :] for r in range(ROWS)]

    lane = lane_ids((NB, LANES))
    fetch(field_hbm, field_in, 0).wait()
    field_rows = split_rows(field_in)
    for r in range(ROWS):
        gath[0, chan, r] = field_rows[r].astype(BF16)
    edge_field = pack(field_rows)
    fetch(cot_hbm, cot_in, 1).wait()
    cot_rows = split_rows(cot_in)
    for r in range(ROWS):
        gath[1, chan, r] = cot_rows[r].astype(BF16)
        cot32[r] = cot_rows[r]
    near = (lane % 16 < 4) | (lane % 16 >= 12)
    edge[...] = jnp.where(near, edge_field, roll(pack(cot_rows), 8)).astype(BF16)

    fetch(w1_hbm, w1_in, 2).wait()
    fetch(w1_hbm, w_in, 3).wait()

    def w_copy(k, dest, slot):
        return remote(wsend.at[dest], wrecv.at[core, column, slot], w_sems, k, chan=chan_at(k))

    @pl.when(column < 3)
    def _():
        loaded = [
            jnp.where(
                4 * column + u < 9, w_in[jnp.maximum(8 - 4 * column - u, 0)].astype(F32), 0.0
            )
            for u in range(4)
        ]
        for dest in range(CH):
            half, place = dest // 4, dest % 4
            total = jnp.zeros((NB, LANES), F32)
            for u, values in enumerate(loaded):
                source = values[:, half * LANES : (half + 1) * LANES]
                total = jnp.where(lane // NB == u, roll(source, (u - place) * NB), total)
            wsend[dest] = total.astype(BF16)
        wrecv[core, column, chan] = wsend[chan]

    pl.semaphore_wait(barrier, 2 * (CH - 1) + PEERS - 1 + 2)

    to_left = remote(edge, edge_in.at[0], edge_sems, 0, space=left)
    to_right = remote(edge, edge_in.at[1], edge_sems, 1, space=right)
    to_left.start()
    to_right.start()

    @pl.when(column < 3)
    def _():
        @pl.loop(1, CH)
        def _(k):
            w_copy(k, chan_at(k), chan).start()

    field_all, cot_all = (gath.at[0], main_sems.at[0]), (gath.at[1], main_sems.at[1])
    send(*field_all, 3, 2)
    send(*cot_all, 3, 2)
    send(*field_all, 0, 1)

    to_left.wait_recv()
    to_right.wait_recv()
    from_right = edge_in[0].astype(F32)
    from_left = edge_in[1].astype(F32)
    halo[chan] = jnp.where(lane % 8 < 4, from_right, from_left).astype(BF16)

    def halo_copy(k, slot):
        return remote(halo.at[slot], halo.at[slot], halo_sems, k, chan=chan_at(k))

    @pl.loop(1, CH)
    def _(k):
        halo_copy(k, chan).start()

    def tile_copy(k, tile):
        target = (chip - column + lax.rem(column + k, 4)) * 2 + core
        return pltpu.make_async_remote_copy(
            src_ref=wrecv.at[core, tile], dst_ref=wrecv.at[core, tile], send_sem=tile_sems.at[0, k],
            recv_sem=tile_sems.at[1, tile], device_id={"space": target}, device_id_type=MESH,
        )

    second_hops(*field_all)
    send(*cot_all, 0, 1)

    @pl.when(column < 3)
    def _():
        @pl.loop(1, CH)
        def _(k):
            w_copy(k, chan_at(k), chan_at(CH - k)).wait_recv()

        @pl.loop(1, 4)
        def _(k):
            tile_copy(k, column).start()

    second_hops(*cot_all)

    @pl.loop(0, 3)
    def _(tile):
        @pl.when(tile != column)
        def _():
            tile_copy(1, tile).wait_recv()

    w_out = remote(wrecv.at[core], wrecv.at[core], wsib_sems, 0, space=sibling)
    w_out.start()

    last_hops(*field_all)

    @pl.loop(1, CH)
    def _(k):
        halo_copy(k, chan_at(CH - k)).wait_recv()

    group_size = 8
    shifted32[:, 0] = jnp.zeros((3, NB, LANES), F32)
    shifted32[:, ROWS + 1] = jnp.zeros((3, NB, LANES), F32)
    products(w1_in[...].reshape(9 * NB, CH * NB), gath.at[0], halo[...], prod)

    @pl.loop(0, NB // group_size)
    def _(group):
        resample_forward(prod, group, group_size, slopes, shifted32)

    shifted[0] = shifted32[...].astype(BF16)

    last_hops(*cot_all)
    total = jnp.zeros((CH * NB, 3 * LANES), F32)
    for r in range(0, ROWS, 2):
        rhs = tap_row_pair(shifted.at[0], r, 1)
        rhs = jnp.concatenate([rhs, jnp.zeros((3 * NB, 2 * LANES), BF16)], axis=0)
        total = total + contract_last(row_pair(gath.at[1], r), rhs)
    total = total * scale
    for k in range(3):
        g2part[:, k] = total[:, k * LANES : (k + 1) * LANES].reshape(CH, NB, LANES)

    g2_swap = remote(g2part.at[pl.ds(4 - 4 * core, 4)], g2swap, g2swap_sems, 0, space=sibling)
    g2_swap.start()

    remote(wrecv.at[1 - core], wrecv.at[1 - core], wsib_sems, 0, space=sibling).wait_recv()

    def turn_weights(which):
        for k in range(3):
            turned = wrecv[which, k].reshape(CH * NB, LANES).T
            if k < 2:
                lhs2[which, k * LANES : (k + 1) * LANES, :] = turned
            else:
                lhs2[which, 2 * LANES :, :] = turned[:NB]

    turn_weights(1)
    products(lhs2[1], gath.at[1], halo[...], prod)

    def g2_copy(j, slot):
        return remote(
            g2send.at[j], g2recv.at[slot], g2_sems, slot, chan=core * 4 + j, space=2 * chip + 1
        )

    def g2_sent(j):
        return pltpu.make_async_remote_copy(
            src_ref=g2send.at[j], dst_ref=g2recv.at[chan], send_sem=g2_sems.at[0, j],
            recv_sem=g2_sems.at[1, chan],
            device_id={"chan": core * 4 + j, "space": 2 * chip + 1}, device_id_type=MESH,
        )

    g2_swap.wait_recv()
    for j in range(4):
        g2send[j] = (g2part[core * 4 + j] + g2swap[j]).astype(BF16)
        mine = (core == 1) & (core * 4 + j == chan)

        @pl.when(mine)
        def _():
            g2recv[chan] = g2send[j]

        @pl.when(jnp.logical_not(mine))
        def _():
            g2_sent(j).start()

    @pl.loop(0, NB // group_size)
    def _(group):
        resample_backward(prod, group, group_size, slopes, shifted32, packed32)

    shifted[1] = shifted32[...].astype(BF16)
    hgath[chan, 0:ROWS] = shifted[1, 1, 1 : ROWS + 1]
    hgath[chan, ROWS] = packed32[...].astype(BF16)
    send(hgath, hg_sems, 3, 2, 0, 1)

    def g1_copy(p):
        return remote(g1part.at[p], g1swap.at[p], g1_sems, p, space=sibling)

    for p in range(3):
        total = jnp.zeros((3 * NB, CH * NB), F32)
        for r in range(0, ROWS, 2):
            lhs = jnp.concatenate(
                [shifted[1, :, r + i - p + 2].reshape(3 * NB, LANES) for i in range(2)], axis=1
            )
            total = total + contract_last(lhs, row_pair(gath.at[0], r))
        g1part[p] = total * scale

        @pl.when(core == 1)
        def _():
            g1_copy(p).start()

    def piece_of(ref, owner):
        rows = pl.ds(pl.multiple_of(lax.div(owner, 2) * PIECE, 16), PIECE)
        return ref.at[lax.rem(owner, 2), rows]

    def rs_copy(owner, slot):
        return pltpu.make_async_remote_copy(
            src_ref=piece_of(rs_send, owner), dst_ref=rs_recv.at[slot], send_sem=rs_sems.at[0, owner],
            recv_sem=rs_sems.at[1, slot],
            device_id={"space": owner * 2 + core}, device_id_type=MESH,
        )

    def to_owners(low, high):
        @pl.loop(low, high)
        def _(owner):
            @pl.when(owner == chip)
            def _():
                rs_recv[chip] = piece_of(rs_send, chip)[...]

            @pl.when(owner != chip)
            def _():
                rs_copy(owner, chip).start()

    def put_rows(first, values):
        for half in range(2):
            rs_send[half, first : first + values.shape[0]] = values[
                :, half * LANES : (half + 1) * LANES
            ].astype(BF16)

    @pl.when(core == 1)
    def _():
        @pl.loop(0, CH)
        def _(s):
            @pl.when((s != chan) | (chan < 4))
            def _():
                g2_copy(0, s).wait_recv()

        for k in range(3):
            loaded = [g2recv[s, k].astype(F32) for s in range(CH)]
            for t in range(4 * k, min(4 * k + 4, 9)):
                for half in range(2):
                    total = jnp.zeros((NB, LANES), F32)
                    for place in range(4):
                        moved = roll(loaded[4 * half + place], (place - t % 4) * NB)
                        total = jnp.where(lane // NB == place, moved, total)
                    rs_send[half, t * NB : (t + 1) * NB] = total.astype(BF16)
        to_owners(0, OWNERS)

    @pl.when(core == 0)
    def _():
        for p in range(3):
            g1_copy(p).wait_recv()
            put_rows(96 * p, g1part[p] + g1swap[p])
            to_owners(4 * p, 4 * p + 4)

    second_hops(hgath, hg_sems)
    turn_weights(0)

    def ag_copy(k, slot):
        return pltpu.make_async_remote_copy(
            src_ref=piece_of(sums, slot), dst_ref=piece_of(sums, slot), send_sem=ag_sems.at[0, k],
            recv_sem=ag_sems.at[1, slot],
            device_id={"space": chip_at(k) * 2 + core}, device_id_type=MESH,
        )

    def sib_copy(slot):
        return remote(piece_of(sums, slot), piece_of(sib_in, slot), sib_sems, slot, space=sibling)

    @pl.when(chip < OWNERS)
    def _():
        @pl.loop(1, PEERS)
        def _(k):
            rs_copy(0, lax.rem(chip + k, PEERS)).wait_recv()

        total = rs_recv[0].astype(F32)
        for s in range(1, PEERS):
            total = total + rs_recv[s].astype(F32)
        piece_of(sums, chip)[...] = total.astype(BF16)

        for k in reversed(range(PEERS - 1)):
            ag_copy(k, chip).start()
        sib_copy(chip).start()

    last_hops(hgath, hg_sems)
    products(lhs2[0], hgath, hgath[:, ROWS], prod)

    @pl.loop(0, NB // group_size)
    def _(group):
        main, _ = combine(prod, group, group_size)
        rows = group_rows(group, group_size)
        cot32[:, rows, :] = cot32[:, rows, :] + main.reshape(ROWS, group_size, LANES)

    for r in range(ROWS):
        rows32[pl.ds(r, NB, stride=ROWS), :] = cot32[r]
    out_ref[...] = rows32[...].reshape(NB, ROWS, LANES).astype(BF16)

    for k in range(PEERS - 1):
        source = chip_at(k)

        @pl.when(source < OWNERS)
        def _():
            ag_copy(k, source).wait_recv()
            sib_copy(source).start()

    def store(source, which):
        for grad, ref in enumerate((g1_ref, g2_ref)):
            @pl.when(which == grad)
            def _():
                for half in range(2):
                    ref[:, half * LANES : (half + 1) * LANES] = source[half]

    store(sums, core)

    @pl.loop(0, OWNERS)
    def _(source):
        sib_copy(source).wait_recv()

    store(sib_in, 1 - core)

    to_left.wait_send()
    to_right.wait_send()
    w_out.wait_send()
    g2_swap.wait_send()
    for buf, sems in ((gath.at[0], main_sems.at[0]), (gath.at[1], main_sems.at[1]), (hgath, hg_sems)):
        for j in range(len(HOPS)):
            hop(buf, sems, j).wait_send()

    @pl.loop(1, CH)
    def _(k):
        halo_copy(k, chan).wait_send()

    @pl.when(column < 3)
    def _():
        @pl.loop(1, CH)
        def _(k):
            w_copy(k, chan_at(k), chan).wait_send()

        @pl.loop(1, 4)
        def _(k):
            tile_copy(k, column).wait_send()

    for j in range(4):
        @pl.when((core == 0) | (core * 4 + j != chan))
        def _():
            g2_sent(j).wait_send()

    @pl.when(core == 1)
    def _():
        for p in range(3):
            g1_copy(p).wait_send()

    @pl.loop(0, OWNERS)
    def _(owner):
        sib_copy(owner).wait_send()

        @pl.when(owner != chip)
        def _():
            rs_copy(owner, chip).wait_send()

    @pl.when(chip < OWNERS)
    def _():
        for k in range(PEERS - 1):
            ag_copy(k, chip).wait_send()


def on_device(field, first_weight, second_weight, cotangent):
    vmem = pl.BlockSpec(memory_space=pltpu.VMEM)
    hbm = pl.BlockSpec(memory_space=pltpu.HBM)
    dma = pltpu.SemaphoreType.DMA
    out, first_grad, second_grad = pl.pallas_call(
        kernel,
        out_shape=(
            jax.ShapeDtypeStruct((NB, ROWS, LANES), BF16),
            jax.ShapeDtypeStruct((9 * NB, CH * NB), BF16),
            jax.ShapeDtypeStruct((9 * NB, CH * NB), BF16),
        ),
        in_specs=[hbm] * 4,
        out_specs=(vmem, vmem, vmem),
        scratch_shapes=[
            pltpu.VMEM((NB, ROWS, LANES), BF16),
            pltpu.VMEM((NB, ROWS, LANES), BF16),
            pltpu.VMEM((9, NB, CH * NB), BF16),
            pltpu.VMEM((9, NB, CH * NB), BF16),
            pltpu.VMEM((NB * ROWS, LANES), F32),
            pltpu.VMEM((2, CH, ROWS, NB, LANES), BF16),
            pltpu.VMEM((CH, NB, LANES), BF16),
            pltpu.VMEM((NB, LANES), BF16),
            pltpu.VMEM((2, NB, LANES), BF16),
            pltpu.VMEM((ROWS, NB, LANES), F32),
            pltpu.VMEM((2, 9 * NB, CH * NB), BF16),
            pltpu.VMEM((CH, NB, LANES), BF16),
            pltpu.VMEM((2, 3, CH, NB, LANES), BF16),
            pltpu.VMEM((ROWS + 1, 9 * NB, LANES), F32),
            pltpu.VMEM((2, 4, ROWS, NB, LANES), F32),
            pltpu.VMEM((3, ROWS + 2, NB, LANES), F32),
            pltpu.VMEM((2, 3, ROWS + 2, NB, LANES), BF16),
            pltpu.VMEM((NB, LANES), F32),
            pltpu.VMEM((CH, ROWS + 1, NB, LANES), BF16),
            pltpu.VMEM((CH, 3, NB, LANES), F32),
            pltpu.VMEM((4, 3, NB, LANES), F32),
            pltpu.VMEM((4, 3, NB, LANES), BF16),
            pltpu.VMEM((CH, 3, NB, LANES), BF16),
            pltpu.VMEM((3, 3 * NB, CH * NB), F32),
            pltpu.VMEM((3, 3 * NB, CH * NB), F32),
            pltpu.VMEM((2, 9 * NB, LANES), BF16),
            pltpu.VMEM((PEERS, PIECE, LANES), BF16),
            pltpu.VMEM((2, 9 * NB, LANES), BF16),
            pltpu.VMEM((2, 9 * NB, LANES), BF16),
            dma((4,)),
            dma((2, 2)),
            dma((2, 2, len(HOPS))),
            dma((2, CH)),
            dma((2, CH)),
            dma((2, 4)),
            dma((2, 1)),
            dma((2, len(HOPS))),
            dma((2, 1)),
            dma((2, CH)),
            dma((2, 3)),
            dma((2, PEERS)),
            dma((2, PEERS)),
            dma((2, OWNERS)),
        ],
        compiler_params=pltpu.CompilerParams(
            collective_id=0, has_side_effects=True, vmem_limit_bytes=40 * 1024 * 1024
        ),
    )(
        *(
            pltpu.with_memory_space_constraint(x, pltpu.HBM)
            for x in (
                field, first_weight.transpose(1, 0, 2), second_weight.transpose(1, 0, 2), cotangent
            )
        )
    )

    def taps_inside(grad):
        return grad.astype(F32).reshape(9, NB, CH * NB).transpose(1, 0, 2)

    return (out, taps_inside(first_grad), taps_inside(second_grad))


def solution(mesh):
    in_specs = (
        P("chan", None, "space"),
        P("chan", None, None),
        P("chan", None, None),
        P("chan", None, "space"),
    )
    out_specs = (P("chan", None, "space"), P("chan", None, None), P("chan", None, None))
    return jax.shard_map(
        on_device, mesh=mesh, in_specs=in_specs, out_specs=out_specs, check_vma=False
    )
```

```python
import math

import jax
import jax.numpy as jnp
from jax import lax
from jax.experimental import pallas as pl
from jax.experimental.pallas import tpu as pltpu
from jax.sharding import PartitionSpec as P

MESH = pl.DeviceIdType.MESH
F32 = jnp.float32
BF16 = jnp.bfloat16
CH = 8
SP = 32
NB = 32
ROWS = 8
LANES = 128
PEERS = SP // 2
OWNERS = 12
PIECE = 48
TAPS = [(p, q) for p in (-1, 0, 1) for q in (-1, 0, 1)]


def tap(p, q):
    return 3 * (p + 1) + q + 1


def lane_ids(shape):
    return lax.broadcasted_iota(jnp.int32, shape, len(shape) - 1)


def roll(values, amount):
    amount = amount % LANES
    if amount == 0:
        return values
    return pltpu.roll(values, amount, 1)


def shift(main, ext, step):
    rolled, rolled_ext = roll(main, -step), roll(ext, -step)
    edge = lane_ids(main.shape) == (LANES - 1 if step == 1 else 0)
    return jnp.where(edge, rolled_ext, rolled), jnp.where(edge, rolled, rolled_ext)


def row_up(values, size):
    return jnp.concatenate([values[size:], jnp.zeros((size, LANES), F32)], axis=0)


def row_down(values, size):
    return jnp.concatenate([jnp.zeros((size, LANES), F32), values[:-size]], axis=0)


def row_of_lane(shape, offset=0):
    return ((lane_ids(shape) + 8 - offset) // 16) % 8


def pack(tiles):
    total = jnp.zeros(tiles[0].shape, F32)
    owner = row_of_lane(tiles[0].shape)
    for r in range(ROWS):
        total = jnp.where(owner == r, roll(tiles[r], 16 * r), total)
    return total


def load_tap(prod, t, group, size):
    rows = pl.ds(pl.multiple_of(t * NB + group * size, 8), size)
    main = prod[0:ROWS, rows, :].reshape(ROWS * size, LANES)
    return main, prod[ROWS, rows, :]


def combine(prod, group, size, offset=0):
    mains, packs = [], []
    owner = row_of_lane((size, LANES), offset)
    for q in (-1, 0, 1):
        up_main, up_pack = load_tap(prod, tap(1, q), group, size)
        mid_main, mid_pack = load_tap(prod, tap(0, q), group, size)
        down_main, down_pack = load_tap(prod, tap(-1, q), group, size)
        mains.append(mid_main + row_up(up_main, size) + row_down(down_main, size))
        packs.append(
            mid_pack
            + jnp.where(owner == ROWS - 1, 0.0, roll(up_pack, -16))
            + jnp.where(owner == 0, 0.0, roll(down_pack, 16))
        )
    lane = lane_ids(mains[1].shape)
    left_edge, right_edge = lane == 0, lane == LANES - 1

    def expand(values, q):
        return jnp.concatenate([roll(values, -16 * r - q - offset) for r in range(ROWS)], axis=0)

    before, before_ext = roll(mains[0], 1), expand(packs[0], -1)
    after, after_ext = roll(mains[2], -1), expand(packs[2], 1)
    main = mains[1] + jnp.where(left_edge, before_ext, before) + jnp.where(right_edge, after_ext, after)
    ext = (
        expand(packs[1], 0)
        + jnp.where(left_edge, before, before_ext)
        + jnp.where(right_edge, after, after_ext)
    )
    return main, ext


def gelu_both(v):
    scale = math.sqrt(2.0 / math.pi)
    square = v * v
    t = jnp.tanh(scale * v * (1.0 + 0.044715 * square))
    half = 0.5 * (1.0 + t)
    slope = half + 0.5 * v * (1.0 - t * t) * (scale * (1.0 + 3.0 * 0.044715 * square))
    return v * half, slope


def rounded(values):
    return values.astype(BF16).astype(F32)


def resample_forward(prod, group, size, slopes, smooth):
    h, h_ext = combine(prod, group, size)
    h, h_ext = rounded(h), rounded(h_ext)
    hc, hc_ext = shift(h, h_ext, 1)
    acts = []
    for part, (x, y) in enumerate(((h, hc), (h_ext, hc_ext))):
        x_low, y_low = row_up(x, size), row_up(y, size)
        points = (x, (x + y) * 0.5, (x + x_low) * 0.5, (x + y + x_low + y_low) * 0.25)
        values = []
        for kind, point in enumerate(points):
            value, slope = gelu_both(point)
            values.append(value)
            slopes[part, kind, :, group_rows(group, size), :] = slope.reshape(ROWS, size, LANES)
        acts.append(values)
    left_even = shift(acts[0][1], acts[1][1], -1)
    left_odd = shift(acts[0][3], acts[1][3], -1)
    out = []
    for part in range(2):
        even = (left_even[part] + 2.0 * acts[part][0] + acts[part][1]) * 0.25
        odd = (left_odd[part] + 2.0 * acts[part][2] + acts[part][3]) * 0.25
        out.append(rounded((row_down(odd, size) + 2.0 * even + odd) * 0.25))
    main, ext = out
    store_shifted(smooth, shift(main, ext, -1)[0], main, shift(main, ext, 1)[0], group, size)


def group_rows(group, size):
    return pl.ds(pl.multiple_of(group * size, 8), size)


def store_shifted(ref, *args):
    before, here, after, group, size = args
    for q, values in enumerate((before, here, after)):
        ref[q, 1 : ROWS + 1, group_rows(group, size), :] = values.reshape(ROWS, size, LANES)


def resample_backward(prod, group, size, slopes, grads, packed):
    g, g_ext = combine(prod, group, size, 8)
    g, g_ext = rounded(g), rounded(g_ext)
    gc, gc_ext = shift(g, g_ext, 1)
    base, moved = [], []
    for part, (x, y) in enumerate(((g, gc), (g_ext, gc_ext))):
        odd = (x + row_up(x, size)) * 0.25
        odd_next = (y + row_up(y, size)) * 0.25
        ups = (x * 0.25, (x + y) * 0.125, odd * 0.5, (odd + odd_next) * 0.25)
        b = [
            up * slopes[part, kind, :, group_rows(group, size), :].reshape(ROWS * size, LANES)
            for kind, up in enumerate(ups)
        ]
        half = b[1] * 0.5 + (b[3] + row_down(b[3], size)) * 0.25
        base.append(b[0] + (b[2] + row_down(b[2], size)) * 0.5 + half)
        moved.append(half)
    left, left_ext = shift(moved[0], moved[1], -1)
    main, ext = rounded(base[0] + left), rounded(base[1] + left_ext)
    store_shifted(grads, shift(main, ext, 1)[0], main, shift(main, ext, -1)[0], group, size)
    packed[group_rows(group, size), :] = pack([ext[r * size : (r + 1) * size] for r in range(ROWS)])


def products(weights, block, halo, prod):
    for r in range(0, ROWS, 2):
        pair = jnp.concatenate(
            [block[:, r].reshape(CH * NB, LANES), block[:, r + 1].reshape(CH * NB, LANES)], axis=1
        )
        out = jnp.dot(weights, pair, preferred_element_type=F32)
        prod[r] = out[:, :LANES]
        prod[r + 1] = out[:, LANES:]
    prod[ROWS] = jnp.dot(weights, halo.reshape(CH * NB, LANES), preferred_element_type=F32)


def row_pair(block, r):
    return jnp.concatenate(
        [block[:, r].reshape(CH * NB, LANES), block[:, r + 1].reshape(CH * NB, LANES)], axis=1
    )


def tap_rows(ref, r, sign):
    return jnp.concatenate(
        [ref[:, r + sign * p + 1].reshape(3 * NB, LANES) for p in (-1, 0, 1)], axis=0
    )


def tap_row_pair(ref, r, sign):
    return jnp.concatenate([tap_rows(ref, r, sign), tap_rows(ref, r + 1, sign)], axis=1)


def contract_last(a, b):
    return lax.dot_general(a, b, (((1,), (1,)), ((), ())), preferred_element_type=F32)


NEAREST = sorted(
    ((dz, dx) for dz in range(4) for dx in range(4) if dz or dx),
    key=lambda d: (2 * min(d[0], 4 - d[0]) + min(d[1], 4 - d[1]), d),
)

HOPS = (
    ((0, 0), (1, 0), (-1, 0)),
    ((0, 0), (-1, 0), (1, 0)),
    ((0, 0), (0, 1), (0, 1)),
    ((0, 0), (2, 0), (2, 0)),
    ((0, 1), (1, 0), (-1, 1)),
    ((0, 1), (-1, 0), (1, 1)),
    ((2, 0), (0, 1), (2, 1)),
    ((0, 1), (2, 0), (2, 1)),
)


def kernel(
    field_hbm, w1_hbm, w2_hbm, cot_hbm, out_ref, g1_ref, g2_ref,
    field_in, cot_in, w1_in, w_in,
    rows32, gath, halo, edge, edge_in, cot32, lhs2, wsend, wrecv,
    prod, slopes, shifted32, shifted, packed32, hgath,
    g2send, g2recv, g1part, g1swap, rs_send, rs_recv, sums, sib_in,
    in_sems, edge_sems, main_sems, halo_sems, w_sems, tile_sems, wsib_sems, hg_sems, g2_sems,
    g1_sems, rs_sems, ag_sems, sib_sems,
):
    chan = lax.axis_index("chan")
    space = lax.axis_index("space")
    core = lax.rem(space, 2)
    chip = lax.div(space, 2)
    line, level = lax.div(chan, 2), lax.rem(chan, 2)
    column = lax.rem(chip, 4)
    plane = lax.div(chip, 4)
    left = lax.rem(space + SP - 1, SP)
    right = lax.rem(space + 1, SP)
    sibling = space + 1 - 2 * core
    scale = 1.0 / math.sqrt(ROWS * LANES * SP)

    def chan_at(k):
        return lax.rem(chan + k, CH)

    def chip_at(k):
        dz, dx = NEAREST[k]
        return lax.rem(plane + dz, 4) * 4 + lax.rem(column + dx, 4)

    def block_at(place):
        step, other = place
        at = 1 - level if other else level
        return lax.rem(line + step + 4, 4) * 2 + at

    def fetch(src, dst, k):
        return pltpu.make_async_copy(src, dst, in_sems.at[k])

    fetch(field_hbm, field_in, 0).start()
    fetch(cot_hbm, cot_in, 1).start()

    barrier = pltpu.get_barrier_semaphore()

    def greet(**target):
        pl.semaphore_signal(barrier, inc=1, device_id=target, device_id_type=MESH)

    @pl.loop(1, CH)
    def _(k):
        greet(chan=chan_at(k))
        greet(chan=chan_at(k), space=sibling)

    greet(space=left)
    greet(space=right)

    @pl.loop(1, PEERS)
    def _(k):
        greet(space=lax.rem(chip + k, PEERS) * 2 + core)

    fetch(w1_hbm, w1_in, 2).start()

    @pl.when(core == 0)
    def _():
        fetch(w1_hbm, w_in, 3).start()

    @pl.when(core == 1)
    def _():
        fetch(w2_hbm, w_in, 3).start()

    def remote(src, dst, sems, k, **target):
        return pltpu.make_async_remote_copy(
            src_ref=src, dst_ref=dst, send_sem=sems.at[0, k], recv_sem=sems.at[1, k],
            device_id=target, device_id_type=MESH,
        )

    def hop(buf, sems, j):
        sent = block_at(HOPS[j][0])
        return remote(buf.at[sent], buf.at[sent], sems, j, chan=block_at(HOPS[j][1]))

    def hop_in(buf, sems, j):
        got = block_at(HOPS[j][2])
        return remote(buf.at[got], buf.at[got], sems, j, chan=block_at(HOPS[j][1]))

    def send(buf, sems, *hops):
        for j in hops:
            hop(buf, sems, j).start()

    def arrive(buf, sems, *hops):
        for j in hops:
            hop_in(buf, sems, j).wait_recv()

    def second_hops(buf, sems):
        arrive(buf, sems, 2)
        send(buf, sems, 4, 5)
        arrive(buf, sems, 3)
        send(buf, sems, 6)

    def last_hops(buf, sems):
        arrive(buf, sems, 0, 1, 4, 5, 6)

    def split_rows(source):
        rows32[...] = source[...].astype(F32).reshape(NB * ROWS, LANES)
        return [rows32[pl.ds(r, NB, stride=ROWS), :] for r in range(ROWS)]

    lane = lane_ids((NB, LANES))
    fetch(field_hbm, field_in, 0).wait()
    field_rows = split_rows(field_in)
    for r in range(ROWS):
        gath[0, chan, r] = field_rows[r].astype(BF16)
    edge_field = pack(field_rows)
    fetch(cot_hbm, cot_in, 1).wait()
    cot_rows = split_rows(cot_in)
    for r in range(ROWS):
        gath[1, chan, r] = cot_rows[r].astype(BF16)
        cot32[r] = cot_rows[r]
    near = (lane % 16 < 4) | (lane % 16 >= 12)
    edge[...] = jnp.where(near, edge_field, roll(pack(cot_rows), 8)).astype(BF16)

    fetch(w1_hbm, w1_in, 2).wait()
    fetch(w1_hbm, w_in, 3).wait()

    def w_copy(k, dest, slot):
        return remote(wsend.at[dest], wrecv.at[core, column, slot], w_sems, k, chan=chan_at(k))

    @pl.when(column < 3)
    def _():
        loaded = [
            jnp.where(
                4 * column + u < 9, w_in[jnp.maximum(8 - 4 * column - u, 0)].astype(F32), 0.0
            )
            for u in range(4)
        ]
        for dest in range(CH):
            half, place = dest // 4, dest % 4
            total = jnp.zeros((NB, LANES), F32)
            for u, values in enumerate(loaded):
                source = values[:, half * LANES : (half + 1) * LANES]
                total = jnp.where(lane // NB == u, roll(source, (u - place) * NB), total)
            wsend[dest] = total.astype(BF16)
        wrecv[core, column, chan] = wsend[chan]

    pl.semaphore_wait(barrier, 2 * (CH - 1) + PEERS - 1 + 2)

    to_left = remote(edge, edge_in.at[0], edge_sems, 0, space=left)
    to_right = remote(edge, edge_in.at[1], edge_sems, 1, space=right)
    to_left.start()
    to_right.start()

    @pl.when(column < 3)
    def _():
        @pl.loop(1, CH)
        def _(k):
            w_copy(k, chan_at(k), chan).start()

    field_all, cot_all = (gath.at[0], main_sems.at[0]), (gath.at[1], main_sems.at[1])
    send(*field_all, 3, 2)
    send(*cot_all, 3, 2)
    send(*field_all, 0, 1)

    to_left.wait_recv()
    to_right.wait_recv()
    from_right = edge_in[0].astype(F32)
    from_left = edge_in[1].astype(F32)
    halo[chan] = jnp.where(lane % 8 < 4, from_right, from_left).astype(BF16)

    def halo_copy(k, slot):
        return remote(halo.at[slot], halo.at[slot], halo_sems, k, chan=chan_at(k))

    @pl.loop(1, CH)
    def _(k):
        halo_copy(k, chan).start()

    def tile_copy(k, tile):
        target = (chip - column + lax.rem(column + k, 4)) * 2 + core
        return pltpu.make_async_remote_copy(
            src_ref=wrecv.at[core, tile], dst_ref=wrecv.at[core, tile], send_sem=tile_sems.at[0, k],
            recv_sem=tile_sems.at[1, tile], device_id={"space": target}, device_id_type=MESH,
        )

    second_hops(*field_all)
    send(*cot_all, 0, 1)

    @pl.when(column < 3)
    def _():
        @pl.loop(1, CH)
        def _(k):
            w_copy(k, chan_at(k), chan_at(CH - k)).wait_recv()

        @pl.loop(1, 4)
        def _(k):
            tile_copy(k, column).start()

    second_hops(*cot_all)

    @pl.loop(0, 3)
    def _(tile):
        @pl.when(tile != column)
        def _():
            tile_copy(1, tile).wait_recv()

    w_out = remote(wrecv.at[core], wrecv.at[core], wsib_sems, 0, space=sibling)
    w_out.start()

    last_hops(*field_all)

    @pl.loop(1, CH)
    def _(k):
        halo_copy(k, chan_at(CH - k)).wait_recv()

    group_size = 16
    shifted32[:, 0] = jnp.zeros((3, NB, LANES), F32)
    shifted32[:, ROWS + 1] = jnp.zeros((3, NB, LANES), F32)
    products(w1_in[...].reshape(9 * NB, CH * NB), gath.at[0], halo[...], prod)

    @pl.loop(0, NB // group_size)
    def _(group):
        resample_forward(prod, group, group_size, slopes, shifted32)

    shifted[0] = shifted32[...].astype(BF16)

    last_hops(*cot_all)
    total = jnp.zeros((CH * NB, 3 * LANES), F32)
    for r in range(0, ROWS, 2):
        rhs = tap_row_pair(shifted.at[0], r, 1)
        rhs = jnp.concatenate([rhs, jnp.zeros((3 * NB, 2 * LANES), BF16)], axis=0)
        total = total + contract_last(row_pair(gath.at[1], r), rhs)
    total = (total * scale).astype(BF16)
    for k in range(3):
        g2send[:, k] = total[:, k * LANES : (k + 1) * LANES].reshape(CH, NB, LANES)

    def g2_copy(dest, source_core, source):
        return pltpu.make_async_remote_copy(
            src_ref=g2send.at[dest], dst_ref=g2recv.at[source_core, source],
            send_sem=g2_sems.at[0, 0, dest], recv_sem=g2_sems.at[1, source_core, source],
            device_id={"chan": dest, "space": 2 * chip + 1}, device_id_type=MESH,
        )

    @pl.loop(1, CH)
    def _(k):
        g2_copy(chan_at(k), core, chan).start()

    @pl.when(core == 0)
    def _():
        g2_copy(chan, core, chan).start()

    @pl.when(core == 1)
    def _():
        g2recv[1, chan] = g2send[chan]

    remote(wrecv.at[1 - core], wrecv.at[1 - core], wsib_sems, 0, space=sibling).wait_recv()

    def turn_weights(which):
        for k in range(3):
            turned = wrecv[which, k].reshape(CH * NB, LANES).T
            if k < 2:
                lhs2[which, k * LANES : (k + 1) * LANES, :] = turned
            else:
                lhs2[which, 2 * LANES :, :] = turned[:NB]

    turn_weights(1)
    products(lhs2[1], gath.at[1], halo[...], prod)

    @pl.loop(0, NB // group_size)
    def _(group):
        resample_backward(prod, group, group_size, slopes, shifted32, packed32)

    shifted[1] = shifted32[...].astype(BF16)
    hgath[chan, 0:ROWS] = shifted[1, 1, 1 : ROWS + 1]
    hgath[chan, ROWS] = packed32[...].astype(BF16)
    send(hgath, hg_sems, *(2, 3, 0, 1))

    def g1_copy(p):
        return remote(g1part.at[p], g1swap.at[p], g1_sems, p, space=sibling)

    for p in range(3):
        total = jnp.zeros((3 * NB, CH * NB), F32)
        for r in range(0, ROWS, 2):
            lhs = jnp.concatenate(
                [shifted[1, :, r + i - p + 2].reshape(3 * NB, LANES) for i in range(2)], axis=1
            )
            total = total + contract_last(lhs, row_pair(gath.at[0], r))
        g1part[p] = total * scale

        @pl.when(core == 1)
        def _():
            g1_copy(p).start()

    def piece_of(ref, owner):
        rows = pl.ds(pl.multiple_of(lax.div(owner, 2) * PIECE, 16), PIECE)
        return ref.at[lax.rem(owner, 2), rows]

    def rs_copy(owner):
        slot = lax.rem(chip - owner + PEERS, PEERS) - 1
        return pltpu.make_async_remote_copy(
            src_ref=piece_of(rs_send, owner), dst_ref=rs_recv.at[slot], send_sem=rs_sems.at[0],
            recv_sem=rs_sems.at[1],
            device_id={"space": owner * 2 + core}, device_id_type=MESH,
        )

    def all_pieces(count):
        return pltpu.make_async_remote_copy(
            src_ref=rs_recv.at[pl.ds(0, count)], dst_ref=rs_recv.at[pl.ds(0, count)],
            send_sem=rs_sems.at[0], recv_sem=rs_sems.at[1],
            device_id={"space": sibling}, device_id_type=MESH,
        )

    def to_owners(low, high):
        @pl.loop(low, high)
        def _(owner):
            @pl.when(owner == chip)
            def _():
                rs_recv[PEERS - 1] = piece_of(rs_send, chip)[...]

            @pl.when(owner != chip)
            def _():
                rs_copy(owner).start()

    def put_rows(first, values):
        for half in range(2):
            rs_send[half, first : first + values.shape[0]] = values[
                :, half * LANES : (half + 1) * LANES
            ].astype(BF16)

    @pl.when(core == 1)
    def _():
        g2_copy(chan, 0, chan).wait_recv()

        @pl.loop(1, CH)
        def _(k):
            for source_core in range(2):
                g2_copy(chan, source_core, chan_at(k)).wait_recv()

        for k in range(3):
            loaded = [
                g2recv[0, s, k].astype(F32) + g2recv[1, s, k].astype(F32) for s in range(CH)
            ]
            for t in range(4 * k, min(4 * k + 4, 9)):
                for half in range(2):
                    total = jnp.zeros((NB, LANES), F32)
                    for place in range(4):
                        moved = roll(loaded[4 * half + place], (place - t % 4) * NB)
                        total = jnp.where(lane // NB == place, moved, total)
                    rs_send[half, t * NB : (t + 1) * NB] = total.astype(BF16)
        to_owners(0, OWNERS)

    @pl.when(core == 0)
    def _():
        for p in range(3):
            g1_copy(p).wait_recv()
            put_rows(96 * p, g1part[p] + g1swap[p])
            to_owners(4 * p, 4 * p + 4)

    arrive(hgath, hg_sems, 2)
    send(hgath, hg_sems, 7, 4, 5)
    turn_weights(0)

    def ag_copy(k, slot):
        return pltpu.make_async_remote_copy(
            src_ref=piece_of(sums, slot), dst_ref=piece_of(sums, slot), send_sem=ag_sems.at[0, k],
            recv_sem=ag_sems.at[1, slot],
            device_id={"space": chip_at(k) * 2 + core}, device_id_type=MESH,
        )

    def sib_copy(slot):
        return remote(piece_of(sums, slot), piece_of(sib_in, slot), sib_sems, slot, space=sibling)

    @pl.when(chip < OWNERS)
    def _():
        all_pieces(PEERS - 1).wait_recv()
        total = rs_recv[0].astype(F32)
        for s in range(1, PEERS):
            total = total + rs_recv[s].astype(F32)
        piece_of(sums, chip)[...] = total.astype(BF16)

        for k in reversed(range(PEERS - 1)):
            ag_copy(k, chip).start()
        sib_copy(chip).start()

    arrive(hgath, hg_sems, 0, 1, 3, 4, 5, 7)
    products(lhs2[0], hgath, hgath[:, ROWS], prod)

    @pl.loop(0, NB // group_size)
    def _(group):
        main, _ = combine(prod, group, group_size)
        rows = group_rows(group, group_size)
        cot32[:, rows, :] = cot32[:, rows, :] + main.reshape(ROWS, group_size, LANES)

    for r in range(ROWS):
        rows32[pl.ds(r, NB, stride=ROWS), :] = cot32[r]
    out_ref[...] = rows32[...].reshape(NB, ROWS, LANES).astype(BF16)

    for k in range(PEERS - 1):
        source = chip_at(k)

        @pl.when(source < OWNERS)
        def _():
            ag_copy(k, source).wait_recv()
            sib_copy(source).start()

    def store(source, which):
        for grad, ref in enumerate((g1_ref, g2_ref)):
            @pl.when(which == grad)
            def _():
                for half in range(2):
                    ref[:, half * LANES : (half + 1) * LANES] = source[half]

    store(sums, core)

    @pl.loop(0, OWNERS)
    def _(source):
        sib_copy(source).wait_recv()

    store(sib_in, 1 - core)

    to_left.wait_send()
    to_right.wait_send()
    w_out.wait_send()
    for buf, sems in ((gath.at[0], main_sems.at[0]), (gath.at[1], main_sems.at[1]), (hgath, hg_sems)):
        for j in (0, 1, 2, 3, 4, 5, 7 if buf is hgath else 6):
            hop(buf, sems, j).wait_send()

    @pl.loop(1, CH)
    def _(k):
        halo_copy(k, chan).wait_send()

    @pl.when(column < 3)
    def _():
        @pl.loop(1, CH)
        def _(k):
            w_copy(k, chan_at(k), chan).wait_send()

        @pl.loop(1, 4)
        def _(k):
            tile_copy(k, column).wait_send()

    @pl.loop(1, CH)
    def _(k):
        g2_copy(chan_at(k), core, chan).wait_send()

    @pl.when(core == 0)
    def _():
        g2_copy(chan, core, chan).wait_send()

    @pl.when(core == 1)
    def _():
        for p in range(3):
            g1_copy(p).wait_send()

    @pl.loop(0, OWNERS)
    def _(owner):
        sib_copy(owner).wait_send()

        @pl.when(owner != chip)
        def _():
            rs_copy(owner).wait_send()

    @pl.when(chip < OWNERS)
    def _():
        for k in range(PEERS - 1):
            ag_copy(k, chip).wait_send()


def on_device(field, first_weight, second_weight, cotangent):
    vmem = pl.BlockSpec(memory_space=pltpu.VMEM)
    hbm = pl.BlockSpec(memory_space=pltpu.HBM)
    dma = pltpu.SemaphoreType.DMA
    out, first_grad, second_grad = pl.pallas_call(
        kernel,
        out_shape=(
            jax.ShapeDtypeStruct((NB, ROWS, LANES), BF16),
            jax.ShapeDtypeStruct((9 * NB, CH * NB), BF16),
            jax.ShapeDtypeStruct((9 * NB, CH * NB), BF16),
        ),
        in_specs=[hbm] * 4,
        out_specs=(vmem, vmem, vmem),
        scratch_shapes=[
            pltpu.VMEM((NB, ROWS, LANES), BF16),
            pltpu.VMEM((NB, ROWS, LANES), BF16),
            pltpu.VMEM((9, NB, CH * NB), BF16),
            pltpu.VMEM((9, NB, CH * NB), BF16),
            pltpu.VMEM((NB * ROWS, LANES), F32),
            pltpu.VMEM((2, CH, ROWS, NB, LANES), BF16),
            pltpu.VMEM((CH, NB, LANES), BF16),
            pltpu.VMEM((NB, LANES), BF16),
            pltpu.VMEM((2, NB, LANES), BF16),
            pltpu.VMEM((ROWS, NB, LANES), F32),
            pltpu.VMEM((2, 9 * NB, CH * NB), BF16),
            pltpu.VMEM((CH, NB, LANES), BF16),
            pltpu.VMEM((2, 3, CH, NB, LANES), BF16),
            pltpu.VMEM((ROWS + 1, 9 * NB, LANES), F32),
            pltpu.VMEM((2, 4, ROWS, NB, LANES), F32),
            pltpu.VMEM((3, ROWS + 2, NB, LANES), F32),
            pltpu.VMEM((2, 3, ROWS + 2, NB, LANES), BF16),
            pltpu.VMEM((NB, LANES), F32),
            pltpu.VMEM((CH, ROWS + 1, NB, LANES), BF16),
            pltpu.VMEM((CH, 3, NB, LANES), BF16),
            pltpu.VMEM((2, CH, 3, NB, LANES), BF16),
            pltpu.VMEM((3, 3 * NB, CH * NB), F32),
            pltpu.VMEM((3, 3 * NB, CH * NB), F32),
            pltpu.VMEM((2, 9 * NB, LANES), BF16),
            pltpu.VMEM((PEERS, PIECE, LANES), BF16),
            pltpu.VMEM((2, 9 * NB, LANES), BF16),
            pltpu.VMEM((2, 9 * NB, LANES), BF16),
            dma((4,)),
            dma((2, 2)),
            dma((2, 2, len(HOPS))),
            dma((2, CH)),
            dma((2, CH)),
            dma((2, 4)),
            dma((2, 1)),
            dma((2, len(HOPS))),
            dma((2, 2, CH)),
            dma((2, 3)),
            dma((2,)),
            dma((2, PEERS)),
            dma((2, OWNERS)),
        ],
        compiler_params=pltpu.CompilerParams(
            collective_id=0, has_side_effects=True, vmem_limit_bytes=40 * 1024 * 1024
        ),
    )(
        *(
            pltpu.with_memory_space_constraint(x, pltpu.HBM)
            for x in (
                field, first_weight.transpose(1, 0, 2), second_weight.transpose(1, 0, 2), cotangent
            )
        )
    )

    def taps_inside(grad):
        return grad.astype(F32).reshape(9, NB, CH * NB).transpose(1, 0, 2)

    return (out, taps_inside(first_grad), taps_inside(second_grad))


def solution(mesh):
    in_specs = (
        P("chan", None, "space"),
        P("chan", None, None),
        P("chan", None, None),
        P("chan", None, "space"),
    )
    out_specs = (P("chan", None, "space"), P("chan", None, None), P("chan", None, None))
    return jax.shard_map(
        on_device, mesh=mesh, in_specs=in_specs, out_specs=out_specs, check_vma=False
    )
```

```python
import math

import jax
import jax.numpy as jnp
from jax import lax
from jax.experimental import pallas as pl
from jax.experimental.pallas import tpu as pltpu
from jax.sharding import PartitionSpec as P

MESH = pl.DeviceIdType.MESH
F32 = jnp.float32
BF16 = jnp.bfloat16
CH = 8
SP = 32
NB = 32
ROWS = 8
LANES = 128
PEERS = SP // 2
OWNERS = 12
PIECE = 48
TAPS = [(p, q) for p in (-1, 0, 1) for q in (-1, 0, 1)]


def tap(p, q):
    return 3 * (p + 1) + q + 1


def lane_ids(shape):
    return lax.broadcasted_iota(jnp.int32, shape, len(shape) - 1)


def roll(values, amount):
    amount = amount % LANES
    if amount == 0:
        return values
    return pltpu.roll(values, amount, 1)


def shift_main(main, ext, step):
    wraps = lane_ids(main.shape) == (0 if step == 1 else LANES - 1)
    return roll(jnp.where(wraps, ext, main), -step)


def shift(main, ext, step):
    return shift_main(main, ext, step), shift_main(ext, main, step)


def row_up(values, size):
    return jnp.concatenate([values[size:], jnp.zeros((size, LANES), F32)], axis=0)


def row_down(values, size):
    return jnp.concatenate([jnp.zeros((size, LANES), F32), values[:-size]], axis=0)


def row_of_lane(shape, offset=0):
    return ((lane_ids(shape) + 8 - offset) // 16) % 8


def pack(tiles):
    total = jnp.zeros(tiles[0].shape, F32)
    owner = row_of_lane(tiles[0].shape)
    for r in range(ROWS):
        total = jnp.where(owner == r, roll(tiles[r], 16 * r), total)
    return total


def load_tap(prod, t, group, size):
    rows = pl.ds(pl.multiple_of(t * NB + group * size, 8), size)
    main = prod[0:ROWS, rows, :].reshape(ROWS * size, LANES)
    return main, prod[ROWS, rows, :]


def combine(prod, group, size, offset=0):
    mains, packs = [], []
    owner = row_of_lane((size, LANES), offset)
    for q in (-1, 0, 1):
        up_main, up_pack = load_tap(prod, tap(1, q), group, size)
        mid_main, mid_pack = load_tap(prod, tap(0, q), group, size)
        down_main, down_pack = load_tap(prod, tap(-1, q), group, size)
        mains.append(mid_main + row_up(up_main, size) + row_down(down_main, size))
        packs.append(
            mid_pack
            + jnp.where(owner == ROWS - 1, 0.0, roll(up_pack, -16))
            + jnp.where(owner == 0, 0.0, roll(down_pack, 16))
        )
    near = (lane_ids((size, LANES)) - offset) % 16
    from_left, from_right = roll(packs[0], 1), roll(packs[2], -1)
    edges = jnp.where(near == 0, from_left, from_right)
    outer = packs[1] + jnp.where(near == 0, 0.0, from_left) + jnp.where(near == 15, 0.0, from_right)

    def expand(values):
        return jnp.concatenate([roll(values, -16 * r - offset) for r in range(ROWS)], axis=0)

    lane = lane_ids(mains[1].shape)
    first, last = lane == 0, lane == LANES - 1
    before, after, edges = roll(mains[0], 1), roll(mains[2], -1), expand(edges)
    main = mains[1] + jnp.where(first, edges, before) + jnp.where(last, edges, after)
    ext = expand(outer) + jnp.where(first, before, 0.0) + jnp.where(last, after, 0.0)
    return main, ext


def gelu_both(v):
    scale = math.sqrt(2.0 / math.pi)
    square = v * v
    t = jnp.tanh(scale * v * (1.0 + 0.044715 * square))
    half = 0.5 * (1.0 + t)
    slope = half + 0.5 * v * (1.0 - t * t) * (scale * (1.0 + 3.0 * 0.044715 * square))
    return v * half, slope


def rounded(values):
    return values.astype(BF16).astype(F32)


def resample_forward(prod, group, size, slopes, smooth):
    h, h_ext = combine(prod, group, size)
    h, h_ext = rounded(h), rounded(h_ext)
    hc, hc_ext = shift(h, h_ext, 1)
    acts = []
    for part, (x, y) in enumerate(((h, hc), (h_ext, hc_ext))):
        x_low, y_low = row_up(x, size), row_up(y, size)
        points = (x, (x + y) * 0.5, (x + x_low) * 0.5, (x + y + x_low + y_low) * 0.25)
        values = []
        for kind, point in enumerate(points):
            value, slope = gelu_both(point)
            values.append(value)
            slopes[part, kind, :, group_rows(group, size), :] = slope.reshape(ROWS, size, LANES)
        acts.append(values)
    base, moved = [], []
    for values in acts:
        side = 2.0 * values[1] + values[3] + row_down(values[3], size)
        base.append(side + 4.0 * values[0] + 2.0 * (values[2] + row_down(values[2], size)))
        moved.append(side)
    left, left_ext = shift(moved[0], moved[1], -1)
    main, ext = rounded((base[0] + left) * 0.0625), rounded((base[1] + left_ext) * 0.0625)
    store_shifted(smooth, shift_main(main, ext, -1), main, shift_main(main, ext, 1), group, size)


def group_rows(group, size):
    return pl.ds(pl.multiple_of(group * size, 8), size)


def store_shifted(ref, *args):
    before, here, after, group, size = args
    for q, values in enumerate((before, here, after)):
        ref[q, 1 : ROWS + 1, group_rows(group, size), :] = values.reshape(ROWS, size, LANES)


def resample_backward(prod, group, size, slopes, grads, packed):
    g, g_ext = combine(prod, group, size, 8)
    g, g_ext = rounded(g), rounded(g_ext)
    gc, gc_ext = shift(g, g_ext, 1)
    base, moved = [], []
    for part, (x, y) in enumerate(((g, gc), (g_ext, gc_ext))):
        odd = (x + row_up(x, size)) * 0.25
        odd_next = (y + row_up(y, size)) * 0.25
        ups = (x * 0.25, (x + y) * 0.125, odd * 0.5, (odd + odd_next) * 0.25)
        b = [
            up * slopes[part, kind, :, group_rows(group, size), :].reshape(ROWS * size, LANES)
            for kind, up in enumerate(ups)
        ]
        half = b[1] * 0.5 + (b[3] + row_down(b[3], size)) * 0.25
        base.append(b[0] + (b[2] + row_down(b[2], size)) * 0.5 + half)
        moved.append(half)
    left, left_ext = shift(moved[0], moved[1], -1)
    main, ext = rounded(base[0] + left), rounded(base[1] + left_ext)
    store_shifted(grads, shift_main(main, ext, 1), main, shift_main(main, ext, -1), group, size)
    packed[group_rows(group, size), :] = pack([ext[r * size : (r + 1) * size] for r in range(ROWS)])


def products(weights, block, halo, prod):
    for r in range(0, ROWS, 2):
        pair = jnp.concatenate(
            [block[:, r].reshape(CH * NB, LANES), block[:, r + 1].reshape(CH * NB, LANES)], axis=1
        )
        out = jnp.dot(weights, pair, preferred_element_type=F32)
        prod[r] = out[:, :LANES]
        prod[r + 1] = out[:, LANES:]
    prod[ROWS] = jnp.dot(weights, halo.reshape(CH * NB, LANES), preferred_element_type=F32)


def row_pair(block, r):
    return jnp.concatenate(
        [block[:, r].reshape(CH * NB, LANES), block[:, r + 1].reshape(CH * NB, LANES)], axis=1
    )


def tap_rows(ref, r, sign):
    return jnp.concatenate(
        [ref[:, r + sign * p + 1].reshape(3 * NB, LANES) for p in (-1, 0, 1)], axis=0
    )


def tap_row_pair(ref, r, sign):
    return jnp.concatenate([tap_rows(ref, r, sign), tap_rows(ref, r + 1, sign)], axis=1)


def contract_last(a, b):
    return lax.dot_general(a, b, (((1,), (1,)), ((), ())), preferred_element_type=F32)


NEAREST = sorted(
    ((dz, dx) for dz in range(4) for dx in range(4) if dz or dx),
    key=lambda d: (2 * min(d[0], 4 - d[0]) + min(d[1], 4 - d[1]), d),
)

HOPS = (
    ((0, 0), (1, 0), (-1, 0)),
    ((0, 0), (-1, 0), (1, 0)),
    ((0, 0), (0, 1), (0, 1)),
    ((0, 0), (2, 0), (2, 0)),
    ((0, 1), (1, 0), (-1, 1)),
    ((0, 1), (-1, 0), (1, 1)),
    ((2, 0), (0, 1), (2, 1)),
    ((0, 1), (2, 0), (2, 1)),
)


def kernel(
    field_hbm, w1_hbm, w2_hbm, cot_hbm, out_ref, g1_ref, g2_ref,
    field_in, cot_in, w1_in, w_in,
    rows32, gath, halo, edge, edge_in, cot32, lhs2, wsend, wrecv,
    prod, slopes, shifted32, shifted, packed32, hgath,
    g2send, g2recv, g1part, g1swap, rs_send, rs_recv, sums, sib_in,
    in_sems, edge_sems, main_sems, halo_sems, w_sems, tile_sems, wsib_sems, hg_sems, g2_sems,
    g1_sems, rs_sems, ag_sems, sib_sems,
):
    chan = lax.axis_index("chan")
    space = lax.axis_index("space")
    core = lax.rem(space, 2)
    chip = lax.div(space, 2)
    line, level = lax.div(chan, 2), lax.rem(chan, 2)
    column = lax.rem(chip, 4)
    plane = lax.div(chip, 4)
    left = lax.rem(space + SP - 1, SP)
    right = lax.rem(space + 1, SP)
    sibling = space + 1 - 2 * core
    scale = 1.0 / math.sqrt(ROWS * LANES * SP)

    def chan_at(k):
        return lax.rem(chan + k, CH)

    def chip_at(k):
        dz, dx = NEAREST[k]
        return lax.rem(plane + dz, 4) * 4 + lax.rem(column + dx, 4)

    def block_at(place):
        step, other = place
        at = 1 - level if other else level
        return lax.rem(line + step + 4, 4) * 2 + at

    def fetch(src, dst, k):
        return pltpu.make_async_copy(src, dst, in_sems.at[k])

    fetch(field_hbm, field_in, 0).start()
    fetch(cot_hbm, cot_in, 1).start()

    barrier = pltpu.get_barrier_semaphore()

    def greet(**target):
        pl.semaphore_signal(barrier, inc=1, device_id=target, device_id_type=MESH)

    @pl.loop(1, CH)
    def _(k):
        greet(chan=chan_at(k))
        greet(chan=chan_at(k), space=sibling)

    greet(space=left)
    greet(space=right)

    @pl.loop(1, PEERS)
    def _(k):
        greet(space=lax.rem(chip + k, PEERS) * 2 + core)

    fetch(w1_hbm, w1_in, 2).start()

    @pl.when(core == 0)
    def _():
        fetch(w1_hbm, w_in, 3).start()

    @pl.when(core == 1)
    def _():
        fetch(w2_hbm, w_in, 3).start()

    def remote(src, dst, sems, k, **target):
        return pltpu.make_async_remote_copy(
            src_ref=src, dst_ref=dst, send_sem=sems.at[0, k], recv_sem=sems.at[1, k],
            device_id=target, device_id_type=MESH,
        )

    def hop(buf, sems, j):
        sent = block_at(HOPS[j][0])
        return remote(buf.at[sent], buf.at[sent], sems, j, chan=block_at(HOPS[j][1]))

    def hop_in(buf, sems, j):
        got = block_at(HOPS[j][2])
        return remote(buf.at[got], buf.at[got], sems, j, chan=block_at(HOPS[j][1]))

    def send(buf, sems, *hops):
        for j in hops:
            hop(buf, sems, j).start()

    def arrive(buf, sems, *hops):
        for j in hops:
            hop_in(buf, sems, j).wait_recv()

    def second_hops(buf, sems):
        arrive(buf, sems, 2)
        send(buf, sems, 4, 5)
        arrive(buf, sems, 3)
        send(buf, sems, 6)

    def last_hops(buf, sems):
        arrive(buf, sems, 0, 1, 4, 5, 6)

    def split_rows(source):
        rows32[...] = source[...].astype(F32).reshape(NB * ROWS, LANES)
        return [rows32[pl.ds(r, NB, stride=ROWS), :] for r in range(ROWS)]

    lane = lane_ids((NB, LANES))
    fetch(field_hbm, field_in, 0).wait()
    field_rows = split_rows(field_in)
    for r in range(ROWS):
        gath[0, chan, r] = field_rows[r].astype(BF16)
    edge_field = pack(field_rows)
    fetch(cot_hbm, cot_in, 1).wait()
    cot_rows = split_rows(cot_in)
    for r in range(ROWS):
        gath[1, chan, r] = cot_rows[r].astype(BF16)
        cot32[r] = cot_rows[r]
    near = (lane % 16 < 4) | (lane % 16 >= 12)
    edge[...] = jnp.where(near, edge_field, roll(pack(cot_rows), 8)).astype(BF16)

    fetch(w1_hbm, w1_in, 2).wait()
    fetch(w1_hbm, w_in, 3).wait()

    def w_copy(k, dest, slot):
        return remote(wsend.at[dest], wrecv.at[core, column, slot], w_sems, k, chan=chan_at(k))

    @pl.when(column < 3)
    def _():
        loaded = [
            jnp.where(
                4 * column + u < 9, w_in[jnp.maximum(8 - 4 * column - u, 0)].astype(F32), 0.0
            )
            for u in range(4)
        ]
        for dest in range(CH):
            half, place = dest // 4, dest % 4
            total = jnp.zeros((NB, LANES), F32)
            for u, values in enumerate(loaded):
                source = values[:, half * LANES : (half + 1) * LANES]
                total = jnp.where(lane // NB == u, roll(source, (u - place) * NB), total)
            wsend[dest] = total.astype(BF16)
        wrecv[core, column, chan] = wsend[chan]

    pl.semaphore_wait(barrier, 2 * (CH - 1) + PEERS - 1 + 2)

    to_left = remote(edge, edge_in.at[0], edge_sems, 0, space=left)
    to_right = remote(edge, edge_in.at[1], edge_sems, 1, space=right)
    to_left.start()
    to_right.start()

    @pl.when(column < 3)
    def _():
        @pl.loop(1, CH)
        def _(k):
            w_copy(k, chan_at(k), chan).start()

    field_all, cot_all = (gath.at[0], main_sems.at[0]), (gath.at[1], main_sems.at[1])
    send(*field_all, 3, 2)
    send(*cot_all, 3, 2)
    send(*field_all, 0, 1)

    to_left.wait_recv()
    to_right.wait_recv()
    from_right = edge_in[0].astype(F32)
    from_left = edge_in[1].astype(F32)
    halo[chan] = jnp.where(lane % 8 < 4, from_right, from_left).astype(BF16)

    def halo_copy(k, slot):
        return remote(halo.at[slot], halo.at[slot], halo_sems, k, chan=chan_at(k))

    @pl.loop(1, CH)
    def _(k):
        halo_copy(k, chan).start()

    def tile_copy(k, tile):
        target = (chip - column + lax.rem(column + k, 4)) * 2 + core
        return pltpu.make_async_remote_copy(
            src_ref=wrecv.at[core, tile], dst_ref=wrecv.at[core, tile], send_sem=tile_sems.at[0, k],
            recv_sem=tile_sems.at[1, tile], device_id={"space": target}, device_id_type=MESH,
        )

    second_hops(*field_all)
    send(*cot_all, 0, 1)

    @pl.when(column < 3)
    def _():
        @pl.loop(1, CH)
        def _(k):
            w_copy(k, chan_at(k), chan_at(CH - k)).wait_recv()

        @pl.loop(1, 4)
        def _(k):
            tile_copy(k, column).start()

    second_hops(*cot_all)

    @pl.loop(0, 3)
    def _(tile):
        @pl.when(tile != column)
        def _():
            tile_copy(1, tile).wait_recv()

    w_out = remote(wrecv.at[core], wrecv.at[core], wsib_sems, 0, space=sibling)
    w_out.start()

    last_hops(*field_all)

    @pl.loop(1, CH)
    def _(k):
        halo_copy(k, chan_at(CH - k)).wait_recv()

    group_size = 16
    shifted32[:, 0] = jnp.zeros((3, NB, LANES), F32)
    shifted32[:, ROWS + 1] = jnp.zeros((3, NB, LANES), F32)
    products(w1_in[...].reshape(9 * NB, CH * NB), gath.at[0], halo[...], prod)

    @pl.loop(0, NB // group_size)
    def _(group):
        resample_forward(prod, group, group_size, slopes, shifted32)

    shifted[0] = shifted32[...].astype(BF16)

    remote(wrecv.at[1 - core], wrecv.at[1 - core], wsib_sems, 0, space=sibling).wait_recv()

    def turn_weights(which):
        for k in range(3):
            turned = wrecv[which, k].reshape(CH * NB, LANES).T
            if k < 2:
                lhs2[which, k * LANES : (k + 1) * LANES, :] = turned
            else:
                lhs2[which, 2 * LANES :, :] = turned[:NB]

    turn_weights(1)
    last_hops(*cot_all)
    total = jnp.zeros((CH * NB, 3 * LANES), F32)
    for r in range(0, ROWS, 2):
        rhs = tap_row_pair(shifted.at[0], r, 1)
        rhs = jnp.concatenate([rhs, jnp.zeros((3 * NB, 2 * LANES), BF16)], axis=0)
        total = total + contract_last(row_pair(gath.at[1], r), rhs)
    total = (total * scale).astype(BF16)
    for k in range(3):
        g2send[:, k] = total[:, k * LANES : (k + 1) * LANES].reshape(CH, NB, LANES)

    def g2_copy(dest, source_core, source):
        return pltpu.make_async_remote_copy(
            src_ref=g2send.at[dest], dst_ref=g2recv.at[source_core, source],
            send_sem=g2_sems.at[0, 0, dest], recv_sem=g2_sems.at[1, source_core, source],
            device_id={"chan": dest, "space": 2 * chip + 1}, device_id_type=MESH,
        )

    @pl.loop(1, CH)
    def _(k):
        g2_copy(chan_at(k), core, chan).start()

    @pl.when(core == 0)
    def _():
        g2_copy(chan, core, chan).start()

    @pl.when(core == 1)
    def _():
        g2recv[1, chan] = g2send[chan]

    products(lhs2[1], gath.at[1], halo[...], prod)

    @pl.loop(0, NB // group_size)
    def _(group):
        resample_backward(prod, group, group_size, slopes, shifted32, packed32)

    shifted[1] = shifted32[...].astype(BF16)
    hgath[chan, 0:ROWS] = shifted[1, 1, 1 : ROWS + 1]
    hgath[chan, ROWS] = packed32[...].astype(BF16)
    send(hgath, hg_sems, *(2, 3, 0, 1))

    def g1_copy(p):
        return remote(g1part.at[p], g1swap.at[p], g1_sems, p, space=sibling)

    for p in range(3):
        total = jnp.zeros((3 * NB, CH * NB), F32)
        for r in range(0, ROWS, 2):
            lhs = jnp.concatenate(
                [shifted[1, :, r + i - p + 2].reshape(3 * NB, LANES) for i in range(2)], axis=1
            )
            total = total + contract_last(lhs, row_pair(gath.at[0], r))
        g1part[p] = total * scale

        @pl.when(core == 1)
        def _():
            g1_copy(p).start()

    def piece_of(ref, owner):
        rows = pl.ds(pl.multiple_of(lax.div(owner, 2) * PIECE, 16), PIECE)
        return ref.at[lax.rem(owner, 2), rows]

    def rs_copy(owner):
        slot = lax.rem(chip - owner + PEERS, PEERS) - 1
        return pltpu.make_async_remote_copy(
            src_ref=piece_of(rs_send, owner), dst_ref=rs_recv.at[slot], send_sem=rs_sems.at[0],
            recv_sem=rs_sems.at[1],
            device_id={"space": owner * 2 + core}, device_id_type=MESH,
        )

    def all_pieces(count):
        return pltpu.make_async_remote_copy(
            src_ref=rs_recv.at[pl.ds(0, count)], dst_ref=rs_recv.at[pl.ds(0, count)],
            send_sem=rs_sems.at[0], recv_sem=rs_sems.at[1],
            device_id={"space": sibling}, device_id_type=MESH,
        )

    def to_owners(low, high):
        @pl.loop(low, high)
        def _(owner):
            @pl.when(owner == chip)
            def _():
                rs_recv[PEERS - 1] = piece_of(rs_send, chip)[...]

            @pl.when(owner != chip)
            def _():
                rs_copy(owner).start()

    def put_rows(first, values):
        for half in range(2):
            rs_send[half, first : first + values.shape[0]] = values[
                :, half * LANES : (half + 1) * LANES
            ].astype(BF16)

    @pl.when(core == 1)
    def _():
        g2_copy(chan, 0, chan).wait_recv()

        @pl.loop(1, CH)
        def _(k):
            for source_core in range(2):
                g2_copy(chan, source_core, chan_at(k)).wait_recv()

        for k in range(3):
            loaded = [
                g2recv[0, s, k].astype(F32) + g2recv[1, s, k].astype(F32) for s in range(CH)
            ]
            for t in range(4 * k, min(4 * k + 4, 9)):
                for half in range(2):
                    total = jnp.zeros((NB, LANES), F32)
                    for place in range(4):
                        moved = roll(loaded[4 * half + place], (place - t % 4) * NB)
                        total = jnp.where(lane // NB == place, moved, total)
                    rs_send[half, t * NB : (t + 1) * NB] = total.astype(BF16)
        to_owners(0, OWNERS)

    @pl.when(core == 0)
    def _():
        for p in range(3):
            g1_copy(p).wait_recv()
            put_rows(96 * p, g1part[p] + g1swap[p])
            to_owners(4 * p, 4 * p + 4)

    arrive(hgath, hg_sems, 2)
    send(hgath, hg_sems, 7, 4, 5)
    turn_weights(0)

    def ag_copy(k, slot):
        return pltpu.make_async_remote_copy(
            src_ref=piece_of(sums, slot), dst_ref=piece_of(sums, slot), send_sem=ag_sems.at[0, k],
            recv_sem=ag_sems.at[1, slot],
            device_id={"space": chip_at(k) * 2 + core}, device_id_type=MESH,
        )

    def sib_copy(slot):
        return remote(piece_of(sums, slot), piece_of(sib_in, slot), sib_sems, slot, space=sibling)

    @pl.when(chip < OWNERS)
    def _():
        all_pieces(PEERS - 1).wait_recv()
        total = rs_recv[0].astype(F32)
        for s in range(1, PEERS):
            total = total + rs_recv[s].astype(F32)
        piece_of(sums, chip)[...] = total.astype(BF16)

        for k in reversed(range(PEERS - 1)):
            ag_copy(k, chip).start()
        sib_copy(chip).start()

    arrive(hgath, hg_sems, 0, 1, 3, 4, 5, 7)
    products(lhs2[0], hgath, hgath[:, ROWS], prod)

    @pl.loop(0, NB // group_size)
    def _(group):
        main, _ = combine(prod, group, group_size)
        rows = group_rows(group, group_size)
        cot32[:, rows, :] = cot32[:, rows, :] + main.reshape(ROWS, group_size, LANES)

    for r in range(ROWS):
        rows32[pl.ds(r, NB, stride=ROWS), :] = cot32[r]
    out_ref[...] = rows32[...].reshape(NB, ROWS, LANES).astype(BF16)

    for k in range(PEERS - 1):
        source = chip_at(k)

        @pl.when(source < OWNERS)
        def _():
            ag_copy(k, source).wait_recv()
            sib_copy(source).start()

    def store(source, which):
        for grad, ref in enumerate((g1_ref, g2_ref)):
            @pl.when(which == grad)
            def _():
                for half in range(2):
                    ref[:, half * LANES : (half + 1) * LANES] = source[half]

    store(sums, core)

    @pl.loop(0, OWNERS)
    def _(source):
        sib_copy(source).wait_recv()

    store(sib_in, 1 - core)

    to_left.wait_send()
    to_right.wait_send()
    w_out.wait_send()
    for buf, sems in ((gath.at[0], main_sems.at[0]), (gath.at[1], main_sems.at[1]), (hgath, hg_sems)):
        for j in (0, 1, 2, 3, 4, 5, 7 if buf is hgath else 6):
            hop(buf, sems, j).wait_send()

    @pl.loop(1, CH)
    def _(k):
        halo_copy(k, chan).wait_send()

    @pl.when(column < 3)
    def _():
        @pl.loop(1, CH)
        def _(k):
            w_copy(k, chan_at(k), chan).wait_send()

        @pl.loop(1, 4)
        def _(k):
            tile_copy(k, column).wait_send()

    @pl.loop(1, CH)
    def _(k):
        g2_copy(chan_at(k), core, chan).wait_send()

    @pl.when(core == 0)
    def _():
        g2_copy(chan, core, chan).wait_send()

    @pl.when(core == 1)
    def _():
        for p in range(3):
            g1_copy(p).wait_send()

    @pl.loop(0, OWNERS)
    def _(owner):
        sib_copy(owner).wait_send()

        @pl.when(owner != chip)
        def _():
            rs_copy(owner).wait_send()

    @pl.when(chip < OWNERS)
    def _():
        for k in range(PEERS - 1):
            ag_copy(k, chip).wait_send()


def on_device(field, first_weight, second_weight, cotangent):
    vmem = pl.BlockSpec(memory_space=pltpu.VMEM)
    hbm = pl.BlockSpec(memory_space=pltpu.HBM)
    dma = pltpu.SemaphoreType.DMA
    out, first_grad, second_grad = pl.pallas_call(
        kernel,
        out_shape=(
            jax.ShapeDtypeStruct((NB, ROWS, LANES), BF16),
            jax.ShapeDtypeStruct((9 * NB, CH * NB), BF16),
            jax.ShapeDtypeStruct((9 * NB, CH * NB), BF16),
        ),
        in_specs=[hbm] * 4,
        out_specs=(vmem, vmem, vmem),
        scratch_shapes=[
            pltpu.VMEM((NB, ROWS, LANES), BF16),
            pltpu.VMEM((NB, ROWS, LANES), BF16),
            pltpu.VMEM((9, NB, CH * NB), BF16),
            pltpu.VMEM((9, NB, CH * NB), BF16),
            pltpu.VMEM((NB * ROWS, LANES), F32),
            pltpu.VMEM((2, CH, ROWS, NB, LANES), BF16),
            pltpu.VMEM((CH, NB, LANES), BF16),
            pltpu.VMEM((NB, LANES), BF16),
            pltpu.VMEM((2, NB, LANES), BF16),
            pltpu.VMEM((ROWS, NB, LANES), F32),
            pltpu.VMEM((2, 9 * NB, CH * NB), BF16),
            pltpu.VMEM((CH, NB, LANES), BF16),
            pltpu.VMEM((2, 3, CH, NB, LANES), BF16),
            pltpu.VMEM((ROWS + 1, 9 * NB, LANES), F32),
            pltpu.VMEM((2, 4, ROWS, NB, LANES), F32),
            pltpu.VMEM((3, ROWS + 2, NB, LANES), F32),
            pltpu.VMEM((2, 3, ROWS + 2, NB, LANES), BF16),
            pltpu.VMEM((NB, LANES), F32),
            pltpu.VMEM((CH, ROWS + 1, NB, LANES), BF16),
            pltpu.VMEM((CH, 3, NB, LANES), BF16),
            pltpu.VMEM((2, CH, 3, NB, LANES), BF16),
            pltpu.VMEM((3, 3 * NB, CH * NB), F32),
            pltpu.VMEM((3, 3 * NB, CH * NB), F32),
            pltpu.VMEM((2, 9 * NB, LANES), BF16),
            pltpu.VMEM((PEERS, PIECE, LANES), BF16),
            pltpu.VMEM((2, 9 * NB, LANES), BF16),
            pltpu.VMEM((2, 9 * NB, LANES), BF16),
            dma((4,)),
            dma((2, 2)),
            dma((2, 2, len(HOPS))),
            dma((2, CH)),
            dma((2, CH)),
            dma((2, 4)),
            dma((2, 1)),
            dma((2, len(HOPS))),
            dma((2, 2, CH)),
            dma((2, 3)),
            dma((2,)),
            dma((2, PEERS)),
            dma((2, OWNERS)),
        ],
        compiler_params=pltpu.CompilerParams(
            collective_id=0, has_side_effects=True, vmem_limit_bytes=40 * 1024 * 1024
        ),
    )(
        *(
            pltpu.with_memory_space_constraint(x, pltpu.HBM)
            for x in (
                field, first_weight.transpose(1, 0, 2), second_weight.transpose(1, 0, 2), cotangent
            )
        )
    )

    def taps_inside(grad):
        return grad.astype(F32).reshape(9, NB, CH * NB).transpose(1, 0, 2)

    return (out, taps_inside(first_grad), taps_inside(second_grad))


def solution(mesh):
    in_specs = (
        P("chan", None, "space"),
        P("chan", None, None),
        P("chan", None, None),
        P("chan", None, "space"),
    )
    out_specs = (P("chan", None, "space"), P("chan", None, None), P("chan", None, None))
    return jax.shard_map(
        on_device, mesh=mesh, in_specs=in_specs, out_specs=out_specs, check_vma=False
    )
```

```python
import math

import jax
import jax.numpy as jnp
from jax import lax
from jax.experimental import pallas as pl
from jax.experimental.pallas import tpu as pltpu
from jax.sharding import PartitionSpec as P

MESH = pl.DeviceIdType.MESH
F32 = jnp.float32
BF16 = jnp.bfloat16
CH = 8
SP = 32
NB = 32
ROWS = 8
LANES = 128
PEERS = SP // 2
OWNERS = 12
PIECE = 48
TAPS = [(p, q) for p in (-1, 0, 1) for q in (-1, 0, 1)]


def tap(p, q):
    return 3 * (p + 1) + q + 1


def lane_ids(shape):
    return lax.broadcasted_iota(jnp.int32, shape, len(shape) - 1)


def roll(values, amount):
    amount = amount % LANES
    if amount == 0:
        return values
    return pltpu.roll(values, amount, 1)


def shift_main(main, ext, step):
    wraps = lane_ids(main.shape) == (0 if step == 1 else LANES - 1)
    return roll(jnp.where(wraps, ext, main), -step)


def shift(main, ext, step):
    return shift_main(main, ext, step), shift_main(ext, main, step)


def row_up(values, size):
    return jnp.concatenate([values[size:], jnp.zeros((size, LANES), F32)], axis=0)


def row_down(values, size):
    return jnp.concatenate([jnp.zeros((size, LANES), F32), values[:-size]], axis=0)


def row_of_lane(shape, offset=0):
    return ((lane_ids(shape) + 8 - offset) // 16) % 8


def pack(tiles):
    total = jnp.zeros(tiles[0].shape, F32)
    owner = row_of_lane(tiles[0].shape)
    for r in range(ROWS):
        total = jnp.where(owner == r, roll(tiles[r], 16 * r), total)
    return total


def load_tap(prod, t, group, size):
    rows = pl.ds(pl.multiple_of(t * NB + group * size, 8), size)
    main = prod[0:ROWS, rows, :].reshape(ROWS * size, LANES)
    return main, prod[ROWS, rows, :]


def combine(prod, group, size, offset=0):
    mains, packs = [], []
    owner = row_of_lane((size, LANES), offset)
    for q in (-1, 0, 1):
        up_main, up_pack = load_tap(prod, tap(1, q), group, size)
        mid_main, mid_pack = load_tap(prod, tap(0, q), group, size)
        down_main, down_pack = load_tap(prod, tap(-1, q), group, size)
        mains.append(mid_main + row_up(up_main, size) + row_down(down_main, size))
        packs.append(
            mid_pack
            + jnp.where(owner == ROWS - 1, 0.0, roll(up_pack, -16))
            + jnp.where(owner == 0, 0.0, roll(down_pack, 16))
        )
    near = (lane_ids((size, LANES)) - offset) % 16
    from_left, from_right = roll(packs[0], 1), roll(packs[2], -1)
    edges = jnp.where(near == 0, from_left, from_right)
    outer = packs[1] + jnp.where(near == 0, 0.0, from_left) + jnp.where(near == 15, 0.0, from_right)

    def expand(values):
        return jnp.concatenate([roll(values, -16 * r - offset) for r in range(ROWS)], axis=0)

    lane = lane_ids(mains[1].shape)
    first, last = lane == 0, lane == LANES - 1
    before, after, edges = roll(mains[0], 1), roll(mains[2], -1), expand(edges)
    main = mains[1] + jnp.where(first, edges, before) + jnp.where(last, edges, after)
    ext = expand(outer) + jnp.where(first, before, 0.0) + jnp.where(last, after, 0.0)
    return main, ext


def gelu_both(v):
    scale = math.sqrt(2.0 / math.pi)
    square = v * v
    t = jnp.tanh(scale * v * (1.0 + 0.044715 * square))
    half = 0.5 * (1.0 + t)
    slope = half + 0.5 * v * (1.0 - t * t) * (scale * (1.0 + 3.0 * 0.044715 * square))
    return v * half, slope


def rounded(values):
    return values.astype(BF16).astype(F32)


def resample_forward(prod, group, size, slopes, smooth):
    h, h_ext = combine(prod, group, size)
    h, h_ext = rounded(h), rounded(h_ext)
    hc, hc_ext = shift(h, h_ext, 1)
    acts = []
    for part, (x, y) in enumerate(((h, hc), (h_ext, hc_ext))):
        x_low, y_low = row_up(x, size), row_up(y, size)
        points = (x, (x + y) * 0.5, (x + x_low) * 0.5, (x + y + x_low + y_low) * 0.25)
        values = []
        for kind, point in enumerate(points):
            value, slope = gelu_both(point)
            values.append(value)
            slopes[part, kind, :, group_rows(group, size), :] = slope.reshape(ROWS, size, LANES)
        acts.append(values)
    base, moved = [], []
    for values in acts:
        side = 2.0 * values[1] + values[3] + row_down(values[3], size)
        base.append(side + 4.0 * values[0] + 2.0 * (values[2] + row_down(values[2], size)))
        moved.append(side)
    left, left_ext = shift(moved[0], moved[1], -1)
    main, ext = rounded((base[0] + left) * 0.0625), rounded((base[1] + left_ext) * 0.0625)
    store_shifted(smooth, shift_main(main, ext, -1), main, shift_main(main, ext, 1), group, size)


def group_rows(group, size):
    return pl.ds(pl.multiple_of(group * size, 8), size)


def store_shifted(ref, *args):
    before, here, after, group, size = args
    for q, values in enumerate((before, here, after)):
        ref[q, 1 : ROWS + 1, group_rows(group, size), :] = values.reshape(ROWS, size, LANES)


def resample_backward(prod, group, size, slopes, grads, packed):
    g, g_ext = combine(prod, group, size, 8)
    g, g_ext = rounded(g), rounded(g_ext)
    gc, gc_ext = shift(g, g_ext, 1)
    base, moved = [], []
    for part, (x, y) in enumerate(((g, gc), (g_ext, gc_ext))):
        odd = (x + row_up(x, size)) * 0.25
        odd_next = (y + row_up(y, size)) * 0.25
        ups = (x * 0.25, (x + y) * 0.125, odd * 0.5, (odd + odd_next) * 0.25)
        b = [
            up * slopes[part, kind, :, group_rows(group, size), :].reshape(ROWS * size, LANES)
            for kind, up in enumerate(ups)
        ]
        half = b[1] * 0.5 + (b[3] + row_down(b[3], size)) * 0.25
        base.append(b[0] + (b[2] + row_down(b[2], size)) * 0.5 + half)
        moved.append(half)
    left, left_ext = shift(moved[0], moved[1], -1)
    main, ext = rounded(base[0] + left), rounded(base[1] + left_ext)
    store_shifted(grads, shift_main(main, ext, 1), main, shift_main(main, ext, -1), group, size)
    packed[group_rows(group, size), :] = pack([ext[r * size : (r + 1) * size] for r in range(ROWS)])


def products(weights, block, halo, prod):
    for r in range(0, ROWS, 2):
        pair = jnp.concatenate(
            [block[:, r].reshape(CH * NB, LANES), block[:, r + 1].reshape(CH * NB, LANES)], axis=1
        )
        out = jnp.dot(weights, pair, preferred_element_type=F32)
        prod[r] = out[:, :LANES]
        prod[r + 1] = out[:, LANES:]
    prod[ROWS] = jnp.dot(weights, halo.reshape(CH * NB, LANES), preferred_element_type=F32)


def row_pair(block, r):
    return jnp.concatenate(
        [block[:, r].reshape(CH * NB, LANES), block[:, r + 1].reshape(CH * NB, LANES)], axis=1
    )


def tap_rows(ref, r, sign):
    return jnp.concatenate(
        [ref[:, r + sign * p + 1].reshape(3 * NB, LANES) for p in (-1, 0, 1)], axis=0
    )


def tap_row_pair(ref, r, sign):
    return jnp.concatenate([tap_rows(ref, r, sign), tap_rows(ref, r + 1, sign)], axis=1)


def contract_last(a, b):
    return lax.dot_general(a, b, (((1,), (1,)), ((), ())), preferred_element_type=F32)


NEAREST = sorted(
    ((dz, dx) for dz in range(4) for dx in range(4) if dz or dx),
    key=lambda d: (2 * min(d[0], 4 - d[0]) + min(d[1], 4 - d[1]), d),
)

HOPS = (
    ((0, 0), (1, 0), (-1, 0)),
    ((0, 0), (-1, 0), (1, 0)),
    ((0, 0), (0, 1), (0, 1)),
    ((0, 0), (2, 0), (2, 0)),
    ((0, 1), (1, 0), (-1, 1)),
    ((0, 1), (-1, 0), (1, 1)),
    ((2, 0), (0, 1), (2, 1)),
    ((0, 1), (2, 0), (2, 1)),
)


def kernel(
    field_hbm, w1_hbm, w2_hbm, cot_hbm, out_ref, g1_ref, g2_ref,
    field_in, cot_in, w1_in, w_in,
    rows32, gath, halo, edge, edge_in, cot32, lhs2, wsend, wrecv,
    prod, slopes, shifted32, shifted, packed32, hgath,
    g2send, g2recv, g1part, g1swap, rs_send, rs_recv, sums, sib_in,
    in_sems, edge_sems, main_sems, halo_sems, w_sems, tile_sems, wsib_sems, hg_sems, g2_sems,
    g1_sems, rs_sems, ag_sems, sib_sems,
):
    chan = lax.axis_index("chan")
    space = lax.axis_index("space")
    core = lax.rem(space, 2)
    chip = lax.div(space, 2)
    line, level = lax.div(chan, 2), lax.rem(chan, 2)
    column = lax.rem(chip, 4)
    plane = lax.div(chip, 4)
    left = lax.rem(space + SP - 1, SP)
    right = lax.rem(space + 1, SP)
    sibling = space + 1 - 2 * core
    scale = 1.0 / math.sqrt(ROWS * LANES * SP)

    def chan_at(k):
        return lax.rem(chan + k, CH)

    def chip_at(k):
        dz, dx = NEAREST[k]
        return lax.rem(plane + dz, 4) * 4 + lax.rem(column + dx, 4)

    def block_at(place):
        step, other = place
        at = 1 - level if other else level
        return lax.rem(line + step + 4, 4) * 2 + at

    def fetch(src, dst, k):
        return pltpu.make_async_copy(src, dst, in_sems.at[k])

    fetch(field_hbm, field_in, 0).start()
    fetch(cot_hbm, cot_in, 1).start()

    barrier = pltpu.get_barrier_semaphore()

    def greet(**target):
        pl.semaphore_signal(barrier, inc=1, device_id=target, device_id_type=MESH)

    @pl.loop(1, CH)
    def _(k):
        greet(chan=chan_at(k))
        greet(chan=chan_at(k), space=sibling)

    greet(space=left)
    greet(space=right)

    @pl.loop(1, PEERS)
    def _(k):
        greet(space=lax.rem(chip + k, PEERS) * 2 + core)

    fetch(w1_hbm, w1_in, 2).start()

    @pl.when(core == 0)
    def _():
        fetch(w1_hbm, w_in, 3).start()

    @pl.when(core == 1)
    def _():
        fetch(w2_hbm, w_in, 3).start()

    def remote(src, dst, sems, k, **target):
        return pltpu.make_async_remote_copy(
            src_ref=src, dst_ref=dst, send_sem=sems.at[0, k], recv_sem=sems.at[1, k],
            device_id=target, device_id_type=MESH,
        )

    def hop(buf, sems, j):
        sent = block_at(HOPS[j][0])
        return remote(buf.at[sent], buf.at[sent], sems, j, chan=block_at(HOPS[j][1]))

    def hop_in(buf, sems, j):
        got = block_at(HOPS[j][2])
        return remote(buf.at[got], buf.at[got], sems, j, chan=block_at(HOPS[j][1]))

    def send(buf, sems, *hops):
        for j in hops:
            hop(buf, sems, j).start()

    def arrive(buf, sems, *hops):
        for j in hops:
            hop_in(buf, sems, j).wait_recv()

    def second_hops(buf, sems):
        arrive(buf, sems, 2)
        send(buf, sems, 4, 5)
        arrive(buf, sems, 3)
        send(buf, sems, 6)

    def last_hops(buf, sems):
        arrive(buf, sems, 0, 1, 4, 5, 6)

    def split_rows(source):
        rows32[...] = source[...].astype(F32).reshape(NB * ROWS, LANES)
        return [rows32[pl.ds(r, NB, stride=ROWS), :] for r in range(ROWS)]

    lane = lane_ids((NB, LANES))
    fetch(field_hbm, field_in, 0).wait()
    field_rows = split_rows(field_in)
    for r in range(ROWS):
        gath[0, chan, r] = field_rows[r].astype(BF16)
    edge_field = pack(field_rows)
    fetch(cot_hbm, cot_in, 1).wait()
    cot_rows = split_rows(cot_in)
    for r in range(ROWS):
        gath[1, chan, r] = cot_rows[r].astype(BF16)
        cot32[r] = cot_rows[r]
    near = (lane % 16 < 4) | (lane % 16 >= 12)
    edge[...] = jnp.where(near, edge_field, roll(pack(cot_rows), 8)).astype(BF16)

    fetch(w1_hbm, w1_in, 2).wait()
    fetch(w1_hbm, w_in, 3).wait()

    def w_copy(k, dest, slot):
        return remote(wsend.at[dest], wrecv.at[core, column, slot], w_sems, k, chan=chan_at(k))

    @pl.when(column < 3)
    def _():
        loaded = [
            jnp.where(
                4 * column + u < 9, w_in[jnp.maximum(8 - 4 * column - u, 0)].astype(F32), 0.0
            )
            for u in range(4)
        ]
        for dest in range(CH):
            half, place = dest // 4, dest % 4
            total = jnp.zeros((NB, LANES), F32)
            for u, values in enumerate(loaded):
                source = values[:, half * LANES : (half + 1) * LANES]
                total = jnp.where(lane // NB == u, roll(source, (u - place) * NB), total)
            wsend[dest] = total.astype(BF16)
        wrecv[core, column, chan] = wsend[chan]

    pl.semaphore_wait(barrier, 2 * (CH - 1) + PEERS - 1 + 2)

    to_left = remote(edge, edge_in.at[0], edge_sems, 0, space=left)
    to_right = remote(edge, edge_in.at[1], edge_sems, 1, space=right)
    to_left.start()
    to_right.start()

    @pl.when(column < 3)
    def _():
        @pl.loop(1, CH)
        def _(k):
            w_copy(k, chan_at(k), chan).start()

    field_all, cot_all = (gath.at[0], main_sems.at[0]), (gath.at[1], main_sems.at[1])
    send(*field_all, 3, 2)
    send(*cot_all, 3, 2)
    send(*field_all, 0, 1)

    to_left.wait_recv()
    to_right.wait_recv()
    from_right = edge_in[0].astype(F32)
    from_left = edge_in[1].astype(F32)
    halo[chan] = jnp.where(lane % 8 < 4, from_right, from_left).astype(BF16)

    def halo_copy(k, slot):
        return remote(halo.at[slot], halo.at[slot], halo_sems, k, chan=chan_at(k))

    @pl.loop(1, CH)
    def _(k):
        halo_copy(k, chan).start()

    def tile_copy(k, tile):
        target = (chip - column + lax.rem(column + k, 4)) * 2 + core
        return pltpu.make_async_remote_copy(
            src_ref=wrecv.at[core, tile], dst_ref=wrecv.at[core, tile], send_sem=tile_sems.at[0, k],
            recv_sem=tile_sems.at[1, tile], device_id={"space": target}, device_id_type=MESH,
        )

    second_hops(*field_all)
    send(*cot_all, 0, 1)

    @pl.when(column < 3)
    def _():
        @pl.loop(1, CH)
        def _(k):
            w_copy(k, chan_at(k), chan_at(CH - k)).wait_recv()

        @pl.loop(1, 4)
        def _(k):
            tile_copy(k, column).start()

    second_hops(*cot_all)

    @pl.loop(0, 3)
    def _(tile):
        @pl.when(tile != column)
        def _():
            tile_copy(1, tile).wait_recv()

    w_out = remote(wrecv.at[core], wrecv.at[core], wsib_sems, 0, space=sibling)
    w_out.start()

    last_hops(*field_all)

    @pl.loop(1, CH)
    def _(k):
        halo_copy(k, chan_at(CH - k)).wait_recv()

    group_size = 16
    shifted32[:, 0] = jnp.zeros((3, NB, LANES), F32)
    shifted32[:, ROWS + 1] = jnp.zeros((3, NB, LANES), F32)
    products(w1_in[...].reshape(9 * NB, CH * NB), gath.at[0], halo[...], prod)

    @pl.loop(0, NB // group_size)
    def _(group):
        resample_forward(prod, group, group_size, slopes, shifted32)

    shifted[0] = shifted32[...].astype(BF16)

    remote(wrecv.at[1 - core], wrecv.at[1 - core], wsib_sems, 0, space=sibling).wait_recv()

    def turn_weights(which):
        for k in range(3):
            turned = wrecv[which, k].reshape(CH * NB, LANES).T
            if k < 2:
                lhs2[which, k * LANES : (k + 1) * LANES, :] = turned
            else:
                lhs2[which, 2 * LANES :, :] = turned[:NB]

    turn_weights(1)
    last_hops(*cot_all)
    total = jnp.zeros((CH * NB, 3 * LANES), F32)
    for r in range(0, ROWS, 2):
        rhs = tap_row_pair(shifted.at[0], r, 1)
        rhs = jnp.concatenate([rhs, jnp.zeros((3 * NB, 2 * LANES), BF16)], axis=0)
        total = total + contract_last(row_pair(gath.at[1], r), rhs)
    total = (total * scale).astype(BF16)
    for k in range(3):
        g2send[:, k] = total[:, k * LANES : (k + 1) * LANES].reshape(CH, NB, LANES)

    def g2_copy(dest, source_core, source):
        return pltpu.make_async_remote_copy(
            src_ref=g2send.at[dest], dst_ref=g2recv.at[source_core, source],
            send_sem=g2_sems.at[0, 0, dest], recv_sem=g2_sems.at[1, source_core, source],
            device_id={"chan": dest, "space": 2 * chip + 1}, device_id_type=MESH,
        )

    @pl.loop(1, CH)
    def _(k):
        g2_copy(chan_at(k), core, chan).start()

    @pl.when(core == 0)
    def _():
        g2_copy(chan, core, chan).start()

    @pl.when(core == 1)
    def _():
        g2recv[1, chan] = g2send[chan]

    products(lhs2[1], gath.at[1], halo[...], prod)

    @pl.loop(0, NB // group_size)
    def _(group):
        resample_backward(prod, group, group_size, slopes, shifted32, packed32)

    shifted[1] = shifted32[...].astype(BF16)
    hgath[chan, 0:ROWS] = shifted[1, 1, 1 : ROWS + 1]
    hgath[chan, ROWS] = packed32[...].astype(BF16)
    send(hgath, hg_sems, *(2, 3, 0, 1))

    def g1_copy(p):
        return remote(g1part.at[p], g1swap.at[p], g1_sems, p, space=sibling)

    chunks = range(3)
    for p in chunks:
        total = jnp.zeros((3 * NB, CH * NB), F32)
        for r in range(0, ROWS, 2):
            lhs = jnp.concatenate(
                [shifted[1, :, r + i - p + 2].reshape(3 * NB, LANES) for i in range(2)], axis=1
            )
            total = total + contract_last(lhs, row_pair(gath.at[0], r))
        g1part[p] = total * scale

        @pl.when(core == 1)
        def _():
            g1_copy(p).start()

    def piece_of(ref, owner):
        rows = pl.ds(pl.multiple_of(lax.div(owner, 2) * PIECE, 16), PIECE)
        return ref.at[lax.rem(owner, 2), rows]

    def rs_copy(owner):
        slot = lax.rem(chip - owner + PEERS, PEERS) - 1
        return pltpu.make_async_remote_copy(
            src_ref=piece_of(rs_send, owner), dst_ref=rs_recv.at[slot], send_sem=rs_sems.at[0],
            recv_sem=rs_sems.at[1],
            device_id={"space": owner * 2 + core}, device_id_type=MESH,
        )

    def all_pieces(count):
        return pltpu.make_async_remote_copy(
            src_ref=rs_recv.at[pl.ds(0, count)], dst_ref=rs_recv.at[pl.ds(0, count)],
            send_sem=rs_sems.at[0], recv_sem=rs_sems.at[1],
            device_id={"space": sibling}, device_id_type=MESH,
        )

    def to_owners(p):
        for step in range(4):
            owner = 4 * p + lax.rem(column + (2, 1, 3, 0)[step], 4)

            @pl.when(owner == chip)
            def _():
                rs_recv[PEERS - 1] = piece_of(rs_send, chip)[...]

            @pl.when(owner != chip)
            def _():
                rs_copy(owner).start()

    def put_rows(first, values):
        for half in range(2):
            rs_send[half, pl.ds(pl.multiple_of(first, 16), values.shape[0])] = values[
                :, half * LANES : (half + 1) * LANES
            ].astype(BF16)

    @pl.when(core == 1)
    def _():
        g2_copy(chan, 0, chan).wait_recv()

        @pl.loop(1, CH)
        def _(k):
            for source_core in range(2):
                g2_copy(chan, source_core, chan_at(k)).wait_recv()

        for k in range(3):
            loaded = [
                g2recv[0, s, k].astype(F32) + g2recv[1, s, k].astype(F32) for s in range(CH)
            ]
            for t in range(4 * k, min(4 * k + 4, 9)):
                for half in range(2):
                    total = jnp.zeros((NB, LANES), F32)
                    for place in range(4):
                        moved = roll(loaded[4 * half + place], (place - t % 4) * NB)
                        total = jnp.where(lane // NB == place, moved, total)
                    rs_send[half, t * NB : (t + 1) * NB] = total.astype(BF16)
        for p in chunks:
            to_owners(p)

    @pl.when(core == 0)
    def _():
        for p in chunks:
            g1_copy(p).wait_recv()
            put_rows(96 * p, g1part[p] + g1swap[p])
            to_owners(p)

    arrive(hgath, hg_sems, 2)
    send(hgath, hg_sems, 7, 4, 5)
    turn_weights(0)

    def ag_copy(k, slot):
        return pltpu.make_async_remote_copy(
            src_ref=piece_of(sums, slot), dst_ref=piece_of(sums, slot), send_sem=ag_sems.at[0, k],
            recv_sem=ag_sems.at[1, slot],
            device_id={"space": chip_at(k) * 2 + core}, device_id_type=MESH,
        )

    def sib_copy(slot):
        return remote(piece_of(sums, slot), piece_of(sib_in, slot), sib_sems, slot, space=sibling)

    @pl.when(chip < OWNERS)
    def _():
        all_pieces(PEERS - 1).wait_recv()
        total = rs_recv[0].astype(F32)
        for s in range(1, PEERS):
            total = total + rs_recv[s].astype(F32)
        piece_of(sums, chip)[...] = total.astype(BF16)

        for k in reversed(range(PEERS - 1)):
            ag_copy(k, chip).start()
        sib_copy(chip).start()

    arrive(hgath, hg_sems, 0, 1, 3, 4, 5, 7)
    products(lhs2[0], hgath, hgath[:, ROWS], prod)

    @pl.loop(0, NB // group_size)
    def _(group):
        main, _ = combine(prod, group, group_size)
        rows = group_rows(group, group_size)
        cot32[:, rows, :] = cot32[:, rows, :] + main.reshape(ROWS, group_size, LANES)

    for r in range(ROWS):
        rows32[pl.ds(r, NB, stride=ROWS), :] = cot32[r]
    out_ref[...] = rows32[...].reshape(NB, ROWS, LANES).astype(BF16)

    for k in range(PEERS - 1):
        source = chip_at(k)

        @pl.when(source < OWNERS)
        def _():
            ag_copy(k, source).wait_recv()
            sib_copy(source).start()

    def store(source, which):
        for grad, ref in enumerate((g1_ref, g2_ref)):
            @pl.when(which == grad)
            def _():
                for half in range(2):
                    ref[:, half * LANES : (half + 1) * LANES] = source[half]

    store(sums, core)

    @pl.loop(0, OWNERS)
    def _(source):
        sib_copy(source).wait_recv()

    store(sib_in, 1 - core)

    to_left.wait_send()
    to_right.wait_send()
    w_out.wait_send()
    for buf, sems in ((gath.at[0], main_sems.at[0]), (gath.at[1], main_sems.at[1]), (hgath, hg_sems)):
        for j in (0, 1, 2, 3, 4, 5, 7 if buf is hgath else 6):
            hop(buf, sems, j).wait_send()

    @pl.loop(1, CH)
    def _(k):
        halo_copy(k, chan).wait_send()

    @pl.when(column < 3)
    def _():
        @pl.loop(1, CH)
        def _(k):
            w_copy(k, chan_at(k), chan).wait_send()

        @pl.loop(1, 4)
        def _(k):
            tile_copy(k, column).wait_send()

    @pl.loop(1, CH)
    def _(k):
        g2_copy(chan_at(k), core, chan).wait_send()

    @pl.when(core == 0)
    def _():
        g2_copy(chan, core, chan).wait_send()

    @pl.when(core == 1)
    def _():
        for p in range(3):
            g1_copy(p).wait_send()

    @pl.loop(0, OWNERS)
    def _(owner):
        sib_copy(owner).wait_send()

        @pl.when(owner != chip)
        def _():
            rs_copy(owner).wait_send()

    @pl.when(chip < OWNERS)
    def _():
        for k in range(PEERS - 1):
            ag_copy(k, chip).wait_send()


def on_device(field, first_weight, second_weight, cotangent):
    vmem = pl.BlockSpec(memory_space=pltpu.VMEM)
    hbm = pl.BlockSpec(memory_space=pltpu.HBM)
    dma = pltpu.SemaphoreType.DMA
    out, first_grad, second_grad = pl.pallas_call(
        kernel,
        out_shape=(
            jax.ShapeDtypeStruct((NB, ROWS, LANES), BF16),
            jax.ShapeDtypeStruct((9 * NB, CH * NB), BF16),
            jax.ShapeDtypeStruct((9 * NB, CH * NB), BF16),
        ),
        in_specs=[hbm] * 4,
        out_specs=(vmem, vmem, vmem),
        scratch_shapes=[
            pltpu.VMEM((NB, ROWS, LANES), BF16),
            pltpu.VMEM((NB, ROWS, LANES), BF16),
            pltpu.VMEM((9, NB, CH * NB), BF16),
            pltpu.VMEM((9, NB, CH * NB), BF16),
            pltpu.VMEM((NB * ROWS, LANES), F32),
            pltpu.VMEM((2, CH, ROWS, NB, LANES), BF16),
            pltpu.VMEM((CH, NB, LANES), BF16),
            pltpu.VMEM((NB, LANES), BF16),
            pltpu.VMEM((2, NB, LANES), BF16),
            pltpu.VMEM((ROWS, NB, LANES), F32),
            pltpu.VMEM((2, 9 * NB, CH * NB), BF16),
            pltpu.VMEM((CH, NB, LANES), BF16),
            pltpu.VMEM((2, 3, CH, NB, LANES), BF16),
            pltpu.VMEM((ROWS + 1, 9 * NB, LANES), F32),
            pltpu.VMEM((2, 4, ROWS, NB, LANES), F32),
            pltpu.VMEM((3, ROWS + 2, NB, LANES), F32),
            pltpu.VMEM((2, 3, ROWS + 2, NB, LANES), BF16),
            pltpu.VMEM((NB, LANES), F32),
            pltpu.VMEM((CH, ROWS + 1, NB, LANES), BF16),
            pltpu.VMEM((CH, 3, NB, LANES), BF16),
            pltpu.VMEM((2, CH, 3, NB, LANES), BF16),
            pltpu.VMEM((3, 3 * NB, CH * NB), F32),
            pltpu.VMEM((3, 3 * NB, CH * NB), F32),
            pltpu.VMEM((2, 9 * NB, LANES), BF16),
            pltpu.VMEM((PEERS, PIECE, LANES), BF16),
            pltpu.VMEM((2, 9 * NB, LANES), BF16),
            pltpu.VMEM((2, 9 * NB, LANES), BF16),
            dma((4,)),
            dma((2, 2)),
            dma((2, 2, len(HOPS))),
            dma((2, CH)),
            dma((2, CH)),
            dma((2, 4)),
            dma((2, 1)),
            dma((2, len(HOPS))),
            dma((2, 2, CH)),
            dma((2, 3)),
            dma((2,)),
            dma((2, PEERS)),
            dma((2, OWNERS)),
        ],
        compiler_params=pltpu.CompilerParams(
            collective_id=0, has_side_effects=True, vmem_limit_bytes=40 * 1024 * 1024
        ),
    )(
        *(
            pltpu.with_memory_space_constraint(x, pltpu.HBM)
            for x in (
                field, first_weight.transpose(1, 0, 2), second_weight.transpose(1, 0, 2), cotangent
            )
        )
    )

    def taps_inside(grad):
        return grad.astype(F32).reshape(9, NB, CH * NB).transpose(1, 0, 2)

    return (out, taps_inside(first_grad), taps_inside(second_grad))


def solution(mesh):
    in_specs = (
        P("chan", None, "space"),
        P("chan", None, None),
        P("chan", None, None),
        P("chan", None, "space"),
    )
    out_specs = (P("chan", None, "space"), P("chan", None, None), P("chan", None, None))
    return jax.shard_map(
        on_device, mesh=mesh, in_specs=in_specs, out_specs=out_specs, check_vma=False
    )
```

```python
import math

import jax
import jax.numpy as jnp
from jax import lax
from jax.experimental import pallas as pl
from jax.experimental.pallas import tpu as pltpu
from jax.sharding import PartitionSpec as P

MESH = pl.DeviceIdType.MESH
F32 = jnp.float32
BF16 = jnp.bfloat16
CH = 8
SP = 32
NB = 32
ROWS = 8
LANES = 128
PEERS = SP // 2
OWNERS = 12
PIECE = 48
TAPS = [(p, q) for p in (-1, 0, 1) for q in (-1, 0, 1)]


def tap(p, q):
    return 3 * (p + 1) + q + 1


def lane_ids(shape):
    return lax.broadcasted_iota(jnp.int32, shape, len(shape) - 1)


def roll(values, amount):
    amount = amount % LANES
    if amount == 0:
        return values
    return pltpu.roll(values, amount, 1)


def shift_main(main, ext, step):
    wraps = lane_ids(main.shape) == (0 if step == 1 else LANES - 1)
    return roll(jnp.where(wraps, ext, main), -step)


def shift(main, ext, step):
    return shift_main(main, ext, step), shift_main(ext, main, step)


def row_up(values, size):
    return jnp.concatenate([values[size:], jnp.zeros((size, LANES), F32)], axis=0)


def row_down(values, size):
    return jnp.concatenate([jnp.zeros((size, LANES), F32), values[:-size]], axis=0)


def row_of_lane(shape, offset=0):
    return ((lane_ids(shape) + 8 - offset) // 16) % 8


def pack(tiles):
    total = jnp.zeros(tiles[0].shape, F32)
    owner = row_of_lane(tiles[0].shape)
    for r in range(ROWS):
        total = jnp.where(owner == r, roll(tiles[r], 16 * r), total)
    return total


def load_tap(prod, t, group, size):
    rows = pl.ds(pl.multiple_of(t * NB + group * size, 8), size)
    main = prod[0:ROWS, rows, :].reshape(ROWS * size, LANES)
    return main, prod[ROWS, rows, :]


def combine(prod, group, size, offset=0):
    mains, packs = [], []
    owner = row_of_lane((size, LANES), offset)
    for q in (-1, 0, 1):
        up_main, up_pack = load_tap(prod, tap(1, q), group, size)
        mid_main, mid_pack = load_tap(prod, tap(0, q), group, size)
        down_main, down_pack = load_tap(prod, tap(-1, q), group, size)
        mains.append(mid_main + row_up(up_main, size) + row_down(down_main, size))
        packs.append(
            mid_pack
            + jnp.where(owner == ROWS - 1, 0.0, roll(up_pack, -16))
            + jnp.where(owner == 0, 0.0, roll(down_pack, 16))
        )
    near = (lane_ids((size, LANES)) - offset) % 16
    from_left, from_right = roll(packs[0], 1), roll(packs[2], -1)
    edges = jnp.where(near == 0, from_left, from_right)
    outer = packs[1] + jnp.where(near == 0, 0.0, from_left) + jnp.where(near == 15, 0.0, from_right)

    def expand(values):
        return jnp.concatenate([roll(values, -16 * r - offset) for r in range(ROWS)], axis=0)

    lane = lane_ids(mains[1].shape)
    first, last = lane == 0, lane == LANES - 1
    before, after, edges = roll(mains[0], 1), roll(mains[2], -1), expand(edges)
    main = mains[1] + jnp.where(first, edges, before) + jnp.where(last, edges, after)
    ext = expand(outer) + jnp.where(first, before, 0.0) + jnp.where(last, after, 0.0)
    return main, ext


def gelu_both(v):
    scale = math.sqrt(2.0 / math.pi)
    square = v * v
    t = jnp.tanh(scale * v * (1.0 + 0.044715 * square))
    half = 0.5 * (1.0 + t)
    slope = half + 0.5 * v * (1.0 - t * t) * (scale * (1.0 + 3.0 * 0.044715 * square))
    return v * half, slope


def rounded(values):
    return values.astype(BF16).astype(F32)


def resample_forward(prod, group, size, slopes, smooth):
    h, h_ext = combine(prod, group, size)
    h, h_ext = rounded(h), rounded(h_ext)
    hc, hc_ext = shift(h, h_ext, 1)
    acts = []
    for part, (x, y) in enumerate(((h, hc), (h_ext, hc_ext))):
        x_low, y_low = row_up(x, size), row_up(y, size)
        points = (x, (x + y) * 0.5, (x + x_low) * 0.5, (x + y + x_low + y_low) * 0.25)
        values = []
        for kind, point in enumerate(points):
            value, slope = gelu_both(point)
            values.append(value)
            slopes[part, kind, :, group_rows(group, size), :] = slope.reshape(ROWS, size, LANES)
        acts.append(values)
    base, moved = [], []
    for values in acts:
        side = 2.0 * values[1] + values[3] + row_down(values[3], size)
        base.append(side + 4.0 * values[0] + 2.0 * (values[2] + row_down(values[2], size)))
        moved.append(side)
    left, left_ext = shift(moved[0], moved[1], -1)
    main, ext = rounded((base[0] + left) * 0.0625), rounded((base[1] + left_ext) * 0.0625)
    store_shifted(smooth, shift_main(main, ext, -1), main, shift_main(main, ext, 1), group, size)


def group_rows(group, size):
    return pl.ds(pl.multiple_of(group * size, 8), size)


def store_shifted(ref, *args):
    before, here, after, group, size = args
    for q, values in enumerate((before, here, after)):
        ref[q, 1 : ROWS + 1, group_rows(group, size), :] = values.reshape(ROWS, size, LANES)


def resample_backward(prod, group, size, slopes, grads, packed):
    g, g_ext = combine(prod, group, size, 8)
    g, g_ext = rounded(g), rounded(g_ext)
    gc, gc_ext = shift(g, g_ext, 1)
    base, moved = [], []
    for part, (x, y) in enumerate(((g, gc), (g_ext, gc_ext))):
        odd = (x + row_up(x, size)) * 0.25
        odd_next = (y + row_up(y, size)) * 0.25
        ups = (x * 0.25, (x + y) * 0.125, odd * 0.5, (odd + odd_next) * 0.25)
        b = [
            up * slopes[part, kind, :, group_rows(group, size), :].reshape(ROWS * size, LANES)
            for kind, up in enumerate(ups)
        ]
        half = b[1] * 0.5 + (b[3] + row_down(b[3], size)) * 0.25
        base.append(b[0] + (b[2] + row_down(b[2], size)) * 0.5 + half)
        moved.append(half)
    left, left_ext = shift(moved[0], moved[1], -1)
    main, ext = rounded(base[0] + left), rounded(base[1] + left_ext)
    store_shifted(grads, shift_main(main, ext, 1), main, shift_main(main, ext, -1), group, size)
    packed[group_rows(group, size), :] = pack([ext[r * size : (r + 1) * size] for r in range(ROWS)])


def products(weights, block, halo, prod):
    for r in range(0, ROWS, 2):
        pair = jnp.concatenate(
            [block[:, r].reshape(CH * NB, LANES), block[:, r + 1].reshape(CH * NB, LANES)], axis=1
        )
        out = jnp.dot(weights, pair, preferred_element_type=F32)
        prod[r] = out[:, :LANES]
        prod[r + 1] = out[:, LANES:]
    prod[ROWS] = jnp.dot(weights, halo.reshape(CH * NB, LANES), preferred_element_type=F32)


def row_pair(block, r):
    return jnp.concatenate(
        [block[:, r].reshape(CH * NB, LANES), block[:, r + 1].reshape(CH * NB, LANES)], axis=1
    )


def tap_rows(ref, r, sign):
    return jnp.concatenate(
        [ref[:, r + sign * p + 1].reshape(3 * NB, LANES) for p in (-1, 0, 1)], axis=0
    )


def tap_row_pair(ref, r, sign):
    return jnp.concatenate([tap_rows(ref, r, sign), tap_rows(ref, r + 1, sign)], axis=1)


def contract_last(a, b):
    return lax.dot_general(a, b, (((1,), (1,)), ((), ())), preferred_element_type=F32)


NEAREST = sorted(
    ((dz, dx) for dz in range(4) for dx in range(4) if dz or dx),
    key=lambda d: (2 * min(d[0], 4 - d[0]) + min(d[1], 4 - d[1]), d),
)

FARTHEST = (4, 3, 5, 2, 6, 1, 7)

HOPS = (
    ((0, 0), (1, 0), (-1, 0)),
    ((0, 0), (-1, 0), (1, 0)),
    ((0, 0), (0, 1), (0, 1)),
    ((0, 0), (2, 0), (2, 0)),
    ((0, 1), (1, 0), (-1, 1)),
    ((0, 1), (-1, 0), (1, 1)),
    ((2, 0), (0, 1), (2, 1)),
    ((0, 1), (2, 0), (2, 1)),
)


def kernel(
    field_hbm, w1_hbm, w2_hbm, cot_hbm, out_ref, g1_ref, g2_ref,
    field_in, cot_in, w1_in, w_in,
    rows32, gath, halo, edge, edge_in, cot32, lhs2, wsend, wrecv,
    prod, slopes, shifted32, shifted, packed32, hgath,
    g2send, g2recv, g1part, g1swap, rs_send, rs_recv, sums, sib_in,
    in_sems, edge_sems, main_sems, halo_sems, w_sems, tile_sems, wsib_sems, hg_sems, g2_sems,
    g1_sems, rs_sems, ag_sems, sib_sems,
):
    chan = lax.axis_index("chan")
    space = lax.axis_index("space")
    core = lax.rem(space, 2)
    chip = lax.div(space, 2)
    line, level = lax.div(chan, 2), lax.rem(chan, 2)
    column = lax.rem(chip, 4)
    plane = lax.div(chip, 4)
    left = lax.rem(space + SP - 1, SP)
    right = lax.rem(space + 1, SP)
    sibling = space + 1 - 2 * core
    scale = 1.0 / math.sqrt(ROWS * LANES * SP)

    def chan_at(k):
        return lax.rem(chan + k, CH)

    def chip_at(k):
        dz, dx = NEAREST[k]
        return lax.rem(plane + dz, 4) * 4 + lax.rem(column + dx, 4)

    def block_at(place):
        step, other = place
        at = 1 - level if other else level
        return lax.rem(line + step + 4, 4) * 2 + at

    def fetch(src, dst, k):
        return pltpu.make_async_copy(src, dst, in_sems.at[k])

    fetch(field_hbm, field_in, 0).start()
    fetch(cot_hbm, cot_in, 1).start()

    barrier = pltpu.get_barrier_semaphore()

    def greet(**target):
        pl.semaphore_signal(barrier, inc=1, device_id=target, device_id_type=MESH)

    @pl.loop(1, CH)
    def _(k):
        greet(chan=chan_at(k))
        greet(chan=chan_at(k), space=sibling)

    greet(space=left)
    greet(space=right)

    @pl.loop(1, PEERS)
    def _(k):
        greet(space=lax.rem(chip + k, PEERS) * 2 + core)

    fetch(w1_hbm, w1_in, 2).start()

    @pl.when(core == 0)
    def _():
        fetch(w1_hbm, w_in, 3).start()

    @pl.when(core == 1)
    def _():
        fetch(w2_hbm, w_in, 3).start()

    def remote(src, dst, sems, k, **target):
        return pltpu.make_async_remote_copy(
            src_ref=src, dst_ref=dst, send_sem=sems.at[0, k], recv_sem=sems.at[1, k],
            device_id=target, device_id_type=MESH,
        )

    def hop(buf, sems, j):
        sent = block_at(HOPS[j][0])
        return remote(buf.at[sent], buf.at[sent], sems, j, chan=block_at(HOPS[j][1]))

    def hop_in(buf, sems, j):
        got = block_at(HOPS[j][2])
        return remote(buf.at[got], buf.at[got], sems, j, chan=block_at(HOPS[j][1]))

    def send(buf, sems, *hops):
        for j in hops:
            hop(buf, sems, j).start()

    def arrive(buf, sems, *hops):
        for j in hops:
            hop_in(buf, sems, j).wait_recv()

    def second_hops(buf, sems):
        arrive(buf, sems, 2)
        send(buf, sems, 4, 5)
        arrive(buf, sems, 3)
        send(buf, sems, 6)

    def last_hops(buf, sems):
        arrive(buf, sems, 0, 1, 4, 5, 6)

    def split_rows(source):
        rows32[...] = source[...].astype(F32).reshape(NB * ROWS, LANES)
        return [rows32[pl.ds(r, NB, stride=ROWS), :] for r in range(ROWS)]

    lane = lane_ids((NB, LANES))
    fetch(field_hbm, field_in, 0).wait()
    field_rows = split_rows(field_in)
    for r in range(ROWS):
        gath[0, chan, r] = field_rows[r].astype(BF16)
    edge_field = pack(field_rows)
    fetch(cot_hbm, cot_in, 1).wait()
    cot_rows = split_rows(cot_in)
    for r in range(ROWS):
        gath[1, chan, r] = cot_rows[r].astype(BF16)
        cot32[r] = cot_rows[r]
    near = (lane % 16 < 4) | (lane % 16 >= 12)
    edge[...] = jnp.where(near, edge_field, roll(pack(cot_rows), 8)).astype(BF16)

    fetch(w1_hbm, w1_in, 2).wait()
    fetch(w1_hbm, w_in, 3).wait()

    def w_copy(k, dest, slot):
        return remote(wsend.at[dest], wrecv.at[core, column, slot], w_sems, k, chan=chan_at(k))

    @pl.when(column < 3)
    def _():
        loaded = [
            jnp.where(
                4 * column + u < 9, w_in[jnp.maximum(8 - 4 * column - u, 0)].astype(F32), 0.0
            )
            for u in range(4)
        ]
        for dest in range(CH):
            half, place = dest // 4, dest % 4
            total = jnp.zeros((NB, LANES), F32)
            for u, values in enumerate(loaded):
                source = values[:, half * LANES : (half + 1) * LANES]
                total = jnp.where(lane // NB == u, roll(source, (u - place) * NB), total)
            wsend[dest] = total.astype(BF16)
        wrecv[core, column, chan] = wsend[chan]

    pl.semaphore_wait(barrier, 2 * (CH - 1) + PEERS - 1 + 2)

    to_left = remote(edge, edge_in.at[0], edge_sems, 0, space=left)
    to_right = remote(edge, edge_in.at[1], edge_sems, 1, space=right)
    to_left.start()
    to_right.start()

    @pl.when(column < 3)
    def _():
        for k in FARTHEST:
            w_copy(k, chan_at(k), chan).start()

    field_all, cot_all = (gath.at[0], main_sems.at[0]), (gath.at[1], main_sems.at[1])
    send(*field_all, 3, 2)
    send(*cot_all, 3, 2)
    send(*field_all, 0, 1)

    to_left.wait_recv()
    to_right.wait_recv()
    from_right = edge_in[0].astype(F32)
    from_left = edge_in[1].astype(F32)
    halo[chan] = jnp.where(lane % 8 < 4, from_right, from_left).astype(BF16)

    def halo_copy(k, slot):
        return remote(halo.at[slot], halo.at[slot], halo_sems, k, chan=chan_at(k))

    for k in FARTHEST:
        halo_copy(k, chan).start()

    def tile_copy(k, tile):
        target = (chip - column + lax.rem(column + k, 4)) * 2 + core
        return pltpu.make_async_remote_copy(
            src_ref=wrecv.at[core, tile], dst_ref=wrecv.at[core, tile], send_sem=tile_sems.at[0, k],
            recv_sem=tile_sems.at[1, tile], device_id={"space": target}, device_id_type=MESH,
        )

    second_hops(*field_all)
    send(*cot_all, 0, 1)

    @pl.when(column < 3)
    def _():
        @pl.loop(1, CH)
        def _(k):
            w_copy(k, chan_at(k), chan_at(CH - k)).wait_recv()

        for k in (2, 1, 3):
            tile_copy(k, column).start()

    second_hops(*cot_all)

    @pl.loop(0, 3)
    def _(tile):
        @pl.when(tile != column)
        def _():
            tile_copy(1, tile).wait_recv()

    w_out = remote(wrecv.at[core], wrecv.at[core], wsib_sems, 0, space=sibling)
    w_out.start()

    last_hops(*field_all)

    @pl.loop(1, CH)
    def _(k):
        halo_copy(k, chan_at(CH - k)).wait_recv()

    group_size = 16
    shifted32[:, 0] = jnp.zeros((3, NB, LANES), F32)
    shifted32[:, ROWS + 1] = jnp.zeros((3, NB, LANES), F32)
    products(w1_in[...].reshape(9 * NB, CH * NB), gath.at[0], halo[...], prod)

    @pl.loop(0, NB // group_size)
    def _(group):
        resample_forward(prod, group, group_size, slopes, shifted32)

    shifted[0] = shifted32[...].astype(BF16)

    remote(wrecv.at[1 - core], wrecv.at[1 - core], wsib_sems, 0, space=sibling).wait_recv()

    def turn_weights(which):
        for k in range(3):
            turned = wrecv[which, k].reshape(CH * NB, LANES).T
            if k < 2:
                lhs2[which, k * LANES : (k + 1) * LANES, :] = turned
            else:
                lhs2[which, 2 * LANES :, :] = turned[:NB]

    turn_weights(1)
    last_hops(*cot_all)
    total = jnp.zeros((CH * NB, 3 * LANES), F32)
    for r in range(0, ROWS, 2):
        rhs = tap_row_pair(shifted.at[0], r, 1)
        rhs = jnp.concatenate([rhs, jnp.zeros((3 * NB, 2 * LANES), BF16)], axis=0)
        total = total + contract_last(row_pair(gath.at[1], r), rhs)
    total = (total * scale).astype(BF16)
    for k in range(3):
        g2send[:, k] = total[:, k * LANES : (k + 1) * LANES].reshape(CH, NB, LANES)

    def g2_copy(dest, source_core, source):
        return pltpu.make_async_remote_copy(
            src_ref=g2send.at[dest], dst_ref=g2recv.at[source_core, source],
            send_sem=g2_sems.at[0, 0, dest], recv_sem=g2_sems.at[1, source_core, source],
            device_id={"chan": dest, "space": 2 * chip + 1}, device_id_type=MESH,
        )

    for k in FARTHEST:
        g2_copy(chan_at(k), core, chan).start()

    @pl.when(core == 0)
    def _():
        g2_copy(chan, core, chan).start()

    @pl.when(core == 1)
    def _():
        g2recv[1, chan] = g2send[chan]

    products(lhs2[1], gath.at[1], halo[...], prod)

    @pl.loop(0, NB // group_size)
    def _(group):
        resample_backward(prod, group, group_size, slopes, shifted32, packed32)

    shifted[1] = shifted32[...].astype(BF16)
    hgath[chan, 0:ROWS] = shifted[1, 1, 1 : ROWS + 1]
    hgath[chan, ROWS] = packed32[...].astype(BF16)
    send(hgath, hg_sems, *(2, 3, 0, 1))

    def g1_copy(p):
        return remote(g1part.at[p], g1swap.at[p], g1_sems, p, space=sibling)

    chunks = range(3)
    for p in chunks:
        total = jnp.zeros((3 * NB, CH * NB), F32)
        for r in range(0, ROWS, 2):
            lhs = jnp.concatenate(
                [shifted[1, :, r + i - p + 2].reshape(3 * NB, LANES) for i in range(2)], axis=1
            )
            total = total + contract_last(lhs, row_pair(gath.at[0], r))
        g1part[p] = total * scale

        @pl.when(core == 1)
        def _():
            g1_copy(p).start()

    def piece_of(ref, owner):
        rows = pl.ds(pl.multiple_of(lax.div(owner, 2) * PIECE, 16), PIECE)
        return ref.at[lax.rem(owner, 2), rows]

    def rs_copy(owner):
        slot = lax.rem(chip - owner + PEERS, PEERS) - 1
        return pltpu.make_async_remote_copy(
            src_ref=piece_of(rs_send, owner), dst_ref=rs_recv.at[slot], send_sem=rs_sems.at[0],
            recv_sem=rs_sems.at[1],
            device_id={"space": owner * 2 + core}, device_id_type=MESH,
        )

    def all_pieces(count):
        return pltpu.make_async_remote_copy(
            src_ref=rs_recv.at[pl.ds(0, count)], dst_ref=rs_recv.at[pl.ds(0, count)],
            send_sem=rs_sems.at[0], recv_sem=rs_sems.at[1],
            device_id={"space": sibling}, device_id_type=MESH,
        )

    def to_owners(p):
        for step in range(4):
            owner = 4 * p + lax.rem(column + (2, 1, 3, 0)[step], 4)

            @pl.when(owner == chip)
            def _():
                rs_recv[PEERS - 1] = piece_of(rs_send, chip)[...]

            @pl.when(owner != chip)
            def _():
                rs_copy(owner).start()

    def put_rows(first, values):
        for half in range(2):
            rs_send[half, pl.ds(pl.multiple_of(first, 16), values.shape[0])] = values[
                :, half * LANES : (half + 1) * LANES
            ].astype(BF16)

    @pl.when(core == 1)
    def _():
        g2_copy(chan, 0, chan).wait_recv()

        @pl.loop(1, CH)
        def _(k):
            for source_core in range(2):
                g2_copy(chan, source_core, chan_at(k)).wait_recv()

        for k in range(3):
            loaded = [
                g2recv[0, s, k].astype(F32) + g2recv[1, s, k].astype(F32) for s in range(CH)
            ]
            for t in range(4 * k, min(4 * k + 4, 9)):
                for half in range(2):
                    total = jnp.zeros((NB, LANES), F32)
                    for place in range(4):
                        moved = roll(loaded[4 * half + place], (place - t % 4) * NB)
                        total = jnp.where(lane // NB == place, moved, total)
                    rs_send[half, t * NB : (t + 1) * NB] = total.astype(BF16)
        for p in chunks:
            to_owners(p)

    @pl.when(core == 0)
    def _():
        for p in chunks:
            g1_copy(p).wait_recv()
            put_rows(96 * p, g1part[p] + g1swap[p])
            to_owners(p)

    arrive(hgath, hg_sems, 2)
    send(hgath, hg_sems, 7, 4, 5)
    turn_weights(0)

    def ag_copy(k, slot):
        return pltpu.make_async_remote_copy(
            src_ref=piece_of(sums, slot), dst_ref=piece_of(sums, slot), send_sem=ag_sems.at[0, k],
            recv_sem=ag_sems.at[1, slot],
            device_id={"space": chip_at(k) * 2 + core}, device_id_type=MESH,
        )

    def sib_copy(slot):
        return remote(piece_of(sums, slot), piece_of(sib_in, slot), sib_sems, slot, space=sibling)

    @pl.when(chip < OWNERS)
    def _():
        all_pieces(PEERS - 1).wait_recv()
        total = rs_recv[0].astype(F32)
        for s in range(1, PEERS):
            total = total + rs_recv[s].astype(F32)
        piece_of(sums, chip)[...] = total.astype(BF16)

        for k in reversed(range(PEERS - 1)):
            ag_copy(k, chip).start()
        sib_copy(chip).start()

    arrive(hgath, hg_sems, 0, 1, 3, 4, 5, 7)
    products(lhs2[0], hgath, hgath[:, ROWS], prod)

    @pl.loop(0, NB // group_size)
    def _(group):
        main, _ = combine(prod, group, group_size)
        rows = group_rows(group, group_size)
        cot32[:, rows, :] = cot32[:, rows, :] + main.reshape(ROWS, group_size, LANES)

    for r in range(ROWS):
        rows32[pl.ds(r, NB, stride=ROWS), :] = cot32[r]
    out_ref[...] = rows32[...].reshape(NB, ROWS, LANES).astype(BF16)

    for k in range(PEERS - 1):
        source = chip_at(k)

        @pl.when(source < OWNERS)
        def _():
            ag_copy(k, source).wait_recv()
            sib_copy(source).start()

    def store(source, which):
        for grad, ref in enumerate((g1_ref, g2_ref)):
            @pl.when(which == grad)
            def _():
                for half in range(2):
                    ref[:, half * LANES : (half + 1) * LANES] = source[half]

    store(sums, core)

    @pl.loop(0, OWNERS)
    def _(source):
        sib_copy(source).wait_recv()

    store(sib_in, 1 - core)

    to_left.wait_send()
    to_right.wait_send()
    w_out.wait_send()
    for buf, sems in ((gath.at[0], main_sems.at[0]), (gath.at[1], main_sems.at[1]), (hgath, hg_sems)):
        for j in (0, 1, 2, 3, 4, 5, 7 if buf is hgath else 6):
            hop(buf, sems, j).wait_send()

    @pl.loop(1, CH)
    def _(k):
        halo_copy(k, chan).wait_send()

    @pl.when(column < 3)
    def _():
        @pl.loop(1, CH)
        def _(k):
            w_copy(k, chan_at(k), chan).wait_send()

        @pl.loop(1, 4)
        def _(k):
            tile_copy(k, column).wait_send()

    @pl.loop(1, CH)
    def _(k):
        g2_copy(chan_at(k), core, chan).wait_send()

    @pl.when(core == 0)
    def _():
        g2_copy(chan, core, chan).wait_send()

    @pl.when(core == 1)
    def _():
        for p in range(3):
            g1_copy(p).wait_send()

    @pl.loop(0, OWNERS)
    def _(owner):
        sib_copy(owner).wait_send()

        @pl.when(owner != chip)
        def _():
            rs_copy(owner).wait_send()

    @pl.when(chip < OWNERS)
    def _():
        for k in range(PEERS - 1):
            ag_copy(k, chip).wait_send()


def on_device(field, first_weight, second_weight, cotangent):
    vmem = pl.BlockSpec(memory_space=pltpu.VMEM)
    hbm = pl.BlockSpec(memory_space=pltpu.HBM)
    dma = pltpu.SemaphoreType.DMA
    out, first_grad, second_grad = pl.pallas_call(
        kernel,
        out_shape=(
            jax.ShapeDtypeStruct((NB, ROWS, LANES), BF16),
            jax.ShapeDtypeStruct((9 * NB, CH * NB), BF16),
            jax.ShapeDtypeStruct((9 * NB, CH * NB), BF16),
        ),
        in_specs=[hbm] * 4,
        out_specs=(vmem, vmem, vmem),
        scratch_shapes=[
            pltpu.VMEM((NB, ROWS, LANES), BF16),
            pltpu.VMEM((NB, ROWS, LANES), BF16),
            pltpu.VMEM((9, NB, CH * NB), BF16),
            pltpu.VMEM((9, NB, CH * NB), BF16),
            pltpu.VMEM((NB * ROWS, LANES), F32),
            pltpu.VMEM((2, CH, ROWS, NB, LANES), BF16),
            pltpu.VMEM((CH, NB, LANES), BF16),
            pltpu.VMEM((NB, LANES), BF16),
            pltpu.VMEM((2, NB, LANES), BF16),
            pltpu.VMEM((ROWS, NB, LANES), F32),
            pltpu.VMEM((2, 9 * NB, CH * NB), BF16),
            pltpu.VMEM((CH, NB, LANES), BF16),
            pltpu.VMEM((2, 3, CH, NB, LANES), BF16),
            pltpu.VMEM((ROWS + 1, 9 * NB, LANES), F32),
            pltpu.VMEM((2, 4, ROWS, NB, LANES), F32),
            pltpu.VMEM((3, ROWS + 2, NB, LANES), F32),
            pltpu.VMEM((2, 3, ROWS + 2, NB, LANES), BF16),
            pltpu.VMEM((NB, LANES), F32),
            pltpu.VMEM((CH, ROWS + 1, NB, LANES), BF16),
            pltpu.VMEM((CH, 3, NB, LANES), BF16),
            pltpu.VMEM((2, CH, 3, NB, LANES), BF16),
            pltpu.VMEM((3, 3 * NB, CH * NB), F32),
            pltpu.VMEM((3, 3 * NB, CH * NB), F32),
            pltpu.VMEM((2, 9 * NB, LANES), BF16),
            pltpu.VMEM((PEERS, PIECE, LANES), BF16),
            pltpu.VMEM((2, 9 * NB, LANES), BF16),
            pltpu.VMEM((2, 9 * NB, LANES), BF16),
            dma((4,)),
            dma((2, 2)),
            dma((2, 2, len(HOPS))),
            dma((2, CH)),
            dma((2, CH)),
            dma((2, 4)),
            dma((2, 1)),
            dma((2, len(HOPS))),
            dma((2, 2, CH)),
            dma((2, 3)),
            dma((2,)),
            dma((2, PEERS)),
            dma((2, OWNERS)),
        ],
        compiler_params=pltpu.CompilerParams(
            collective_id=0, has_side_effects=True, vmem_limit_bytes=40 * 1024 * 1024
        ),
    )(
        *(
            pltpu.with_memory_space_constraint(x, pltpu.HBM)
            for x in (
                field, first_weight.transpose(1, 0, 2), second_weight.transpose(1, 0, 2), cotangent
            )
        )
    )

    def taps_inside(grad):
        return grad.astype(F32).reshape(9, NB, CH * NB).transpose(1, 0, 2)

    return (out, taps_inside(first_grad), taps_inside(second_grad))


def solution(mesh):
    in_specs = (
        P("chan", None, "space"),
        P("chan", None, None),
        P("chan", None, None),
        P("chan", None, "space"),
    )
    out_specs = (P("chan", None, "space"), P("chan", None, None), P("chan", None, None))
    return jax.shard_map(
        on_device, mesh=mesh, in_specs=in_specs, out_specs=out_specs, check_vma=False
    )
```

```python
import math

import jax
import jax.numpy as jnp
from jax import lax
from jax.experimental import pallas as pl
from jax.experimental.pallas import tpu as pltpu
from jax.sharding import PartitionSpec as P

MESH = pl.DeviceIdType.MESH
F32 = jnp.float32
BF16 = jnp.bfloat16
CH = 8
SP = 32
NB = 32
ROWS = 8
LANES = 128
PEERS = SP // 2
OWNERS = 12
PIECE = 48
TAPS = [(p, q) for p in (-1, 0, 1) for q in (-1, 0, 1)]


def tap(p, q):
    return 3 * (p + 1) + q + 1


def lane_ids(shape):
    return lax.broadcasted_iota(jnp.int32, shape, len(shape) - 1)


def roll(values, amount):
    amount = amount % LANES
    if amount == 0:
        return values
    return pltpu.roll(values, amount, 1)


def shift_main(main, ext, step):
    wraps = lane_ids(main.shape) == (0 if step == 1 else LANES - 1)
    return roll(jnp.where(wraps, ext, main), -step)


def shift(main, ext, step):
    return shift_main(main, ext, step), shift_main(ext, main, step)


def row_up(values, size):
    return jnp.concatenate([values[size:], jnp.zeros((size, LANES), F32)], axis=0)


def row_down(values, size):
    return jnp.concatenate([jnp.zeros((size, LANES), F32), values[:-size]], axis=0)


def row_of_lane(shape, offset=0):
    return ((lane_ids(shape) + 8 - offset) // 16) % 8


def pack(tiles):
    total = jnp.zeros(tiles[0].shape, F32)
    owner = row_of_lane(tiles[0].shape)
    for r in range(ROWS):
        total = jnp.where(owner == r, roll(tiles[r], 16 * r), total)
    return total


def load_tap(prod, t, group, size):
    rows = pl.ds(pl.multiple_of(t * NB + group * size, 8), size)
    main = prod[0:ROWS, rows, :].reshape(ROWS * size, LANES)
    return main, prod[ROWS, rows, :]


def combine(prod, group, size, offset=0):
    mains, packs = [], []
    owner = row_of_lane((size, LANES), offset)
    for q in (-1, 0, 1):
        up_main, up_pack = load_tap(prod, tap(1, q), group, size)
        mid_main, mid_pack = load_tap(prod, tap(0, q), group, size)
        down_main, down_pack = load_tap(prod, tap(-1, q), group, size)
        mains.append(mid_main + row_up(up_main, size) + row_down(down_main, size))
        packs.append(
            mid_pack
            + jnp.where(owner == ROWS - 1, 0.0, roll(up_pack, -16))
            + jnp.where(owner == 0, 0.0, roll(down_pack, 16))
        )
    near = (lane_ids((size, LANES)) - offset) % 16
    from_left, from_right = roll(packs[0], 1), roll(packs[2], -1)
    edges = jnp.where(near == 0, from_left, from_right)
    outer = packs[1] + jnp.where(near == 0, 0.0, from_left) + jnp.where(near == 15, 0.0, from_right)

    def expand(values):
        return jnp.concatenate([roll(values, -16 * r - offset) for r in range(ROWS)], axis=0)

    lane = lane_ids(mains[1].shape)
    first, last = lane == 0, lane == LANES - 1
    before, after, edges = roll(mains[0], 1), roll(mains[2], -1), expand(edges)
    main = mains[1] + jnp.where(first, edges, before) + jnp.where(last, edges, after)
    ext = expand(outer) + jnp.where(first, before, 0.0) + jnp.where(last, after, 0.0)
    return main, ext


def gelu_both(v):
    scale = math.sqrt(2.0 / math.pi)
    square = v * v
    t = jnp.tanh(scale * v * (1.0 + 0.044715 * square))
    half = 0.5 * (1.0 + t)
    slope = half + 0.5 * v * (1.0 - t * t) * (scale * (1.0 + 3.0 * 0.044715 * square))
    return v * half, slope


def rounded(values):
    return values.astype(BF16).astype(F32)


def resample_forward(prod, group, size, slopes, smooth):
    h, h_ext = combine(prod, group, size)
    h, h_ext = rounded(h), rounded(h_ext)
    hc, hc_ext = shift(h, h_ext, 1)
    acts = []
    for part, (x, y) in enumerate(((h, hc), (h_ext, hc_ext))):
        x_low, y_low = row_up(x, size), row_up(y, size)
        points = (x, (x + y) * 0.5, (x + x_low) * 0.5, (x + y + x_low + y_low) * 0.25)
        values = []
        for kind, point in enumerate(points):
            value, slope = gelu_both(point)
            values.append(value)
            slopes[part, kind, :, group_rows(group, size), :] = slope.reshape(ROWS, size, LANES)
        acts.append(values)
    base, moved = [], []
    for values in acts:
        side = 2.0 * values[1] + values[3] + row_down(values[3], size)
        base.append(side + 4.0 * values[0] + 2.0 * (values[2] + row_down(values[2], size)))
        moved.append(side)
    left, left_ext = shift(moved[0], moved[1], -1)
    main, ext = rounded((base[0] + left) * 0.0625), rounded((base[1] + left_ext) * 0.0625)
    store_shifted(smooth, shift_main(main, ext, -1), main, shift_main(main, ext, 1), group, size)


def group_rows(group, size):
    return pl.ds(pl.multiple_of(group * size, 8), size)


def store_shifted(ref, *args):
    before, here, after, group, size = args
    for q, values in enumerate((before, here, after)):
        ref[q, 1 : ROWS + 1, group_rows(group, size), :] = values.reshape(ROWS, size, LANES)


def resample_backward(prod, group, size, slopes, grads, packed):
    g, g_ext = combine(prod, group, size, 8)
    g, g_ext = rounded(g), rounded(g_ext)
    gc, gc_ext = shift(g, g_ext, 1)
    base, moved = [], []
    for part, (x, y) in enumerate(((g, gc), (g_ext, gc_ext))):
        odd = (x + row_up(x, size)) * 0.25
        odd_next = (y + row_up(y, size)) * 0.25
        ups = (x * 0.25, (x + y) * 0.125, odd * 0.5, (odd + odd_next) * 0.25)
        b = [
            up * slopes[part, kind, :, group_rows(group, size), :].reshape(ROWS * size, LANES)
            for kind, up in enumerate(ups)
        ]
        half = b[1] * 0.5 + (b[3] + row_down(b[3], size)) * 0.25
        base.append(b[0] + (b[2] + row_down(b[2], size)) * 0.5 + half)
        moved.append(half)
    left, left_ext = shift(moved[0], moved[1], -1)
    main, ext = rounded(base[0] + left), rounded(base[1] + left_ext)
    store_shifted(grads, shift_main(main, ext, 1), main, shift_main(main, ext, -1), group, size)
    packed[group_rows(group, size), :] = pack([ext[r * size : (r + 1) * size] for r in range(ROWS)])


def products(weights, block, halo, prod):
    for r in range(0, ROWS, 2):
        pair = jnp.concatenate(
            [block[:, r].reshape(CH * NB, LANES), block[:, r + 1].reshape(CH * NB, LANES)], axis=1
        )
        out = jnp.dot(weights, pair, preferred_element_type=F32)
        prod[r] = out[:, :LANES]
        prod[r + 1] = out[:, LANES:]
    prod[ROWS] = jnp.dot(weights, halo.reshape(CH * NB, LANES), preferred_element_type=F32)


def row_pair(block, r):
    return jnp.concatenate(
        [block[:, r].reshape(CH * NB, LANES), block[:, r + 1].reshape(CH * NB, LANES)], axis=1
    )


def tap_rows(ref, r, sign):
    return jnp.concatenate(
        [ref[:, r + sign * p + 1].reshape(3 * NB, LANES) for p in (-1, 0, 1)], axis=0
    )


def tap_row_pair(ref, r, sign):
    return jnp.concatenate([tap_rows(ref, r, sign), tap_rows(ref, r + 1, sign)], axis=1)


def contract_last(a, b):
    return lax.dot_general(a, b, (((1,), (1,)), ((), ())), preferred_element_type=F32)


NEAREST = sorted(
    ((dz, dx) for dz in range(4) for dx in range(4) if dz or dx),
    key=lambda d: (2 * min(d[0], 4 - d[0]) + min(d[1], 4 - d[1]), d),
)

HOPS = (
    ((0, 0), (1, 0), (-1, 0)),
    ((0, 0), (-1, 0), (1, 0)),
    ((0, 0), (0, 1), (0, 1)),
    ((0, 0), (2, 0), (2, 0)),
    ((0, 1), (1, 0), (-1, 1)),
    ((0, 1), (-1, 0), (1, 1)),
    ((2, 0), (0, 1), (2, 1)),
    ((0, 1), (2, 0), (2, 1)),
)


def kernel(
    field_hbm, w1_hbm, w2_hbm, cot_hbm, out_ref, g1_ref, g2_ref,
    field_in, cot_in, w1_in, w_in,
    rows32, gath, halo, edge, edge_in, cot32, lhs2, wsend, wrecv,
    prod, slopes, shifted32, shifted, packed32, hgath,
    g2send, g2recv, g1part, g1swap, rs_send, rs_recv, sums, sib_in,
    in_sems, edge_sems, main_sems, halo_sems, w_sems, tile_sems, wsib_sems, hg_sems, g2_sems,
    g1_sems, rs_sems, ag_sems, sib_sems,
):
    chan = lax.axis_index("chan")
    space = lax.axis_index("space")
    core = lax.rem(space, 2)
    chip = lax.div(space, 2)
    line, level = lax.div(chan, 2), lax.rem(chan, 2)
    column = lax.rem(chip, 4)
    plane = lax.div(chip, 4)
    left = lax.rem(space + SP - 1, SP)
    right = lax.rem(space + 1, SP)
    sibling = space + 1 - 2 * core
    scale = 1.0 / math.sqrt(ROWS * LANES * SP)

    def chan_at(k):
        return lax.rem(chan + k, CH)

    def chip_at(k):
        dz, dx = NEAREST[k]
        return lax.rem(plane + dz, 4) * 4 + lax.rem(column + dx, 4)

    def block_at(place):
        step, other = place
        at = 1 - level if other else level
        return lax.rem(line + step + 4, 4) * 2 + at

    def fetch(src, dst, k):
        return pltpu.make_async_copy(src, dst, in_sems.at[k])

    fetch(field_hbm, field_in, 0).start()
    fetch(cot_hbm, cot_in, 1).start()

    barrier = pltpu.get_barrier_semaphore()

    def greet(**target):
        pl.semaphore_signal(barrier, inc=1, device_id=target, device_id_type=MESH)

    @pl.loop(1, CH)
    def _(k):
        greet(chan=chan_at(k))
        greet(chan=chan_at(k), space=sibling)

    greet(space=left)
    greet(space=right)

    @pl.loop(1, PEERS)
    def _(k):
        greet(space=lax.rem(chip + k, PEERS) * 2 + core)

    fetch(w1_hbm, w1_in, 2).start()

    @pl.when(core == 0)
    def _():
        fetch(w1_hbm, w_in, 3).start()

    @pl.when(core == 1)
    def _():
        fetch(w2_hbm, w_in, 3).start()

    def remote(src, dst, sems, k, **target):
        return pltpu.make_async_remote_copy(
            src_ref=src, dst_ref=dst, send_sem=sems.at[0, k], recv_sem=sems.at[1, k],
            device_id=target, device_id_type=MESH,
        )

    def hop(buf, sems, j):
        sent = block_at(HOPS[j][0])
        return remote(buf.at[sent], buf.at[sent], sems, j, chan=block_at(HOPS[j][1]))

    def hop_in(buf, sems, j):
        got = block_at(HOPS[j][2])
        return remote(buf.at[got], buf.at[got], sems, j, chan=block_at(HOPS[j][1]))

    def send(buf, sems, *hops):
        for j in hops:
            hop(buf, sems, j).start()

    def arrive(buf, sems, *hops):
        for j in hops:
            hop_in(buf, sems, j).wait_recv()

    def second_hops(buf, sems):
        arrive(buf, sems, 2)
        send(buf, sems, 4, 5)
        arrive(buf, sems, 3)
        send(buf, sems, 6)

    def last_hops(buf, sems):
        arrive(buf, sems, 0, 1, 4, 5, 6)

    def split_rows(source):
        rows32[...] = source[...].astype(F32).reshape(NB * ROWS, LANES)
        return [rows32[pl.ds(r, NB, stride=ROWS), :] for r in range(ROWS)]

    lane = lane_ids((NB, LANES))
    fetch(field_hbm, field_in, 0).wait()
    field_rows = split_rows(field_in)
    for r in range(ROWS):
        gath[0, chan, r] = field_rows[r].astype(BF16)
    edge_field = pack(field_rows)
    fetch(cot_hbm, cot_in, 1).wait()
    cot_rows = split_rows(cot_in)
    for r in range(ROWS):
        gath[1, chan, r] = cot_rows[r].astype(BF16)
        cot32[r] = cot_rows[r]
    near = (lane % 16 < 4) | (lane % 16 >= 12)
    edge[...] = jnp.where(near, edge_field, roll(pack(cot_rows), 8)).astype(BF16)

    fetch(w1_hbm, w1_in, 2).wait()
    fetch(w1_hbm, w_in, 3).wait()

    def w_copy(k, dest, slot):
        return remote(wsend.at[dest], wrecv.at[core, column, slot], w_sems, k, chan=chan_at(k))

    @pl.when(column < 3)
    def _():
        loaded = [
            jnp.where(
                4 * column + u < 9, w_in[jnp.maximum(8 - 4 * column - u, 0)].astype(F32), 0.0
            )
            for u in range(4)
        ]
        for dest in range(CH):
            half, place = dest // 4, dest % 4
            total = jnp.zeros((NB, LANES), F32)
            for u, values in enumerate(loaded):
                source = values[:, half * LANES : (half + 1) * LANES]
                total = jnp.where(lane // NB == u, roll(source, (u - place) * NB), total)
            wsend[dest] = total.astype(BF16)
        wrecv[core, column, chan] = wsend[chan]

    pl.semaphore_wait(barrier, 2 * (CH - 1) + PEERS - 1 + 2)

    to_left = remote(edge, edge_in.at[0], edge_sems, 0, space=left)
    to_right = remote(edge, edge_in.at[1], edge_sems, 1, space=right)
    to_left.start()
    to_right.start()

    @pl.when(column < 3)
    def _():
        @pl.loop(1, CH)
        def _(k):
            w_copy(k, chan_at(k), chan).start()

    field_all, cot_all = (gath.at[0], main_sems.at[0]), (gath.at[1], main_sems.at[1])
    send(*field_all, 3, 2)
    send(*cot_all, 3, 2)
    send(*field_all, 0, 1)

    to_left.wait_recv()
    to_right.wait_recv()
    from_right = edge_in[0].astype(F32)
    from_left = edge_in[1].astype(F32)
    halo[chan] = jnp.where(lane % 8 < 4, from_right, from_left).astype(BF16)

    def halo_copy(k, slot):
        return remote(halo.at[slot], halo.at[slot], halo_sems, k, chan=chan_at(k))

    for k in (4, 3, 5, 2, 6, 1, 7):
        halo_copy(k, chan).start()

    def tile_copy(k, tile):
        target = (chip - column + lax.rem(column + k, 4)) * 2 + core
        return pltpu.make_async_remote_copy(
            src_ref=wrecv.at[core, tile], dst_ref=wrecv.at[core, tile], send_sem=tile_sems.at[0, k],
            recv_sem=tile_sems.at[1, tile], device_id={"space": target}, device_id_type=MESH,
        )

    second_hops(*field_all)
    send(*cot_all, 0, 1)

    @pl.when(column < 3)
    def _():
        @pl.loop(1, CH)
        def _(k):
            w_copy(k, chan_at(k), chan_at(CH - k)).wait_recv()

        @pl.loop(1, 4)
        def _(k):
            tile_copy(k, column).start()

    second_hops(*cot_all)

    @pl.loop(0, 3)
    def _(tile):
        @pl.when(tile != column)
        def _():
            tile_copy(1, tile).wait_recv()

    w_out = remote(wrecv.at[core], wrecv.at[core], wsib_sems, 0, space=sibling)
    w_out.start()

    last_hops(*field_all)

    @pl.loop(1, CH)
    def _(k):
        halo_copy(k, chan_at(CH - k)).wait_recv()

    group_size = 16
    shifted32[:, 0] = jnp.zeros((3, NB, LANES), F32)
    shifted32[:, ROWS + 1] = jnp.zeros((3, NB, LANES), F32)
    products(w1_in[...].reshape(9 * NB, CH * NB), gath.at[0], halo[...], prod)

    @pl.loop(0, NB // group_size)
    def _(group):
        resample_forward(prod, group, group_size, slopes, shifted32)

    shifted[0] = shifted32[...].astype(BF16)

    remote(wrecv.at[1 - core], wrecv.at[1 - core], wsib_sems, 0, space=sibling).wait_recv()

    def turn_weights(which):
        for k in range(3):
            turned = wrecv[which, k].reshape(CH * NB, LANES).T
            if k < 2:
                lhs2[which, k * LANES : (k + 1) * LANES, :] = turned
            else:
                lhs2[which, 2 * LANES :, :] = turned[:NB]

    turn_weights(1)
    last_hops(*cot_all)
    total = jnp.zeros((CH * NB, 3 * LANES), F32)
    for r in range(0, ROWS, 2):
        rhs = tap_row_pair(shifted.at[0], r, 1)
        rhs = jnp.concatenate([rhs, jnp.zeros((3 * NB, 2 * LANES), BF16)], axis=0)
        total = total + contract_last(row_pair(gath.at[1], r), rhs)
    total = (total * scale).astype(BF16)
    for k in range(3):
        g2send[:, k] = total[:, k * LANES : (k + 1) * LANES].reshape(CH, NB, LANES)

    def g2_copy(dest, source_core, source):
        return pltpu.make_async_remote_copy(
            src_ref=g2send.at[dest], dst_ref=g2recv.at[source_core, source],
            send_sem=g2_sems.at[0, 0, dest], recv_sem=g2_sems.at[1, source_core, source],
            device_id={"chan": dest, "space": 2 * chip + 1}, device_id_type=MESH,
        )

    @pl.loop(1, CH)
    def _(k):
        g2_copy(chan_at(k), core, chan).start()

    @pl.when(core == 0)
    def _():
        g2_copy(chan, core, chan).start()

    @pl.when(core == 1)
    def _():
        g2recv[1, chan] = g2send[chan]

    products(lhs2[1], gath.at[1], halo[...], prod)

    @pl.loop(0, NB // group_size)
    def _(group):
        resample_backward(prod, group, group_size, slopes, shifted32, packed32)

    shifted[1] = shifted32[...].astype(BF16)
    hgath[chan, 0:ROWS] = shifted[1, 1, 1 : ROWS + 1]
    hgath[chan, ROWS] = packed32[...].astype(BF16)
    send(hgath, hg_sems, *(2, 3, 0, 1))

    def g1_copy(p):
        return remote(g1part.at[p], g1swap.at[p], g1_sems, p, space=sibling)

    chunks = range(3)
    for p in chunks:
        total = jnp.zeros((3 * NB, CH * NB), F32)
        for r in range(0, ROWS, 2):
            lhs = jnp.concatenate(
                [shifted[1, :, r + i - p + 2].reshape(3 * NB, LANES) for i in range(2)], axis=1
            )
            total = total + contract_last(lhs, row_pair(gath.at[0], r))
        g1part[p] = total * scale

        @pl.when(core == 1)
        def _():
            g1_copy(p).start()

    def piece_of(ref, owner):
        rows = pl.ds(pl.multiple_of(lax.div(owner, 2) * PIECE, 16), PIECE)
        return ref.at[lax.rem(owner, 2), rows]

    def rs_copy(owner):
        slot = lax.rem(chip - owner + PEERS, PEERS) - 1
        return pltpu.make_async_remote_copy(
            src_ref=piece_of(rs_send, owner), dst_ref=rs_recv.at[slot], send_sem=rs_sems.at[0],
            recv_sem=rs_sems.at[1],
            device_id={"space": owner * 2 + core}, device_id_type=MESH,
        )

    def all_pieces(count):
        return pltpu.make_async_remote_copy(
            src_ref=rs_recv.at[pl.ds(0, count)], dst_ref=rs_recv.at[pl.ds(0, count)],
            send_sem=rs_sems.at[0], recv_sem=rs_sems.at[1],
            device_id={"space": sibling}, device_id_type=MESH,
        )

    def to_owners(p):
        for step in range(4):
            owner = 4 * p + lax.rem(column + (2, 1, 3, 0)[step], 4)

            @pl.when(owner == chip)
            def _():
                rs_recv[PEERS - 1] = piece_of(rs_send, chip)[...]

            @pl.when(owner != chip)
            def _():
                rs_copy(owner).start()

    def put_rows(first, values):
        for half in range(2):
            rs_send[half, pl.ds(pl.multiple_of(first, 16), values.shape[0])] = values[
                :, half * LANES : (half + 1) * LANES
            ].astype(BF16)

    @pl.when(core == 1)
    def _():
        g2_copy(chan, 0, chan).wait_recv()

        @pl.loop(1, CH)
        def _(k):
            for source_core in range(2):
                g2_copy(chan, source_core, chan_at(k)).wait_recv()

        for k in range(3):
            loaded = [
                g2recv[0, s, k].astype(F32) + g2recv[1, s, k].astype(F32) for s in range(CH)
            ]
            for t in range(4 * k, min(4 * k + 4, 9)):
                for half in range(2):
                    total = jnp.zeros((NB, LANES), F32)
                    for place in range(4):
                        moved = roll(loaded[4 * half + place], (place - t % 4) * NB)
                        total = jnp.where(lane // NB == place, moved, total)
                    rs_send[half, t * NB : (t + 1) * NB] = total.astype(BF16)
        for p in chunks:
            to_owners(p)

    @pl.when(core == 0)
    def _():
        for p in chunks:
            g1_copy(p).wait_recv()
            put_rows(96 * p, g1part[p] + g1swap[p])
            to_owners(p)

    arrive(hgath, hg_sems, 2)
    send(hgath, hg_sems, 7, 4, 5)
    turn_weights(0)

    def ag_copy(k, slot):
        return pltpu.make_async_remote_copy(
            src_ref=piece_of(sums, slot), dst_ref=piece_of(sums, slot), send_sem=ag_sems.at[0, k],
            recv_sem=ag_sems.at[1, slot],
            device_id={"space": chip_at(k) * 2 + core}, device_id_type=MESH,
        )

    def sib_copy(slot):
        return remote(piece_of(sums, slot), piece_of(sib_in, slot), sib_sems, slot, space=sibling)

    @pl.when(chip < OWNERS)
    def _():
        all_pieces(PEERS - 1).wait_recv()
        total = rs_recv[0].astype(F32)
        for s in range(1, PEERS):
            total = total + rs_recv[s].astype(F32)
        piece_of(sums, chip)[...] = total.astype(BF16)

        for k in reversed(range(PEERS - 1)):
            ag_copy(k, chip).start()
        sib_copy(chip).start()

    arrive(hgath, hg_sems, 0, 1, 3, 4, 5, 7)
    products(lhs2[0], hgath, hgath[:, ROWS], prod)

    @pl.loop(0, NB // group_size)
    def _(group):
        main, _ = combine(prod, group, group_size)
        rows = group_rows(group, group_size)
        cot32[:, rows, :] = cot32[:, rows, :] + main.reshape(ROWS, group_size, LANES)

    for r in range(ROWS):
        rows32[pl.ds(r, NB, stride=ROWS), :] = cot32[r]
    out_ref[...] = rows32[...].reshape(NB, ROWS, LANES).astype(BF16)

    for k in range(PEERS - 1):
        source = chip_at(k)

        @pl.when(source < OWNERS)
        def _():
            ag_copy(k, source).wait_recv()
            sib_copy(source).start()

    def store(source, which):
        for grad, ref in enumerate((g1_ref, g2_ref)):
            @pl.when(which == grad)
            def _():
                for half in range(2):
                    ref[:, half * LANES : (half + 1) * LANES] = source[half]

    store(sums, core)

    @pl.loop(0, OWNERS)
    def _(source):
        sib_copy(source).wait_recv()

    store(sib_in, 1 - core)

    to_left.wait_send()
    to_right.wait_send()
    w_out.wait_send()
    for buf, sems in ((gath.at[0], main_sems.at[0]), (gath.at[1], main_sems.at[1]), (hgath, hg_sems)):
        for j in (0, 1, 2, 3, 4, 5, 7 if buf is hgath else 6):
            hop(buf, sems, j).wait_send()

    @pl.loop(1, CH)
    def _(k):
        halo_copy(k, chan).wait_send()

    @pl.when(column < 3)
    def _():
        @pl.loop(1, CH)
        def _(k):
            w_copy(k, chan_at(k), chan).wait_send()

        @pl.loop(1, 4)
        def _(k):
            tile_copy(k, column).wait_send()

    @pl.loop(1, CH)
    def _(k):
        g2_copy(chan_at(k), core, chan).wait_send()

    @pl.when(core == 0)
    def _():
        g2_copy(chan, core, chan).wait_send()

    @pl.when(core == 1)
    def _():
        for p in range(3):
            g1_copy(p).wait_send()

    @pl.loop(0, OWNERS)
    def _(owner):
        sib_copy(owner).wait_send()

        @pl.when(owner != chip)
        def _():
            rs_copy(owner).wait_send()

    @pl.when(chip < OWNERS)
    def _():
        for k in range(PEERS - 1):
            ag_copy(k, chip).wait_send()


def on_device(field, first_weight, second_weight, cotangent):
    vmem = pl.BlockSpec(memory_space=pltpu.VMEM)
    hbm = pl.BlockSpec(memory_space=pltpu.HBM)
    dma = pltpu.SemaphoreType.DMA
    out, first_grad, second_grad = pl.pallas_call(
        kernel,
        out_shape=(
            jax.ShapeDtypeStruct((NB, ROWS, LANES), BF16),
            jax.ShapeDtypeStruct((9 * NB, CH * NB), BF16),
            jax.ShapeDtypeStruct((9 * NB, CH * NB), BF16),
        ),
        in_specs=[hbm] * 4,
        out_specs=(vmem, vmem, vmem),
        scratch_shapes=[
            pltpu.VMEM((NB, ROWS, LANES), BF16),
            pltpu.VMEM((NB, ROWS, LANES), BF16),
            pltpu.VMEM((9, NB, CH * NB), BF16),
            pltpu.VMEM((9, NB, CH * NB), BF16),
            pltpu.VMEM((NB * ROWS, LANES), F32),
            pltpu.VMEM((2, CH, ROWS, NB, LANES), BF16),
            pltpu.VMEM((CH, NB, LANES), BF16),
            pltpu.VMEM((NB, LANES), BF16),
            pltpu.VMEM((2, NB, LANES), BF16),
            pltpu.VMEM((ROWS, NB, LANES), F32),
            pltpu.VMEM((2, 9 * NB, CH * NB), BF16),
            pltpu.VMEM((CH, NB, LANES), BF16),
            pltpu.VMEM((2, 3, CH, NB, LANES), BF16),
            pltpu.VMEM((ROWS + 1, 9 * NB, LANES), F32),
            pltpu.VMEM((2, 4, ROWS, NB, LANES), F32),
            pltpu.VMEM((3, ROWS + 2, NB, LANES), F32),
            pltpu.VMEM((2, 3, ROWS + 2, NB, LANES), BF16),
            pltpu.VMEM((NB, LANES), F32),
            pltpu.VMEM((CH, ROWS + 1, NB, LANES), BF16),
            pltpu.VMEM((CH, 3, NB, LANES), BF16),
            pltpu.VMEM((2, CH, 3, NB, LANES), BF16),
            pltpu.VMEM((3, 3 * NB, CH * NB), F32),
            pltpu.VMEM((3, 3 * NB, CH * NB), F32),
            pltpu.VMEM((2, 9 * NB, LANES), BF16),
            pltpu.VMEM((PEERS, PIECE, LANES), BF16),
            pltpu.VMEM((2, 9 * NB, LANES), BF16),
            pltpu.VMEM((2, 9 * NB, LANES), BF16),
            dma((4,)),
            dma((2, 2)),
            dma((2, 2, len(HOPS))),
            dma((2, CH)),
            dma((2, CH)),
            dma((2, 4)),
            dma((2, 1)),
            dma((2, len(HOPS))),
            dma((2, 2, CH)),
            dma((2, 3)),
            dma((2,)),
            dma((2, PEERS)),
            dma((2, OWNERS)),
        ],
        compiler_params=pltpu.CompilerParams(
            collective_id=0, has_side_effects=True, vmem_limit_bytes=40 * 1024 * 1024
        ),
    )(
        *(
            pltpu.with_memory_space_constraint(x, pltpu.HBM)
            for x in (
                field, first_weight.transpose(1, 0, 2), second_weight.transpose(1, 0, 2), cotangent
            )
        )
    )

    def taps_inside(grad):
        return grad.astype(F32).reshape(9, NB, CH * NB).transpose(1, 0, 2)

    return (out, taps_inside(first_grad), taps_inside(second_grad))


def solution(mesh):
    in_specs = (
        P("chan", None, "space"),
        P("chan", None, None),
        P("chan", None, None),
        P("chan", None, "space"),
    )
    out_specs = (P("chan", None, "space"), P("chan", None, None), P("chan", None, None))
    return jax.shard_map(
        on_device, mesh=mesh, in_specs=in_specs, out_specs=out_specs, check_vma=False
    )
```
